32 devices in a mesh: section: 8 (over z, core), dp: 4 (over y, x).
Axes of the slice: x: 2, y: 2, z: 4, core: 2. Of those that a mesh axis runs over, the one named last changes fastest.
Arguments:
- w_up: bfloat16 [8, 32, 128, 128], P('section'), may hold values from -0.375 to 0.375
- up_index: int32 [8, 32], P('section'), may hold values from 0 to 31
- w_down: bfloat16 [8, 32, 128, 128], P('section'), may hold values from -0.375 to 0.375
- down_index: int32 [8, 32], P('section'), may hold values from 0 to 31
- tick_order: int32 [8, 2], P('section'), may hold values from 0 to 1, each once within a row
- values_in: bfloat16 [8, 32, 4096], P('section', 'dp'), may hold values from -6 to 6
- score_grad_in: bfloat16 [8, 32, 4096], P('section', 'dp'), may hold values from -6 to 6
- tangent_in: bfloat16 [8, 32, 4096], P('section', 'dp'), may hold values from -6 to 6
- state_adjoint_in: bfloat16 [8, 32, 4096], P('section', 'dp'), may hold values from -6 to 6
- saved_back: bfloat16 [8, 2, 32, 4096], P('section', None, 'dp'), may hold values from -6 to 6
- saved_tan: bfloat16 [8, 2, 32, 4096], P('section', None, 'dp'), may hold values from -6 to 6
- saved_second: bfloat16 [8, 2, 32, 4096], P('section', None, 'dp'), may hold values from -6 to 6
- saved_second_tan: bfloat16 [8, 2, 32, 4096], P('section', None, 'dp'), may hold values from -6 to 6
- saved_second_grad: bfloat16 [8, 2, 32, 4096], P('section', None, 'dp'), may hold values from -6 to 6
Outputs:
- values_out: bfloat16 [8, 32, 4096], P('section', 'dp')
- score_grad_out: bfloat16 [8, 32, 4096], P('section', 'dp')
- tangent_out: bfloat16 [8, 32, 4096], P('section', 'dp')
- state_adjoint_out: bfloat16 [8, 32, 4096], P('section', 'dp')
- grad_up: bfloat16 [8, 32, 128, 128], P('section', 'dp')
- grad_down: bfloat16 [8, 32, 128, 128], P('section', 'dp')
The draws below stay inside these ranges and needn't reach their ends.
Inputs may be any that keep to these rules, and one draw needn't show every extreme that they name: up_index[s, j] is the input block that hidden block j of layer s reads. down_index[s, i] is the hidden block that output block i of layer s reads. `tick_order`: each row is a permutation of the 2 slots.
All inputs are finite; a program needn't handle non-finite values.
Results may differ from the reference program's by a relative error of at most 0.023.
Values may be sent and summed in bfloat16 or wider, within the bound.
No kernel may reach another device: no remote copies, remote signals or barrier semaphores. Data moves between devices by JAX's collectives and lax.ppermute only.
A program may use at most 64 MiB of HBM per device.

```python
import jax
import jax.numpy as jnp
from jax import lax

D = 4096
BLOCK = 128
TICKS = 2
LAYERS = 8
ROWS = 32
DB = 32
FB = 32
N_DP = 4


def touch_ends(drawn, rng, smallest, top_value):
    spot = [jax.random.randint(jax.random.fold_in(rng, axis), (), 0, length) for axis, length in enumerate(drawn.shape)]
    longest = drawn.shape.index(max(drawn.shape))
    neighbour = spot[:longest] + [(spot[longest] + 1) % drawn.shape[longest]] + spot[longest + 1:]
    return drawn.at[tuple(spot)].set(smallest).at[tuple(neighbour)].set(top_value)


def shard_levels(key, shape, split, least, high):
    gain, own = 1.0, jax.random.fold_in(key, 6)
    for dim, blocks in split:
        heights = jnp.exp(jax.random.uniform(jax.random.fold_in(own, dim), (blocks,), jnp.float32, least / len(split), high / len(split)))
        gain = gain * jnp.repeat(heights, shape[dim] // blocks).reshape([-1 if axis == dim else 1 for axis in range(len(shape))])
    return gain


def gaussian(rng, dims, scale, bound, cuts=(), held_as=jnp.bfloat16):
    array = jax.random.normal(rng, dims, jnp.float32) * scale
    if len(cuts) > 0:
        array = shard_levels(rng, dims, cuts, -0.22, 0.18) * array
    return jnp.clip(array, min=-bound, max=bound).astype(held_as)


def setup_inputs(seed: int = 0) -> dict:
    key_list = jax.random.split(jax.random.key(seed), 15)
    w_up = gaussian(key_list[0], (LAYERS, FB, BLOCK, BLOCK), (2 * BLOCK) ** -0.5, 0.375, ((0, 8),))
    up_index = touch_ends(jax.random.randint(key_list[1], (LAYERS, FB), 0, DB), jax.random.fold_in(key_list[1], 1), 0, DB - 1).astype(jnp.int32)
    w_down = gaussian(key_list[2], (LAYERS, DB, BLOCK, BLOCK), (2 * BLOCK) ** -0.5, 0.375, ((0, 8),))
    down_index = touch_ends(jax.random.randint(key_list[3], (LAYERS, DB), 0, FB), jax.random.fold_in(key_list[3], 1), 0, FB - 1).astype(jnp.int32)
    tick_order = jax.vmap(lambda own: jax.random.permutation(own, TICKS))(jax.random.split(key_list[4], LAYERS)).reshape((LAYERS, TICKS)).astype(jnp.int32)
    values_in = gaussian(key_list[5], (LAYERS, ROWS, D), 1.0, 6.0, ((0, 8), (1, 4)))
    score_grad_in = gaussian(key_list[6], (LAYERS, ROWS, D), 1.0, 6.0, ((0, 8), (1, 4)))
    tangent_in = gaussian(key_list[7], (LAYERS, ROWS, D), 1.0, 6.0, ((0, 8), (1, 4)))
    state_adjoint_in = gaussian(key_list[8], (LAYERS, ROWS, D), 1.0, 6.0, ((0, 8), (1, 4)))
    saved_back = gaussian(key_list[9], (LAYERS, TICKS, ROWS, D), 1.0, 6.0, ((0, 8), (2, 4)))
    saved_tan = gaussian(key_list[10], (LAYERS, TICKS, ROWS, D), 1.0, 6.0, ((0, 8), (2, 4)))
    saved_second = gaussian(key_list[11], (LAYERS, TICKS, ROWS, D), 1.0, 6.0, ((0, 8), (2, 4)))
    saved_second_tan = gaussian(key_list[12], (LAYERS, TICKS, ROWS, D), 1.0, 6.0, ((0, 8), (2, 4)))
    saved_second_grad = gaussian(key_list[13], (LAYERS, TICKS, ROWS, D), 1.0, 6.0, ((0, 8), (2, 4)))
    return dict(w_up=w_up, up_index=up_index, w_down=w_down, down_index=down_index, tick_order=tick_order, values_in=values_in, score_grad_in=score_grad_in, tangent_in=tangent_in, state_adjoint_in=state_adjoint_in, saved_back=saved_back, saved_tan=saved_tan, saved_second=saved_second, saved_second_tan=saved_second_tan, saved_second_grad=saved_second_grad)


def silu_parts(inputs):
    logistic = jax.nn.sigmoid(inputs)
    slopes = logistic * (1.0 + inputs * (1.0 - logistic))
    curves = logistic * (1.0 - logistic) * (2.0 + inputs * (1.0 - 2.0 * logistic))
    return (inputs * logistic, slopes, curves)

def block_map(matrix, weight, block_table):
    block_width = weight.shape[-1]
    row_count = matrix.shape[0]
    pieces = matrix.astype(jnp.float32).reshape(row_count, -1, block_width)
    picked = jnp.take(pieces, block_table, axis=1)
    result = jnp.einsum('rnk,nkj->rnj', picked, weight.astype(jnp.float32), precision=lax.Precision.HIGHEST)
    return result.reshape(row_count, -1)

def block_map_back(matrix, weight, block_table, block_count):
    block_width = weight.shape[-1]
    row_count = matrix.shape[0]
    pieces = matrix.astype(jnp.float32).reshape(row_count, -1, block_width)
    partial_value = jnp.einsum('rnj,nkj->rnk', pieces, weight.astype(jnp.float32), precision=lax.Precision.HIGHEST)
    placing = (block_table[:, None] == jnp.arange(block_count, dtype=jnp.int32)[None, :]).astype(jnp.float32)
    result = jnp.einsum('rnk,nc->rck', partial_value, placing, precision=lax.Precision.HIGHEST)
    return result.reshape(row_count, -1)

def layer_tick(params, streams, saved):
    up_weight, up_table, down_weight, down_table = params
    values, score_grad, tangent, adjoint = streams
    back_input, tangent_input, second_input, second_tangent, second_grad = saved
    hidden_blocks = up_weight.shape[0]
    model_blocks = down_weight.shape[0]
    hidden_values = silu_parts(block_map(values, up_weight, up_table))[0].astype(jnp.bfloat16)
    new_values = (values.astype(jnp.float32) + block_map(hidden_values, down_weight, down_table)).astype(jnp.bfloat16)
    active_back, slope_back, unused_curve = silu_parts(block_map(back_input, up_weight, up_table))
    hidden_back = active_back.astype(jnp.bfloat16)
    gate_back = (slope_back * block_map_back(score_grad, down_weight, down_table, hidden_blocks)).astype(jnp.bfloat16)
    new_score_grad = (score_grad.astype(jnp.float32) + block_map_back(gate_back, up_weight, up_table, model_blocks)).astype(jnp.bfloat16)
    tangent_slope = silu_parts(block_map(tangent_input, up_weight, up_table))[1]
    tangent_hidden = (tangent_slope * block_map(tangent, up_weight, up_table)).astype(jnp.bfloat16)
    new_tangent = (tangent.astype(jnp.float32) + block_map(tangent_hidden, down_weight, down_table)).astype(jnp.bfloat16)
    active_second, slope_second, curve_second = silu_parts(block_map(second_input, up_weight, up_table))
    raised_second_tangent = block_map(second_tangent, up_weight, up_table)
    pulled_second = block_map_back(second_grad, down_weight, down_table, hidden_blocks)
    pulled_adjoint = block_map_back(adjoint, down_weight, down_table, hidden_blocks)
    second_push = (slope_second * pulled_adjoint + curve_second * pulled_second * raised_second_tangent).astype(jnp.bfloat16)
    new_adjoint = (adjoint.astype(jnp.float32) + block_map_back(second_push, up_weight, up_table, model_blocks)).astype(jnp.bfloat16)
    hidden_second = active_second.astype(jnp.bfloat16)
    tangent_second = (slope_second * raised_second_tangent).astype(jnp.bfloat16)
    gated_second = (slope_second * pulled_second).astype(jnp.bfloat16)
    up_pairs = ((back_input, gate_back), (second_input, second_push), (second_tangent, gated_second))
    down_pairs = ((hidden_back, score_grad), (hidden_second, adjoint), (tangent_second, second_grad))
    return ((new_values, new_score_grad, new_tangent, new_adjoint), up_pairs, down_pairs)

def pair_grad(inputs, cotangents, block_table, groups):
    row_count = inputs.shape[0]
    pieces = inputs.astype(jnp.float32).reshape(groups, row_count // groups, -1, BLOCK)
    picked = jnp.take(pieces, block_table, axis=2)
    cot_pieces = cotangents.astype(jnp.float32).reshape(groups, row_count // groups, -1, BLOCK)
    return jnp.einsum('grnk,grnj->gnkj', picked, cot_pieces, precision=lax.Precision.HIGHEST)

def reference(w_up, up_index, w_down, down_index, tick_order, values_in, score_grad_in, tangent_in, state_adjoint_in, saved_back, saved_tan, saved_second, saved_second_tan, saved_second_grad):

    def gather_inputs(layer_index, tick_number, streams):
        slot_index = tick_order[layer_index, tick_number]
        params = (w_up[layer_index], up_index[layer_index], w_down[layer_index], down_index[layer_index])
        local = (streams[0][layer_index], streams[1][layer_index], streams[2][layer_index], streams[3][layer_index])
        saved = (saved_back[layer_index, slot_index], saved_tan[layer_index, slot_index], saved_second[layer_index, slot_index], saved_second_tan[layer_index, slot_index], saved_second_grad[layer_index, slot_index])
        return (params, local, saved)
    streams = (values_in, score_grad_in, tangent_in, state_adjoint_in)
    history = []
    for tick_number in range(TICKS):
        history.append(streams)

        def advance(layer_index):
            params, local, saved = gather_inputs(layer_index, tick_number, streams)
            return layer_tick(params, local, saved)[0]
        moved = lax.map(advance, jnp.arange(LAYERS, dtype=jnp.int32))
        streams = (jnp.roll(moved[0], 1, 0), jnp.roll(moved[1], -1, 0), jnp.roll(moved[2], 1, 0), jnp.roll(moved[3], -1, 0))

    def layer_grads(layer_index):
        up_total = jnp.zeros((N_DP, FB, BLOCK, BLOCK), jnp.float32)
        down_total = jnp.zeros((N_DP, DB, BLOCK, BLOCK), jnp.float32)
        for tick_number in range(TICKS):
            params, local, saved = gather_inputs(layer_index, tick_number, history[tick_number])
            unused_streams, up_pairs, down_pairs = layer_tick(params, local, saved)
            for entry in up_pairs:
                up_total = up_total + pair_grad(entry[0], entry[1], up_index[layer_index], N_DP)
            for entry in down_pairs:
                down_total = down_total + pair_grad(entry[0], entry[1], down_index[layer_index], N_DP)
        up_share = lax.optimization_barrier((up_total * (1.0 / ROWS)).astype(jnp.bfloat16))
        down_share = lax.optimization_barrier((down_total * (1.0 / ROWS)).astype(jnp.bfloat16))
        up_sum = lax.optimization_barrier(jnp.sum(up_share.astype(jnp.float32), 0)).astype(jnp.bfloat16)
        down_sum = lax.optimization_barrier(jnp.sum(down_share.astype(jnp.float32), 0)).astype(jnp.bfloat16)
        return (up_sum, down_sum)
    grad_up, grad_down = lax.map(layer_grads, jnp.arange(LAYERS, dtype=jnp.int32))
    return (streams[0], streams[1], streams[2], streams[3], grad_up, grad_down)
```

```python
import jax
import jax.numpy as jnp
from jax import lax
from jax.experimental import pallas as pl
from jax.experimental.pallas import tpu as pltpu
from jax.sharding import PartitionSpec as P

BLOCK = 128
F32 = jnp.float32
BF16 = jnp.bfloat16
LIMIT = 40 * 1024 * 1024


def partner(me, step, count):
    if count & (count - 1) == 0:
        return me ^ step
    return lax.rem(me + step, count)


def swap_route(step, count):
    if count & (count - 1) == 0:
        return [(i, i ^ step) for i in range(count)]
    return [(i, (i + step) % count) for i in range(count)]


def from_behind(block, axis, distance):
    devices = range(lax.axis_size(axis))
    route = [((i - distance) % len(devices), i) for i in devices]
    return lax.ppermute(block, axis, route)


def times(rows, weight):
    return lax.dot_general(rows, weight, (((1,), (0,)), ((), ())), preferred_element_type=F32)


def times_transposed(rows, weight):
    return lax.dot_general(rows, weight, (((1,), (1,)), ((), ())), preferred_element_type=F32)


def sigmoid(z):
    return 1.0 / (1.0 + jnp.exp(-z))


def slope_of(z, s):
    return s * (1.0 + z * (1.0 - s))


def lanes(block):
    if isinstance(block, int):
        return pl.ds(block * BLOCK, BLOCK)
    return pl.ds(pl.multiple_of(block * BLOCK, BLOCK), BLOCK)


def stack(parts):
    return jnp.concatenate([part.astype(F32) for part in parts], 0)


def send_order(me, count, per):
    for step in range(count):
        base = partner(me, step, count) * per
        for place in range(per):
            yield step, place, base + place


def back_first(count, per, blocks, up_idx, down_idx, order, w_up, w_down, g_ref, a_ref, back, second, second_tan,
               second_grad, pack, keep, *rest):
    sends = rest[:count]
    pulled, returned, hidden = rest[count:]
    me = lax.axis_index("dp")
    m0 = order[0, 0]
    m1 = order[0, 1]
    for b in range(blocks):
        pulled[b] = jnp.zeros(pulled.shape[1:], F32)
        returned[b] = stack([g_ref[0, :, lanes(b)], a_ref[0, :, lanes(b)]])
    for step, place, i in send_order(me, count, per):
        at = lanes(i)
        c = stack([g_ref[0, :, at], a_ref[0, :, at], second_grad[0, m0, :, at], second_grad[0, m1, :, at]]).astype(BF16)
        sends[step][8, :, lanes(place)] = c[0:16]
        sends[step][9, :, lanes(place)] = c[16:32]
        target = down_idx[0, i]
        pulled[target] = pulled[target] + times_transposed(c, w_down[0, i])
    for step, place, j in send_order(me, count, per):
        u = up_idx[0, j]
        at = lanes(u)
        x = stack([back[0, m0, :, at], second[0, m0, :, at], second_tan[0, m0, :, at],
                   second_tan[0, m1, :, at], back[0, m1, :, at], second[0, m1, :, at]]).astype(BF16)
        out = sends[step]
        here = lanes(place)
        for group in range(3):
            out[group, :, here] = x[16 * group:16 * group + 16]
        z = times(x, w_up[0, j])
        zb0, za0, ta0, ta1, zb1, za1 = (z[8 * k:8 * k + 8] for k in range(6))
        pg, pa, ga0, ga1 = (pulled[j, 8 * k:8 * k + 8] for k in range(4))
        sb0, sa0, sb1, sa1 = sigmoid(zb0), sigmoid(za0), sigmoid(zb1), sigmoid(za1)
        slope_a0 = slope_of(za0, sa0)
        slope_a1 = slope_of(za1, sa1)
        curve_a0 = sa0 * (1.0 - sa0) * (2.0 + za0 * (1.0 - 2.0 * sa0))
        curve_a1 = sa1 * (1.0 - sa1) * (2.0 + za1 * (1.0 - 2.0 * sa1))
        push = slope_a0 * pa + curve_a0 * ga0 * ta0
        e = jnp.concatenate([slope_of(zb0, sb0) * pg, push], 0).astype(BF16)
        out[3, :, here] = e
        out[4, :, here] = jnp.concatenate([slope_a0 * ga0, slope_a1 * ga1], 0).astype(BF16)
        hidden[j] = jnp.concatenate(
            [zb0 * sb0, za0 * sa0, slope_a0 * ta0, slope_a1 * ta1, zb1 * sb1, za1 * sa1], 0).astype(BF16)
        keep[j] = jnp.concatenate([slope_of(zb1, sb1), slope_a1, curve_a1 * ga1 * ta1], 0)
        returned[u] = returned[u] + times_transposed(e, w_up[0, j])
    for b in range(blocks):
        pack[:, lanes(b)] = returned[b].astype(BF16)
    for step, place, i in send_order(me, count, per):
        y = hidden[down_idx[0, i]]
        for group in range(3):
            sends[step][5 + group, :, lanes(place)] = y[16 * group:16 * group + 16]


def forward_first(blocks, up_idx, down_idx, order, w_up, w_down, v_ref, t_ref, tan, pack, keep, hidden):
    m0 = order[0, 0]
    m1 = order[0, 1]
    for j in range(blocks):
        at = lanes(up_idx[0, j])
        x = stack([v_ref[0, :, at], t_ref[0, :, at], tan[0, m0, :, at], tan[0, m1, :, at]]).astype(BF16)
        z = times(x, w_up[0, j])
        zv, zt, z0, z1 = (z[8 * k:8 * k + 8] for k in range(4))
        hidden[j] = jnp.concatenate([zv * sigmoid(zv), slope_of(z0, sigmoid(z0)) * zt], 0).astype(BF16)
        keep[j] = slope_of(z1, sigmoid(z1))
    for i in range(blocks):
        at = lanes(i)
        moved = stack([v_ref[0, :, at], t_ref[0, :, at]]) + times(hidden[down_idx[0, i]], w_down[0, i])
        pack[:, at] = moved.astype(BF16)


def back_second(count, per, blocks, up_idx, down_idx, w_up, w_down, rows, keep, pack, *rest):
    sends = rest[:count]
    pulled, returned = rest[count:]
    me = lax.axis_index("dp")
    for b in range(blocks):
        pulled[b] = jnp.zeros(pulled.shape[1:], F32)
        returned[b] = rows[:, lanes(b)].astype(F32)
    for step, place, i in send_order(me, count, per):
        c = rows[:, lanes(i)]
        sends[step][1, :, lanes(place)] = c
        target = down_idx[0, i]
        pulled[target] = pulled[target] + times_transposed(c, w_down[0, i])
    for step, place, j in send_order(me, count, per):
        u = up_idx[0, j]
        slope_b, slope_a, push = (keep[j, 8 * k:8 * k + 8] for k in range(3))
        e = jnp.concatenate([slope_b * pulled[j, 0:8], slope_a * pulled[j, 8:16] + push], 0).astype(BF16)
        sends[step][0, :, lanes(place)] = e
        returned[u] = returned[u] + times_transposed(e, w_up[0, j])
    for b in range(blocks):
        pack[:, lanes(b)] = returned[b].astype(BF16)


def forward_second(blocks, up_idx, down_idx, w_up, w_down, rows, keep, pack, hidden):
    for j in range(blocks):
        z = times(rows[:, lanes(up_idx[0, j])], w_up[0, j])
        zv, zt = z[0:8], z[8:16]
        hidden[j] = jnp.concatenate([zv * sigmoid(zv), keep[j] * zt], 0).astype(BF16)
    for i in range(blocks):
        at = lanes(i)
        pack[:, at] = (rows[:, at].astype(F32) + times(hidden[down_idx[0, i]], w_down[0, i])).astype(BF16)


def finish(count, per, scale, fwd, bwd, *rest):
    early = rest[:count]
    late = rest[count:2 * count]
    values, score, tangent, adjoint, grad_up, grad_down = rest[2 * count:]
    moved = fwd[...].astype(F32)
    values[0] = moved[0:8].astype(BF16)
    tangent[0] = moved[8:16].astype(BF16)
    moved = bwd[...].astype(F32)
    score[0] = moved[0:8].astype(BF16)
    adjoint[0] = moved[8:16].astype(BF16)
    for place in range(per):
        at = lanes(place)
        for out, left, right, last in ((grad_up, (0, 1, 2), (3, 4), 0), (grad_down, (5, 6, 7), (8, 9), 1)):
            xs, es = [], []
            for source in range(count):
                xs += [early[source][k, :, at] for k in left]
                es += [early[source][k, :, at] for k in right] + [late[source][last, :, at]]
            total = lax.dot_general(jnp.concatenate(xs, 0), jnp.concatenate(es, 0), (((0,), (0,)), ((), ())),
                                    preferred_element_type=F32)
            out[0, place] = (total * scale).astype(BF16)


def call(body, operands, smem, outs, scratch, flops=0):
    specs = [pl.BlockSpec(memory_space=pltpu.SMEM)] * smem
    specs += [pl.BlockSpec(memory_space=pltpu.VMEM)] * (len(operands) - smem)
    moved = sum(x.size * x.dtype.itemsize for x in list(operands) + list(outs))
    return pl.pallas_call(
        body,
        out_shape=outs,
        in_specs=specs,
        out_specs=[pl.BlockSpec(memory_space=pltpu.VMEM)] * len(outs),
        scratch_shapes=scratch,
        compiler_params=pltpu.CompilerParams(vmem_limit_bytes=LIMIT),
        cost_estimate=pl.CostEstimate(flops=flops, bytes_accessed=moved, transcendentals=0),
    )(*operands)


def on_device(w_up, up_index, w_down, down_index, tick_order, values_in, score_grad_in, tangent_in, state_adjoint_in,
              saved_back, saved_tan, saved_second, saved_second_tan, saved_second_grad):
    count = lax.axis_size("dp")
    blocks = w_up.shape[1]
    per = blocks // count
    width = values_in.shape[2]
    part = per * BLOCK
    scale = 1.0 / (values_in.shape[1] * count)
    shape = jax.ShapeDtypeStruct
    pair = shape((16, width), BF16)

    def body(f, *args):
        def kernel(*refs):
            f(*args, *refs)
        return kernel

    bwd, keep, *early = call(
        body(back_first, count, per, blocks),
        (up_index, down_index, tick_order, w_up, w_down, score_grad_in, state_adjoint_in, saved_back, saved_second,
         saved_second_tan, saved_second_grad), 3,
        [pair, shape((blocks, 24, BLOCK), F32)] + [shape((10, 16, part), BF16)] * count,
        [pltpu.VMEM((blocks, 32, BLOCK), F32), pltpu.VMEM((blocks, 16, BLOCK), F32), pltpu.VMEM((blocks, 48, BLOCK), BF16)])
    bwd = from_behind(bwd, "section", -1)
    fwd, keep_tan = call(
        body(forward_first, blocks),
        (up_index, down_index, tick_order, w_up, w_down, values_in, tangent_in, saved_tan), 3,
        [pair, shape((blocks, 8, BLOCK), F32)],
        [pltpu.VMEM((blocks, 16, BLOCK), BF16)])
    fwd = from_behind(fwd, "section", 1)
    early = early[:1] + [lax.ppermute(early[step], "dp", swap_route(step, count)) for step in range(1, count)]
    bwd, *late = call(
        body(back_second, count, per, blocks),
        (up_index, down_index, w_up, w_down, bwd, keep), 2,
        [pair] + [shape((2, 16, part), BF16)] * count,
        [pltpu.VMEM((blocks, 16, BLOCK), F32), pltpu.VMEM((blocks, 16, BLOCK), F32)])
    late = late[:1] + [lax.ppermute(late[step], "dp", swap_route(step, count)) for step in range(1, count)]
    bwd = from_behind(bwd, "section", -1)
    (fwd,) = call(
        body(forward_second, blocks),
        (up_index, down_index, w_up, w_down, fwd, keep_tan), 2,
        [pair], [pltpu.VMEM((blocks, 16, BLOCK), BF16)])
    fwd = from_behind(fwd, "section", 1)
    stream = shape((1,) + values_in.shape[1:], BF16)
    grad = shape((1, per, BLOCK, BLOCK), BF16)
    return tuple(call(
        body(finish, count, per, scale), (fwd, bwd, *early, *late), 0,
        [stream, stream, stream, stream, grad, grad], []))


def solution(mesh):
    layer = P("section", None, None, None)
    table = P("section", None)
    stream = P("section", "dp", None)
    saved = P("section", None, "dp", None)
    return jax.shard_map(
        on_device,
        mesh=mesh,
        in_specs=(layer, table, layer, table, table) + (stream,) * 4 + (saved,) * 5,
        out_specs=(stream,) * 4 + (P("section", "dp", None, None),) * 2,
        check_vma=False,
    )
```

```python
import jax
import jax.numpy as jnp
from jax import lax
from jax.experimental import pallas as pl
from jax.experimental.pallas import tpu as pltpu
from jax.sharding import PartitionSpec as P

BLOCK = 128
F32 = jnp.float32
BF16 = jnp.bfloat16
LIMIT = 40 * 1024 * 1024
WIDE = 60 * 1024 * 1024


def from_behind(block, axis, distance):
    devices = range(lax.axis_size(axis))
    route = [((i - distance) % len(devices), i) for i in devices]
    return lax.ppermute(block, axis, route)


def times(rows, weight):
    return lax.dot_general(rows, weight, (((1,), (0,)), ((), ())), preferred_element_type=F32)


def times_transposed(rows, weight):
    return lax.dot_general(rows, weight, (((1,), (1,)), ((), ())), preferred_element_type=F32)


def sigmoid(z):
    return 1.0 / (1.0 + jnp.exp(-z))


def slope_of(z, s):
    return s * (1.0 + z * (1.0 - s))


def lanes(block):
    if isinstance(block, int):
        return pl.ds(block * BLOCK, BLOCK)
    return pl.ds(pl.multiple_of(block * BLOCK, BLOCK), BLOCK)


def stack(parts):
    return jnp.concatenate([part.astype(F32) for part in parts], 0)


def start_all(copies):
    for copy in copies:
        copy.start()
    return copies


def wait_all(copies):
    for copy in copies:
        copy.wait()


def pack_ready(count, per, *refs):
    sources, send, held, packed, in_sems, out_sems = refs[:8], refs[8], refs[9:17], refs[17], refs[18], refs[19]
    wait_all(start_all([pltpu.make_async_copy(s, t, in_sems.at[k]) for k, (s, t) in enumerate(zip(sources, held))]))
    up_idx, order, g_ref, a_ref, back, second, second_tan, second_grad = held
    m0 = order[0, 0]
    m1 = order[0, 1]
    leaving = []
    for to in range(count):
        for place in range(per):
            j, here = to * per + place, lanes(place)
            at = lanes(up_idx[0, j])
            packed[to, 0, :, here] = stack([back[0, m0, :, at], second[0, m0, :, at]]).astype(BF16)
            packed[to, 1, :, here] = stack([second_tan[0, m0, :, at], second_tan[0, m1, :, at]]).astype(BF16)
            packed[to, 2, :, here] = stack([back[0, m1, :, at], second[0, m1, :, at]]).astype(BF16)
            at = lanes(j)
            packed[to, 3, :, here] = stack([g_ref[0, :, at], a_ref[0, :, at]]).astype(BF16)
            packed[to, 4, :, here] = stack([second_grad[0, m0, :, at], second_grad[0, m1, :, at]]).astype(BF16)
        leaving += start_all([pltpu.make_async_copy(packed.at[to], send.at[to], out_sems.at[to])])
    wait_all(leaving)


def first_tick(count, per, *refs):
    sources, (bwd, fwd, keep, keep_tan, send) = refs[:14], refs[14:19]
    held, (pulled, returned, hidden, hidden_fwd, sems) = refs[19:33], refs[33:]
    copies = start_all([pltpu.make_async_copy(s, t, sems.at[k]) for k, (s, t) in enumerate(zip(sources, held))])
    up_idx, down_idx, order, w_down, g_ref, a_ref, second_grad, w_up, back, second, second_tan, v_ref, t_ref, tan = held
    back_first(count, per, copies, up_idx, down_idx, order, w_up, w_down, g_ref, a_ref, back, second, second_tan,
               second_grad, bwd, keep, send, pulled, returned, hidden)
    wait_all(copies[11:])
    forward_first(count * per, up_idx, down_idx, order, w_up, w_down, v_ref, t_ref, tan, fwd, keep_tan, hidden_fwd)


def back_first(count, per, copies, up_idx, down_idx, order, w_up, w_down, g_ref, a_ref, back, second, second_tan, second_grad,
               pack, keep, send, pulled, returned, hidden):
    blocks = count * per
    for b in range(blocks):
        pulled[b] = jnp.zeros(pulled.shape[1:], F32)
    wait_all(copies[:7])
    m0 = order[0, 0]
    m1 = order[0, 1]
    for b in range(blocks):
        returned[b] = stack([g_ref[0, :, lanes(b)], a_ref[0, :, lanes(b)]])
    for i in range(blocks):
        at = lanes(i)
        c = stack([g_ref[0, :, at], a_ref[0, :, at], second_grad[0, m0, :, at], second_grad[0, m1, :, at]]).astype(BF16)
        target = down_idx[0, i]
        pulled[target] = pulled[target] + times_transposed(c, w_down[0, i])
    wait_all(copies[7:11])
    for j in range(blocks):
        to, here = j // per, lanes(j % per)
        u = up_idx[0, j]
        at = lanes(u)
        x = stack([back[0, m0, :, at], second[0, m0, :, at], second_tan[0, m0, :, at],
                   second_tan[0, m1, :, at], back[0, m1, :, at], second[0, m1, :, at]]).astype(BF16)
        z = times(x, w_up[0, j])
        zb0, za0, ta0, ta1, zb1, za1 = (z[8 * k:8 * k + 8] for k in range(6))
        pg, pa, ga0, ga1 = (pulled[j, 8 * k:8 * k + 8] for k in range(4))
        sb0, sa0, sb1, sa1 = sigmoid(zb0), sigmoid(za0), sigmoid(zb1), sigmoid(za1)
        slope_a0 = slope_of(za0, sa0)
        slope_a1 = slope_of(za1, sa1)
        curve_a0 = sa0 * (1.0 - sa0) * (2.0 + za0 * (1.0 - 2.0 * sa0))
        curve_a1 = sa1 * (1.0 - sa1) * (2.0 + za1 * (1.0 - 2.0 * sa1))
        push = slope_a0 * pa + curve_a0 * ga0 * ta0
        e = jnp.concatenate([slope_of(zb0, sb0) * pg, push], 0).astype(BF16)
        send[to, 0, :, here] = e
        send[to, 1, :, here] = jnp.concatenate([slope_a0 * ga0, slope_a1 * ga1], 0).astype(BF16)
        hidden[j] = jnp.concatenate(
            [zb0 * sb0, za0 * sa0, slope_a0 * ta0, slope_a1 * ta1, zb1 * sb1, za1 * sa1], 0).astype(BF16)
        keep[j] = jnp.concatenate([slope_of(zb1, sb1), slope_a1, curve_a1 * ga1 * ta1], 0)
        returned[u] = returned[u] + times_transposed(e, w_up[0, j])
    for b in range(blocks):
        pack[:, lanes(b)] = returned[b].astype(BF16)
    for i in range(blocks):
        y = hidden[down_idx[0, i]]
        for group in range(3):
            send[i // per, 2 + group, :, lanes(i % per)] = y[16 * group:16 * group + 16]


def forward_first(blocks, up_idx, down_idx, order, w_up, w_down, v_ref, t_ref, tan, pack, keep, hidden):
    m0 = order[0, 0]
    m1 = order[0, 1]
    for j in range(blocks):
        at = lanes(up_idx[0, j])
        x = stack([v_ref[0, :, at], t_ref[0, :, at], tan[0, m0, :, at], tan[0, m1, :, at]]).astype(BF16)
        z = times(x, w_up[0, j])
        zv, zt, z0, z1 = (z[8 * k:8 * k + 8] for k in range(4))
        hidden[j] = jnp.concatenate([zv * sigmoid(zv), slope_of(z0, sigmoid(z0)) * zt], 0).astype(BF16)
        keep[j] = slope_of(z1, sigmoid(z1))
    for i in range(blocks):
        at = lanes(i)
        moved = stack([v_ref[0, :, at], t_ref[0, :, at]]) + times(hidden[down_idx[0, i]], w_down[0, i])
        pack[:, at] = moved.astype(BF16)


def back_second(count, per, up_idx, down_idx, w_up, w_down, rows, keep, pack, send, pulled, returned):
    blocks = count * per
    for b in range(blocks):
        pulled[b] = jnp.zeros(pulled.shape[1:], F32)
        returned[b] = rows[:, lanes(b)].astype(F32)
    for i in range(blocks):
        c = rows[:, lanes(i)]
        send[i // per, 1, :, lanes(i % per)] = c
        target = down_idx[0, i]
        pulled[target] = pulled[target] + times_transposed(c, w_down[0, i])
    for j in range(blocks):
        u = up_idx[0, j]
        slope_b, slope_a, push = (keep[j, 8 * k:8 * k + 8] for k in range(3))
        e = jnp.concatenate([slope_b * pulled[j, 0:8], slope_a * pulled[j, 8:16] + push], 0).astype(BF16)
        send[j // per, 0, :, lanes(j % per)] = e
        returned[u] = returned[u] + times_transposed(e, w_up[0, j])
    for b in range(blocks):
        pack[:, lanes(b)] = returned[b].astype(BF16)


def forward_second(blocks, up_idx, down_idx, w_up, w_down, rows, keep, pack, hidden):
    for j in range(blocks):
        z = times(rows[:, lanes(up_idx[0, j])], w_up[0, j])
        zv, zt = z[0:8], z[8:16]
        hidden[j] = jnp.concatenate([zv * sigmoid(zv), keep[j] * zt], 0).astype(BF16)
    for i in range(blocks):
        at = lanes(i)
        pack[:, at] = (rows[:, at].astype(F32) + times(hidden[down_idx[0, i]], w_down[0, i])).astype(BF16)


def finish(count, per, scale, fwd, bwd, ready, early, late, values, score, tangent, adjoint, grad_up, grad_down):
    moved = fwd[...].astype(F32)
    values[0] = moved[0:8].astype(BF16)
    tangent[0] = moved[8:16].astype(BF16)
    moved = bwd[...].astype(F32)
    score[0] = moved[0:8].astype(BF16)
    adjoint[0] = moved[8:16].astype(BF16)
    sides = (
        (grad_up, ((ready, 0), (ready, 1), (ready, 2)), ((early, 0), (early, 1), (late, 0))),
        (grad_down, ((early, 2), (early, 3), (early, 4)), ((ready, 3), (ready, 4), (late, 1))),
    )
    for place in range(per):
        at = lanes(place)
        for out, left, right in sides:
            xs = [ref[source, k, :, at] for source in range(count) for ref, k in left]
            es = [ref[source, k, :, at] for source in range(count) for ref, k in right]
            total = lax.dot_general(jnp.concatenate(xs, 0), jnp.concatenate(es, 0), (((0,), (0,)), ((), ())),
                                    preferred_element_type=F32)
            out[0, place] = (total * scale).astype(BF16)


def call(body, operands, spaces, outs, scratch, limit=LIMIT, out_space=pltpu.VMEM, after=()):
    moved = sum(x.size * x.dtype.itemsize for x in list(operands) + list(outs))
    taken = len(operands)

    def kernel(*refs):
        body(*refs[:taken], *refs[taken + len(after):])

    return pl.pallas_call(
        kernel,
        out_shape=outs,
        in_specs=[pl.BlockSpec(memory_space=space) for space in spaces] + [pl.BlockSpec(memory_space=pl.ANY)] * len(after),
        out_specs=[pl.BlockSpec(memory_space=out_space)] * len(outs),
        scratch_shapes=scratch,
        compiler_params=pltpu.CompilerParams(vmem_limit_bytes=limit),
        cost_estimate=pl.CostEstimate(flops=0, bytes_accessed=moved, transcendentals=0),
    )(*operands, *after)


def to_replicas(parts):
    return lax.all_to_all(parts, "dp", 0, 0)


def on_device(w_up, up_index, w_down, down_index, tick_order, values_in, score_grad_in, tangent_in, state_adjoint_in,
              saved_back, saved_tan, saved_second, saved_second_tan, saved_second_grad):
    count = lax.axis_size("dp")
    blocks = w_up.shape[1]
    per = blocks // count
    width = values_in.shape[2]
    part = per * BLOCK
    scale = 1.0 / (values_in.shape[1] * count)
    shape = jax.ShapeDtypeStruct
    pair = shape((16, width), BF16)
    vmem, smem = pltpu.VMEM, pltpu.SMEM

    def body(f, *args):
        def kernel(*refs):
            f(*args, *refs)
        return kernel

    tables = (up_index, down_index, tick_order)
    weights = (w_up, w_down)

    def held(arrays, ints):
        return [smem(x.shape, x.dtype) for x in arrays[:ints]] + [vmem(x.shape, x.dtype) for x in arrays[ints:]]

    taken = (up_index, tick_order, score_grad_in, state_adjoint_in, saved_back, saved_second, saved_second_tan,
             saved_second_grad)
    ready_shape = shape((count, 5, 16, part), BF16)
    (ready,) = call(
        body(pack_ready, count, per), taken, [pl.ANY] * 8, [ready_shape],
        held(taken, 2) + [vmem(ready_shape.shape, BF16), pltpu.SemaphoreType.DMA((8,)), pltpu.SemaphoreType.DMA((count,))],
        limit=WIDE, out_space=pl.ANY)
    packed = ready
    ready = to_replicas(ready)
    taken = tables + (w_down, score_grad_in, state_adjoint_in, saved_second_grad, w_up, saved_back, saved_second,
                      saved_second_tan, values_in, tangent_in, saved_tan)
    bwd, fwd, keep, keep_tan, early = call(
        body(first_tick, count, per), taken, [pl.ANY] * 14,
        [pair, pair, shape((blocks, 24, BLOCK), F32), shape((blocks, 8, BLOCK), F32), ready_shape],
        held(taken, 3) + [vmem((blocks, 32, BLOCK), F32), vmem((blocks, 16, BLOCK), F32), vmem((blocks, 48, BLOCK), BF16),
                          vmem((blocks, 16, BLOCK), BF16), pltpu.SemaphoreType.DMA((14,))],
        limit=WIDE, after=(packed,))
    bwd = from_behind(bwd, "section", -1)
    fwd = from_behind(fwd, "section", 1)
    early = to_replicas(early)
    bwd, late = call(
        body(back_second, count, per),
        tables[:2] + weights + (bwd, keep), [smem] * 2 + [vmem] * 4,
        [pair, shape((count, 2, 16, part), BF16)],
        [pltpu.VMEM((blocks, 16, BLOCK), F32), pltpu.VMEM((blocks, 16, BLOCK), F32)])
    packed = bwd
    late = to_replicas(late)
    bwd = from_behind(bwd, "section", -1)
    (fwd,) = call(
        body(forward_second, blocks),
        tables[:2] + weights + (fwd, keep_tan), [smem] * 2 + [vmem] * 4,
        [pair], [pltpu.VMEM((blocks, 16, BLOCK), BF16)], after=(packed,))
    fwd = from_behind(fwd, "section", 1)
    stream = shape((1,) + values_in.shape[1:], BF16)
    grad = shape((1, per, BLOCK, BLOCK), BF16)
    return tuple(call(
        body(finish, count, per, scale), (fwd, bwd, ready, early, late), [vmem] * 5,
        [stream, stream, stream, stream, grad, grad], []))

def solution(mesh):
    layer = P("section", None, None, None)
    table = P("section", None)
    stream = P("section", "dp", None)
    saved = P("section", None, "dp", None)
    return jax.shard_map(
        on_device,
        mesh=mesh,
        in_specs=(layer, table, layer, table, table) + (stream,) * 4 + (saved,) * 5,
        out_specs=(stream,) * 4 + (P("section", "dp", None, None),) * 2,
        check_vma=False,
    )
```

```python
import jax
import jax.numpy as jnp
from jax import lax
from jax.experimental import pallas as pl
from jax.experimental.pallas import tpu as pltpu
from jax.sharding import PartitionSpec as P

BLOCK = 128
F32 = jnp.float32
BF16 = jnp.bfloat16
LIMIT = 40 * 1024 * 1024
WIDE = 60 * 1024 * 1024


def partner(me, step, count):
    if count & (count - 1) == 0:
        return me ^ step
    return lax.rem(me + step, count)


def swap_route(step, count):
    if count & (count - 1) == 0:
        return [(i, i ^ step) for i in range(count)]
    return [(i, (i + step) % count) for i in range(count)]


def swap_sections(near, far):
    count = lax.axis_size("section")
    far = lax.ppermute(far, "section", [(i, (i + 2 * (i % 2) - 1) % count) for i in range(count)])
    near = lax.ppermute(near, "section", [(i, i ^ 1) for i in range(count)])
    return near, far


def times(rows, weight):
    return lax.dot_general(rows, weight, (((1,), (0,)), ((), ())), preferred_element_type=F32)


def times_transposed(rows, weight):
    return lax.dot_general(rows, weight, (((1,), (1,)), ((), ())), preferred_element_type=F32)


def sigmoid(z):
    return 1.0 / (1.0 + jnp.exp(-z))


def slope_of(z, s):
    return s * (1.0 + z * (1.0 - s))


def lanes(block):
    if isinstance(block, int):
        return pl.ds(block * BLOCK, BLOCK)
    return pl.ds(pl.multiple_of(block * BLOCK, BLOCK), BLOCK)


def stack(parts):
    return jnp.concatenate([part.astype(F32) for part in parts], 0)


def send_order(me, count, per):
    for step in range(count):
        base = partner(me, step, count) * per
        for place in range(per):
            yield step, place, base + place


def start_all(copies):
    for copy in copies:
        copy.start()
    return copies


def wait_all(copies):
    for copy in copies:
        copy.wait()


def odd_section():
    return lax.rem(lax.axis_index("section"), 2)


def hand_out(packs, near, far):
    odd = odd_section()
    near[...] = packs[odd]
    far[...] = packs[1 - odd]


def take_in(near, far, packs):
    odd = odd_section()
    packs[1 - odd] = near[...]
    packs[odd] = far[...]


def back_first(count, per, copies, up_idx, down_idx, order, w_up, w_down, g_ref, a_ref, back, second, second_tan,
               second_grad, pack, keep, sends, pulled, returned, hidden):
    blocks = count * per
    me = lax.axis_index("dp")
    for b in range(blocks):
        pulled[b] = jnp.zeros(pulled.shape[1:], F32)
    wait_all(copies[:7])
    m0 = order[0, 0]
    m1 = order[0, 1]
    for b in range(blocks):
        returned[b] = stack([g_ref[0, :, lanes(b)], a_ref[0, :, lanes(b)]])
    for step, place, i in send_order(me, count, per):
        at = lanes(i)
        c = stack([g_ref[0, :, at], a_ref[0, :, at], second_grad[0, m0, :, at], second_grad[0, m1, :, at]]).astype(BF16)
        sends[step][8, :, lanes(place)] = c[0:16]
        sends[step][9, :, lanes(place)] = c[16:32]
        target = down_idx[0, i]
        pulled[target] = pulled[target] + times_transposed(c, w_down[0, i])
    wait_all(copies[7:11])
    for step, place, j in send_order(me, count, per):
        u = up_idx[0, j]
        at = lanes(u)
        x = stack([back[0, m0, :, at], second[0, m0, :, at], second_tan[0, m0, :, at],
                   second_tan[0, m1, :, at], back[0, m1, :, at], second[0, m1, :, at]]).astype(BF16)
        out = sends[step]
        here = lanes(place)
        for group in range(3):
            out[group, :, here] = x[16 * group:16 * group + 16]
        z = times(x, w_up[0, j])
        zb0, za0, ta0, ta1, zb1, za1 = (z[8 * k:8 * k + 8] for k in range(6))
        pg, pa, ga0, ga1 = (pulled[j, 8 * k:8 * k + 8] for k in range(4))
        sb0, sa0, sb1, sa1 = sigmoid(zb0), sigmoid(za0), sigmoid(zb1), sigmoid(za1)
        slope_a0 = slope_of(za0, sa0)
        slope_a1 = slope_of(za1, sa1)
        curve_a0 = sa0 * (1.0 - sa0) * (2.0 + za0 * (1.0 - 2.0 * sa0))
        curve_a1 = sa1 * (1.0 - sa1) * (2.0 + za1 * (1.0 - 2.0 * sa1))
        push = slope_a0 * pa + curve_a0 * ga0 * ta0
        e = jnp.concatenate([slope_of(zb0, sb0) * pg, push], 0).astype(BF16)
        out[3, :, here] = e
        out[4, :, here] = jnp.concatenate([slope_a0 * ga0, slope_a1 * ga1], 0).astype(BF16)
        hidden[j] = jnp.concatenate(
            [zb0 * sb0, za0 * sa0, slope_a0 * ta0, slope_a1 * ta1, zb1 * sb1, za1 * sa1], 0).astype(BF16)
        keep[j] = jnp.concatenate([slope_of(zb1, sb1), slope_a1, curve_a1 * ga1 * ta1], 0)
        returned[u] = returned[u] + times_transposed(e, w_up[0, j])
    for b in range(blocks):
        pack[:, lanes(b)] = returned[b].astype(BF16)
    for step, place, i in send_order(me, count, per):
        y = hidden[down_idx[0, i]]
        for group in range(3):
            sends[step][5 + group, :, lanes(place)] = y[16 * group:16 * group + 16]


def forward_first(blocks, up_idx, down_idx, order, w_up, w_down, v_ref, t_ref, tan, pack, keep, hidden):
    m0 = order[0, 0]
    m1 = order[0, 1]
    for j in range(blocks):
        at = lanes(up_idx[0, j])
        x = stack([v_ref[0, :, at], t_ref[0, :, at], tan[0, m0, :, at], tan[0, m1, :, at]]).astype(BF16)
        z = times(x, w_up[0, j])
        zv, zt, z0, z1 = (z[8 * k:8 * k + 8] for k in range(4))
        hidden[j] = jnp.concatenate([zv * sigmoid(zv), slope_of(z0, sigmoid(z0)) * zt], 0).astype(BF16)
        keep[j] = slope_of(z1, sigmoid(z1))
    for i in range(blocks):
        at = lanes(i)
        moved = stack([v_ref[0, :, at], t_ref[0, :, at]]) + times(hidden[down_idx[0, i]], w_down[0, i])
        pack[:, at] = moved.astype(BF16)


def first_tick(count, per, *refs):
    sources, (near, far, keep, keep_tan) = refs[:14], refs[14:18]
    sends, held = refs[18:18 + count], refs[18 + count:32 + count]
    packs, pulled, returned, hidden, hidden_fwd, sems = refs[32 + count:]
    copies = start_all([pltpu.make_async_copy(s, t, sems.at[k]) for k, (s, t) in enumerate(zip(sources, held))])
    up_idx, down_idx, order, w_down, g_ref, a_ref, second_grad, w_up, back, second, second_tan, v_ref, t_ref, tan = held
    back_first(count, per, copies, up_idx, down_idx, order, w_up, w_down, g_ref, a_ref, back, second, second_tan,
               second_grad, packs.at[1], keep, sends, pulled, returned, hidden)
    wait_all(copies[11:])
    forward_first(count * per, up_idx, down_idx, order, w_up, w_down, v_ref, t_ref, tan, packs.at[0], keep_tan, hidden_fwd)
    hand_out(packs, near, far)


def back_second(count, per, up_idx, down_idx, w_up, w_down, rows, keep, pack, sends, pulled, returned):
    blocks = count * per
    me = lax.axis_index("dp")
    for b in range(blocks):
        pulled[b] = jnp.zeros(pulled.shape[1:], F32)
        returned[b] = rows[:, lanes(b)].astype(F32)
    for step, place, i in send_order(me, count, per):
        c = rows[:, lanes(i)]
        sends[step][1, :, lanes(place)] = c
        target = down_idx[0, i]
        pulled[target] = pulled[target] + times_transposed(c, w_down[0, i])
    for step, place, j in send_order(me, count, per):
        u = up_idx[0, j]
        slope_b, slope_a, push = (keep[j, 8 * k:8 * k + 8] for k in range(3))
        e = jnp.concatenate([slope_b * pulled[j, 0:8], slope_a * pulled[j, 8:16] + push], 0).astype(BF16)
        sends[step][0, :, lanes(place)] = e
        returned[u] = returned[u] + times_transposed(e, w_up[0, j])
    for b in range(blocks):
        pack[:, lanes(b)] = returned[b].astype(BF16)


def forward_second(blocks, up_idx, down_idx, w_up, w_down, rows, keep, pack, hidden):
    for j in range(blocks):
        z = times(rows[:, lanes(up_idx[0, j])], w_up[0, j])
        zv, zt = z[0:8], z[8:16]
        hidden[j] = jnp.concatenate([zv * sigmoid(zv), keep[j] * zt], 0).astype(BF16)
    for i in range(blocks):
        at = lanes(i)
        pack[:, at] = (rows[:, at].astype(F32) + times(hidden[down_idx[0, i]], w_down[0, i])).astype(BF16)


def second_tick(count, per, up_idx, down_idx, w_up, w_down, near_in, far_in, keep, keep_tan, near, far, *refs):
    sends, (came, packs, pulled, returned, hidden) = refs[:count], refs[count:]
    take_in(near_in, far_in, came)
    back_second(count, per, up_idx, down_idx, w_up, w_down, came.at[1], keep, packs.at[1], sends, pulled, returned)
    forward_second(count * per, up_idx, down_idx, w_up, w_down, came.at[0], keep_tan, packs.at[0], hidden)
    hand_out(packs, near, far)


def finish(count, per, scale, near, far, *rest):
    early = rest[:count]
    late = rest[count:2 * count]
    values, score, tangent, adjoint, grad_up, grad_down, came = rest[2 * count:]
    take_in(near, far, came)
    moved = came[0].astype(F32)
    values[0] = moved[0:8].astype(BF16)
    tangent[0] = moved[8:16].astype(BF16)
    moved = came[1].astype(F32)
    score[0] = moved[0:8].astype(BF16)
    adjoint[0] = moved[8:16].astype(BF16)
    for place in range(per):
        at = lanes(place)
        for out, left, right, last in ((grad_up, (0, 1, 2), (3, 4), 0), (grad_down, (5, 6, 7), (8, 9), 1)):
            xs, es = [], []
            for source in range(count):
                xs += [early[source][k, :, at] for k in left]
                es += [early[source][k, :, at] for k in right] + [late[source][last, :, at]]
            total = lax.dot_general(jnp.concatenate(xs, 0), jnp.concatenate(es, 0), (((0,), (0,)), ((), ())),
                                    preferred_element_type=F32)
            out[0, place] = (total * scale).astype(BF16)


def call(body, operands, spaces, outs, scratch, limit=LIMIT, out_space=pltpu.VMEM, after=()):
    moved = sum(x.size * x.dtype.itemsize for x in list(operands) + list(outs))
    taken = len(operands)

    def kernel(*refs):
        body(*refs[:taken], *refs[taken + len(after):])

    return pl.pallas_call(
        kernel,
        out_shape=outs,
        in_specs=[pl.BlockSpec(memory_space=space) for space in spaces] + [pl.BlockSpec(memory_space=pl.ANY)] * len(after),
        out_specs=[pl.BlockSpec(memory_space=out_space)] * len(outs),
        scratch_shapes=scratch,
        compiler_params=pltpu.CompilerParams(vmem_limit_bytes=limit),
        cost_estimate=pl.CostEstimate(flops=0, bytes_accessed=moved, transcendentals=0),
    )(*operands, *after)


def on_device(w_up, up_index, w_down, down_index, tick_order, values_in, score_grad_in, tangent_in, state_adjoint_in,
              saved_back, saved_tan, saved_second, saved_second_tan, saved_second_grad):
    count = lax.axis_size("dp")
    blocks = w_up.shape[1]
    per = blocks // count
    width = values_in.shape[2]
    part = per * BLOCK
    scale = 1.0 / (values_in.shape[1] * count)
    shape = jax.ShapeDtypeStruct
    pair = shape((16, width), BF16)
    vmem, smem = pltpu.VMEM, pltpu.SMEM

    def body(f, *args):
        def kernel(*refs):
            f(*args, *refs)
        return kernel

    def to_replicas(parts):
        return parts[:1] + [lax.ppermute(parts[step], "dp", swap_route(step, count)) for step in range(1, count)]

    taken = (up_index, down_index, tick_order, w_down, score_grad_in, state_adjoint_in, saved_second_grad, w_up,
             saved_back, saved_second, saved_second_tan, values_in, tangent_in, saved_tan)
    near, far, keep, keep_tan, *early = call(
        body(first_tick, count, per), taken, [pl.ANY] * 14,
        [pair, pair, shape((blocks, 24, BLOCK), F32), shape((blocks, 8, BLOCK), F32)]
        + [shape((10, 16, part), BF16)] * count,
        [smem(x.shape, x.dtype) for x in taken[:3]] + [vmem(x.shape, x.dtype) for x in taken[3:]]
        + [vmem((2, 16, width), BF16), vmem((blocks, 32, BLOCK), F32), vmem((blocks, 16, BLOCK), F32),
           vmem((blocks, 48, BLOCK), BF16), vmem((blocks, 16, BLOCK), BF16), pltpu.SemaphoreType.DMA((14,))],
        limit=WIDE)
    near, far = swap_sections(near, far)
    early = to_replicas(early)
    near, far, *late = call(
        body(second_tick, count, per), (up_index, down_index, w_up, w_down, near, far, keep, keep_tan),
        [smem] * 2 + [vmem] * 6,
        [pair, pair] + [shape((2, 16, part), BF16)] * count,
        [vmem((2, 16, width), BF16), vmem((2, 16, width), BF16), vmem((blocks, 16, BLOCK), F32),
         vmem((blocks, 16, BLOCK), F32), vmem((blocks, 16, BLOCK), BF16)])
    near, far = swap_sections(near, far)
    late = to_replicas(late)
    stream = shape((1,) + values_in.shape[1:], BF16)
    grad = shape((1, per, BLOCK, BLOCK), BF16)
    return tuple(call(
        body(finish, count, per, scale), (near, far, *early, *late), [vmem] * (2 + 2 * count),
        [stream, stream, stream, stream, grad, grad], [vmem((2, 16, width), BF16)]))


def solution(mesh):
    layer = P("section", None, None, None)
    table = P("section", None)
    stream = P("section", "dp", None)
    saved = P("section", None, "dp", None)
    return jax.shard_map(
        on_device,
        mesh=mesh,
        in_specs=(layer, table, layer, table, table) + (stream,) * 4 + (saved,) * 5,
        out_specs=(stream,) * 4 + (P("section", "dp", None, None),) * 2,
        check_vma=False,
    )
```

```python
import jax
import jax.numpy as jnp
from jax import lax
from jax.experimental import pallas as pl
from jax.experimental.pallas import tpu as pltpu
from jax.sharding import PartitionSpec as P

BLOCK = 128
F32 = jnp.float32
BF16 = jnp.bfloat16
LIMIT = 40 * 1024 * 1024
WORK = 10 ** 10


def partner(me, step, count):
    if count & (count - 1) == 0:
        return me ^ step
    return lax.rem(me + step, count)


def swap_route(step, count):
    if count & (count - 1) == 0:
        return [(i, i ^ step) for i in range(count)]
    return [(i, (i + step) % count) for i in range(count)]


def swap_sections(near, far):
    count = lax.axis_size("section")
    far = lax.ppermute(far, "section", [(i, (i + 2 * (i % 2) - 1) % count) for i in range(count)])
    near = lax.ppermute(near, "section", [(i, i ^ 1) for i in range(count)])
    return near, far


def times(rows, weight):
    return lax.dot_general(rows, weight, (((1,), (0,)), ((), ())), preferred_element_type=F32)


def times_transposed(rows, weight):
    return lax.dot_general(rows, weight, (((1,), (1,)), ((), ())), preferred_element_type=F32)


def outer(xs, es):
    return lax.dot_general(jnp.concatenate(xs, 0), jnp.concatenate(es, 0), (((0,), (0,)), ((), ())),
                           preferred_element_type=F32)


def sigmoid(z):
    return 1.0 / (1.0 + jnp.exp(-z))


def slope_of(z, s):
    return s * (1.0 + z * (1.0 - s))


def lanes(block):
    if isinstance(block, int):
        return pl.ds(block * BLOCK, BLOCK)
    return pl.ds(pl.multiple_of(block * BLOCK, BLOCK), BLOCK)


def stack(parts):
    return jnp.concatenate([part.astype(F32) for part in parts], 0)


def send_order(me, count, per):
    for step in range(count):
        base = partner(me, step, count) * per
        for place in range(per):
            yield step, place, base + place


def odd_section():
    return lax.rem(lax.axis_index("section"), 2)


def hand_out(packs, near, far):
    odd = odd_section()
    near[...] = packs[odd]
    far[...] = packs[1 - odd]


def take_in(near, far, packs):
    odd = odd_section()
    packs[1 - odd] = near[...]
    packs[odd] = far[...]


def open_launch(token):
    token[...] = jnp.zeros(token.shape, F32)


def pack_ready(count, per, up_idx, order, g_ref, a_ref, back, second, second_tan, second_grad, *sends):
    m0 = order[0, 0]
    m1 = order[0, 1]
    for step, place, j in send_order(lax.axis_index("dp"), count, per):
        out, here = sends[step], lanes(place)
        at = lanes(up_idx[0, j])
        out[0, :, here] = stack([back[0, m0, :, at], second[0, m0, :, at]]).astype(BF16)
        out[1, :, here] = stack([second_tan[0, m0, :, at], second_tan[0, m1, :, at]]).astype(BF16)
        out[2, :, here] = stack([back[0, m1, :, at], second[0, m1, :, at]]).astype(BF16)
        at = lanes(j)
        out[3, :, here] = stack([g_ref[0, :, at], a_ref[0, :, at]]).astype(BF16)
        out[4, :, here] = stack([second_grad[0, m0, :, at], second_grad[0, m1, :, at]]).astype(BF16)


def back_first(count, per, up_idx, down_idx, order, w_up, w_down, g_ref, a_ref, back, second, second_tan,
               second_grad, pack, keep, sends, pulled, returned, hidden):
    blocks = count * per
    me = lax.axis_index("dp")
    for b in range(blocks):
        pulled[b] = jnp.zeros(pulled.shape[1:], F32)
    m0 = order[0, 0]
    m1 = order[0, 1]
    for b in range(blocks):
        returned[b] = stack([g_ref[0, :, lanes(b)], a_ref[0, :, lanes(b)]])
    for step, place, i in send_order(me, count, per):
        at = lanes(i)
        c = stack([g_ref[0, :, at], a_ref[0, :, at], second_grad[0, m0, :, at], second_grad[0, m1, :, at]]).astype(BF16)
        target = down_idx[0, i]
        pulled[target] = pulled[target] + times_transposed(c, w_down[0, i])
    for step, place, j in send_order(me, count, per):
        u = up_idx[0, j]
        at = lanes(u)
        x = stack([back[0, m0, :, at], second[0, m0, :, at], second_tan[0, m0, :, at],
                   second_tan[0, m1, :, at], back[0, m1, :, at], second[0, m1, :, at]]).astype(BF16)
        out = sends[step]
        here = lanes(place)
        z = times(x, w_up[0, j])
        zb0, za0, ta0, ta1, zb1, za1 = (z[8 * k:8 * k + 8] for k in range(6))
        pg, pa, ga0, ga1 = (pulled[j, 8 * k:8 * k + 8] for k in range(4))
        sb0, sa0, sb1, sa1 = sigmoid(zb0), sigmoid(za0), sigmoid(zb1), sigmoid(za1)
        slope_a0 = slope_of(za0, sa0)
        slope_a1 = slope_of(za1, sa1)
        curve_a0 = sa0 * (1.0 - sa0) * (2.0 + za0 * (1.0 - 2.0 * sa0))
        curve_a1 = sa1 * (1.0 - sa1) * (2.0 + za1 * (1.0 - 2.0 * sa1))
        push = slope_a0 * pa + curve_a0 * ga0 * ta0
        e = jnp.concatenate([slope_of(zb0, sb0) * pg, push], 0).astype(BF16)
        out[0, :, here] = e
        out[1, :, here] = jnp.concatenate([slope_a0 * ga0, slope_a1 * ga1], 0).astype(BF16)
        hidden[j] = jnp.concatenate(
            [zb0 * sb0, za0 * sa0, slope_a0 * ta0, slope_a1 * ta1, zb1 * sb1, za1 * sa1], 0).astype(BF16)
        keep[j] = jnp.concatenate([slope_of(zb1, sb1), slope_a1, curve_a1 * ga1 * ta1], 0)
        returned[u] = returned[u] + times_transposed(e, w_up[0, j])
    for b in range(blocks):
        pack[:, lanes(b)] = returned[b].astype(BF16)
    for step, place, i in send_order(me, count, per):
        y = hidden[down_idx[0, i]]
        for group in range(3):
            sends[step][2 + group, :, lanes(place)] = y[16 * group:16 * group + 16]


def forward_first(blocks, up_idx, down_idx, order, w_up, w_down, v_ref, t_ref, tan, pack, keep, hidden):
    m0 = order[0, 0]
    m1 = order[0, 1]
    for j in range(blocks):
        at = lanes(up_idx[0, j])
        x = stack([v_ref[0, :, at], t_ref[0, :, at], tan[0, m0, :, at], tan[0, m1, :, at]]).astype(BF16)
        z = times(x, w_up[0, j])
        zv, zt, z0, z1 = (z[8 * k:8 * k + 8] for k in range(4))
        hidden[j] = jnp.concatenate([zv * sigmoid(zv), slope_of(z0, sigmoid(z0)) * zt], 0).astype(BF16)
        keep[j] = slope_of(z1, sigmoid(z1))
    for i in range(blocks):
        at = lanes(i)
        moved = stack([v_ref[0, :, at], t_ref[0, :, at]]) + times(hidden[down_idx[0, i]], w_down[0, i])
        pack[:, at] = moved.astype(BF16)


def first_tick(count, per, up_idx, down_idx, order, w_up, w_down, g_ref, a_ref, back, second, second_tan, second_grad,
               v_ref, t_ref, tan, near, far, keep, keep_tan, *refs):
    sends, (packs, pulled, returned, hidden, hidden_fwd) = refs[:count], refs[count:]
    back_first(count, per, up_idx, down_idx, order, w_up, w_down, g_ref, a_ref, back, second, second_tan,
               second_grad, packs.at[1], keep, sends, pulled, returned, hidden)
    forward_first(count * per, up_idx, down_idx, order, w_up, w_down, v_ref, t_ref, tan, packs.at[0], keep_tan, hidden_fwd)
    hand_out(packs, near, far)


def back_second(count, per, up_idx, down_idx, w_up, w_down, rows, keep, pack, sends, pulled, returned):
    blocks = count * per
    me = lax.axis_index("dp")
    for b in range(blocks):
        pulled[b] = jnp.zeros(pulled.shape[1:], F32)
        returned[b] = rows[:, lanes(b)].astype(F32)
    for step, place, i in send_order(me, count, per):
        c = rows[:, lanes(i)]
        sends[step][1, :, lanes(place)] = c
        target = down_idx[0, i]
        pulled[target] = pulled[target] + times_transposed(c, w_down[0, i])
    for step, place, j in send_order(me, count, per):
        u = up_idx[0, j]
        slope_b, slope_a, push = (keep[j, 8 * k:8 * k + 8] for k in range(3))
        e = jnp.concatenate([slope_b * pulled[j, 0:8], slope_a * pulled[j, 8:16] + push], 0).astype(BF16)
        sends[step][0, :, lanes(place)] = e
        returned[u] = returned[u] + times_transposed(e, w_up[0, j])
    for b in range(blocks):
        pack[:, lanes(b)] = returned[b].astype(BF16)


def forward_second(blocks, up_idx, down_idx, w_up, w_down, rows, keep, pack, hidden):
    for j in range(blocks):
        z = times(rows[:, lanes(up_idx[0, j])], w_up[0, j])
        zv, zt = z[0:8], z[8:16]
        hidden[j] = jnp.concatenate([zv * sigmoid(zv), keep[j] * zt], 0).astype(BF16)
    for i in range(blocks):
        at = lanes(i)
        pack[:, at] = (rows[:, at].astype(F32) + times(hidden[down_idx[0, i]], w_down[0, i])).astype(BF16)


def second_tick(count, per, up_idx, down_idx, w_up, w_down, near_in, far_in, keep, keep_tan, near, far, *refs):
    sends, (came, packs, pulled, returned, hidden) = refs[:count], refs[count:]
    take_in(near_in, far_in, came)
    back_second(count, per, up_idx, down_idx, w_up, w_down, came.at[1], keep, packs.at[1], sends, pulled, returned)
    forward_second(count * per, up_idx, down_idx, w_up, w_down, came.at[0], keep_tan, packs.at[0], hidden)
    hand_out(packs, near, far)


def early_grads(count, per, *refs):
    ready, early, late = refs[:count], refs[count:2 * count], refs[2 * count:3 * count]
    grads, sends = refs[3 * count], refs[3 * count + 1:]
    for source in range(count):
        sends[source][...] = late[source][...]
    for place in range(per):
        at = lanes(place)
        for out in range(2):
            left, right = (ready, early) if out == 0 else (early, ready)
            first_left, first_right = (0, 0) if out == 0 else (2, 3)
            xs = [left[source][first_left + k, :, at] for source in range(count) for k in range(2)]
            es = [right[source][first_right + k, :, at] for source in range(count) for k in range(2)]
            grads[out, place] = outer(xs, es)


def finish(count, per, scale, near, far, grads, *rest):
    ready, early, late = rest[:count], rest[count:2 * count], rest[2 * count:3 * count]
    values, score, tangent, adjoint, grad_up, grad_down, came = rest[3 * count:]
    take_in(near, far, came)
    moved = came[0].astype(F32)
    values[0] = moved[0:8].astype(BF16)
    tangent[0] = moved[8:16].astype(BF16)
    moved = came[1].astype(F32)
    score[0] = moved[0:8].astype(BF16)
    adjoint[0] = moved[8:16].astype(BF16)
    for place in range(per):
        at = lanes(place)
        for k, (out, left, group) in enumerate(((grad_up, ready, 2), (grad_down, early, 4))):
            xs = [left[source][group, :, at] for source in range(count)]
            es = [late[source][k, :, at] for source in range(count)]
            out[0, place] = ((grads[k, place] + outer(xs, es)) * scale).astype(BF16)


def call(body, operands, spaces, outs, scratch, after=()):
    taken = len(operands)

    def kernel(*refs):
        body(*refs[:taken], *refs[taken + len(after):])

    return pl.pallas_call(
        kernel,
        out_shape=outs,
        in_specs=[pl.BlockSpec(memory_space=space) for space in spaces] + [pl.BlockSpec(memory_space=pl.ANY)] * len(after),
        out_specs=[pl.BlockSpec(memory_space=pltpu.VMEM)] * len(outs),
        scratch_shapes=scratch,
        compiler_params=pltpu.CompilerParams(vmem_limit_bytes=LIMIT),
        cost_estimate=pl.CostEstimate(flops=WORK, bytes_accessed=WORK // 100, transcendentals=0),
    )(*operands, *after)


def on_device(w_up, up_index, w_down, down_index, tick_order, values_in, score_grad_in, tangent_in, state_adjoint_in,
              saved_back, saved_tan, saved_second, saved_second_tan, saved_second_grad):
    count = lax.axis_size("dp")
    blocks = w_up.shape[1]
    per = blocks // count
    width = values_in.shape[2]
    part = per * BLOCK
    scale = 1.0 / (values_in.shape[1] * count)
    shape = jax.ShapeDtypeStruct
    pair = shape((16, width), BF16)
    vmem, smem = pltpu.VMEM, pltpu.SMEM

    def body(f, *args):
        def kernel(*refs):
            f(*args, *refs)
        return kernel

    def to_replicas(parts):
        return [parts[0]] + [lax.ppermute(parts[step], "dp", swap_route(step, count)) for step in range(1, count)]

    rows = (score_grad_in, state_adjoint_in, saved_back, saved_second, saved_second_tan, saved_second_grad)
    five = shape((5, 16, part), BF16)
    (token,) = call(open_launch, (), [], [shape((8, BLOCK), F32)], [])
    ready = call(
        body(pack_ready, count, per), (up_index, tick_order) + rows, [smem] * 2 + [vmem] * 6, [five] * count, [],
        after=(token,))
    packed = ready[0]
    ready = to_replicas(ready)
    near, far, keep, keep_tan, *early = call(
        body(first_tick, count, per),
        (up_index, down_index, tick_order, w_up, w_down) + rows + (values_in, tangent_in, saved_tan),
        [smem] * 3 + [vmem] * 11,
        [pair, pair, shape((blocks, 24, BLOCK), F32), shape((blocks, 8, BLOCK), F32)] + [five] * count,
        [vmem((2, 16, width), BF16), vmem((blocks, 32, BLOCK), F32), vmem((blocks, 16, BLOCK), F32),
         vmem((blocks, 48, BLOCK), BF16), vmem((blocks, 16, BLOCK), BF16)],
        after=(packed,))
    near, far = swap_sections(near, far)
    early = to_replicas(early)
    near, far, *late = call(
        body(second_tick, count, per), (up_index, down_index, w_up, w_down, near, far, keep, keep_tan),
        [smem] * 2 + [vmem] * 6,
        [pair, pair] + [shape((2, 16, part), BF16)] * count,
        [vmem((2, 16, width), BF16), vmem((2, 16, width), BF16), vmem((blocks, 16, BLOCK), F32),
         vmem((blocks, 16, BLOCK), F32), vmem((blocks, 16, BLOCK), BF16)],
        after=tuple(ready[1:]))
    near, far = swap_sections(near, far)
    two = shape((2, 16, part), BF16)
    grads, *late = call(
        body(early_grads, count, per), (*ready, *early, *late), [vmem] * (3 * count),
        [shape((2, per, BLOCK, BLOCK), F32)] + [two] * count, [])
    late = to_replicas(late)
    stream = shape((1,) + values_in.shape[1:], BF16)
    grad = shape((1, per, BLOCK, BLOCK), BF16)
    return tuple(call(
        body(finish, count, per, scale), (near, far, grads, *ready, *early, *late), [vmem] * (3 + 3 * count),
        [stream, stream, stream, stream, grad, grad], [vmem((2, 16, width), BF16)]))


def solution(mesh):
    layer = P("section", None, None, None)
    table = P("section", None)
    stream = P("section", "dp", None)
    saved = P("section", None, "dp", None)
    return jax.shard_map(
        on_device,
        mesh=mesh,
        in_specs=(layer, table, layer, table, table) + (stream,) * 4 + (saved,) * 5,
        out_specs=(stream,) * 4 + (P("section", "dp", None, None),) * 2,
        check_vma=False,
    )
```

```python
import jax
import jax.numpy as jnp
from jax import lax
from jax.experimental import pallas as pl
from jax.experimental.pallas import tpu as pltpu
from jax.sharding import PartitionSpec as P

BLOCK = 128
F32 = jnp.float32
BF16 = jnp.bfloat16
LIMIT = 40 * 1024 * 1024
WORK = 10 ** 10
LIGHT = 10 ** 4


def partner(me, step, count):
    if count & (count - 1) == 0:
        return me ^ step
    return lax.rem(me + step, count)


def swap_route(step, count):
    if count & (count - 1) == 0:
        return [(i, i ^ step) for i in range(count)]
    return [(i, (i + step) % count) for i in range(count)]


def swap_sections(near, far):
    count = lax.axis_size("section")
    far = lax.ppermute(far, "section", [(i, (i + 2 * (i % 2) - 1) % count) for i in range(count)])
    near = lax.ppermute(near, "section", [(i, i ^ 1) for i in range(count)])
    return near, far


def times(rows, weight):
    return lax.dot_general(rows, weight, (((1,), (0,)), ((), ())), preferred_element_type=F32)


def times_transposed(rows, weight):
    return lax.dot_general(rows, weight, (((1,), (1,)), ((), ())), preferred_element_type=F32)


def outer(xs, es):
    return lax.dot_general(jnp.concatenate(xs, 0), jnp.concatenate(es, 0), (((0,), (0,)), ((), ())),
                           preferred_element_type=F32)


def sigmoid(z):
    return 1.0 / (1.0 + jnp.exp(-z))


def slope_of(z, s):
    return s * (1.0 + z * (1.0 - s))


def lanes(block):
    if isinstance(block, int):
        return pl.ds(block * BLOCK, BLOCK)
    return pl.ds(pl.multiple_of(block * BLOCK, BLOCK), BLOCK)


def stack(parts):
    return jnp.concatenate([part.astype(F32) for part in parts], 0)


def send_order(me, count, per):
    for step in range(count):
        base = partner(me, step, count) * per
        for place in range(per):
            yield step, place, base + place


def odd_section():
    return lax.rem(lax.axis_index("section"), 2)


def hand_out(packs, near, far):
    odd = odd_section()
    near[...] = packs[odd]
    far[...] = packs[1 - odd]


def take_in(near, far, packs):
    odd = odd_section()
    packs[1 - odd] = near[...]
    packs[odd] = far[...]


def open_launch(token):
    token[...] = jnp.zeros(token.shape, F32)


def back_first(count, per, up_idx, down_idx, order, w_up, w_down, g_ref, a_ref, back, second, second_tan,
               second_grad, pack, keep, sends, pulled, returned, hidden):
    blocks = count * per
    me = lax.axis_index("dp")
    for b in range(blocks):
        pulled[b] = jnp.zeros(pulled.shape[1:], F32)
    m0 = order[0, 0]
    m1 = order[0, 1]
    for b in range(blocks):
        returned[b] = stack([g_ref[0, :, lanes(b)], a_ref[0, :, lanes(b)]])
    for step, place, i in send_order(me, count, per):
        at = lanes(i)
        c = stack([g_ref[0, :, at], a_ref[0, :, at], second_grad[0, m0, :, at], second_grad[0, m1, :, at]]).astype(BF16)
        sends[step][8, :, lanes(place)] = c[0:16]
        sends[step][9, :, lanes(place)] = c[16:32]
        target = down_idx[0, i]
        pulled[target] = pulled[target] + times_transposed(c, w_down[0, i])
    for step, place, j in send_order(me, count, per):
        u = up_idx[0, j]
        at = lanes(u)
        x = stack([back[0, m0, :, at], second[0, m0, :, at], second_tan[0, m0, :, at],
                   second_tan[0, m1, :, at], back[0, m1, :, at], second[0, m1, :, at]]).astype(BF16)
        out = sends[step]
        here = lanes(place)
        for group in range(3):
            out[group, :, here] = x[16 * group:16 * group + 16]
        z = times(x, w_up[0, j])
        zb0, za0, ta0, ta1, zb1, za1 = (z[8 * k:8 * k + 8] for k in range(6))
        pg, pa, ga0, ga1 = (pulled[j, 8 * k:8 * k + 8] for k in range(4))
        sb0, sa0, sb1, sa1 = sigmoid(zb0), sigmoid(za0), sigmoid(zb1), sigmoid(za1)
        slope_a0 = slope_of(za0, sa0)
        slope_a1 = slope_of(za1, sa1)
        curve_a0 = sa0 * (1.0 - sa0) * (2.0 + za0 * (1.0 - 2.0 * sa0))
        curve_a1 = sa1 * (1.0 - sa1) * (2.0 + za1 * (1.0 - 2.0 * sa1))
        push = slope_a0 * pa + curve_a0 * ga0 * ta0
        e = jnp.concatenate([slope_of(zb0, sb0) * pg, push], 0).astype(BF16)
        out[3, :, here] = e
        out[4, :, here] = jnp.concatenate([slope_a0 * ga0, slope_a1 * ga1], 0).astype(BF16)
        hidden[j] = jnp.concatenate(
            [zb0 * sb0, za0 * sa0, slope_a0 * ta0, slope_a1 * ta1, zb1 * sb1, za1 * sa1], 0).astype(BF16)
        keep[j] = jnp.concatenate([slope_of(zb1, sb1), slope_a1, curve_a1 * ga1 * ta1], 0)
        returned[u] = returned[u] + times_transposed(e, w_up[0, j])
    for b in range(blocks):
        pack[:, lanes(b)] = returned[b].astype(BF16)
    for step, place, i in send_order(me, count, per):
        y = hidden[down_idx[0, i]]
        for group in range(3):
            sends[step][5 + group, :, lanes(place)] = y[16 * group:16 * group + 16]


def forward_first(blocks, up_idx, down_idx, order, w_up, w_down, v_ref, t_ref, tan, pack, keep, hidden):
    m0 = order[0, 0]
    m1 = order[0, 1]
    for j in range(blocks):
        at = lanes(up_idx[0, j])
        x = stack([v_ref[0, :, at], t_ref[0, :, at], tan[0, m0, :, at], tan[0, m1, :, at]]).astype(BF16)
        z = times(x, w_up[0, j])
        zv, zt, z0, z1 = (z[8 * k:8 * k + 8] for k in range(4))
        hidden[j] = jnp.concatenate([zv * sigmoid(zv), slope_of(z0, sigmoid(z0)) * zt], 0).astype(BF16)
        keep[j] = slope_of(z1, sigmoid(z1))
    for i in range(blocks):
        at = lanes(i)
        moved = stack([v_ref[0, :, at], t_ref[0, :, at]]) + times(hidden[down_idx[0, i]], w_down[0, i])
        pack[:, at] = moved.astype(BF16)


def first_tick(count, per, up_idx, down_idx, order, w_up, w_down, g_ref, a_ref, back, second, second_tan, second_grad,
               v_ref, t_ref, tan, near, far, keep, keep_tan, *refs):
    sends, (packs, pulled, returned, hidden, hidden_fwd) = refs[:count], refs[count:]
    back_first(count, per, up_idx, down_idx, order, w_up, w_down, g_ref, a_ref, back, second, second_tan,
               second_grad, packs.at[1], keep, sends, pulled, returned, hidden)
    forward_first(count * per, up_idx, down_idx, order, w_up, w_down, v_ref, t_ref, tan, packs.at[0], keep_tan, hidden_fwd)
    hand_out(packs, near, far)


def back_second(count, per, up_idx, down_idx, w_up, w_down, rows, keep, pack, sends, pulled, returned):
    blocks = count * per
    me = lax.axis_index("dp")
    for b in range(blocks):
        pulled[b] = jnp.zeros(pulled.shape[1:], F32)
        returned[b] = rows[:, lanes(b)].astype(F32)
    for step, place, i in send_order(me, count, per):
        c = rows[:, lanes(i)]
        sends[step][1, :, lanes(place)] = c
        target = down_idx[0, i]
        pulled[target] = pulled[target] + times_transposed(c, w_down[0, i])
    for step, place, j in send_order(me, count, per):
        u = up_idx[0, j]
        slope_b, slope_a, push = (keep[j, 8 * k:8 * k + 8] for k in range(3))
        e = jnp.concatenate([slope_b * pulled[j, 0:8], slope_a * pulled[j, 8:16] + push], 0).astype(BF16)
        sends[step][0, :, lanes(place)] = e
        returned[u] = returned[u] + times_transposed(e, w_up[0, j])
    for b in range(blocks):
        pack[:, lanes(b)] = returned[b].astype(BF16)


def forward_second(blocks, up_idx, down_idx, w_up, w_down, rows, keep, pack, hidden):
    for j in range(blocks):
        z = times(rows[:, lanes(up_idx[0, j])], w_up[0, j])
        zv, zt = z[0:8], z[8:16]
        hidden[j] = jnp.concatenate([zv * sigmoid(zv), keep[j] * zt], 0).astype(BF16)
    for i in range(blocks):
        at = lanes(i)
        pack[:, at] = (rows[:, at].astype(F32) + times(hidden[down_idx[0, i]], w_down[0, i])).astype(BF16)


def second_tick(count, per, up_idx, down_idx, w_up, w_down, near_in, far_in, keep, keep_tan, near, far, *refs):
    sends, (came, packs, pulled, returned, hidden) = refs[:count], refs[count:]
    take_in(near_in, far_in, came)
    back_second(count, per, up_idx, down_idx, w_up, w_down, came.at[1], keep, packs.at[1], sends, pulled, returned)
    forward_second(count * per, up_idx, down_idx, w_up, w_down, came.at[0], keep_tan, packs.at[0], hidden)
    hand_out(packs, near, far)


def early_grads(count, per, *refs):
    early, late = refs[:count], refs[count:2 * count]
    grads, sends = refs[2 * count], refs[2 * count + 1:]
    for source in range(count):
        sends[source][...] = late[source][...]
    for place in range(per):
        at = lanes(place)
        for out, left, right in ((0, 0, 3), (1, 5, 8)):
            xs = [early[source][left + k, :, at] for source in range(count) for k in range(2)]
            es = [early[source][right + k, :, at] for source in range(count) for k in range(2)]
            grads[out, place] = outer(xs, es)


def finish(count, per, scale, near, far, grads, *rest):
    early, late = rest[:count], rest[count:2 * count]
    values, score, tangent, adjoint, grad_up, grad_down, came = rest[2 * count:]
    take_in(near, far, came)
    moved = came[0].astype(F32)
    values[0] = moved[0:8].astype(BF16)
    tangent[0] = moved[8:16].astype(BF16)
    moved = came[1].astype(F32)
    score[0] = moved[0:8].astype(BF16)
    adjoint[0] = moved[8:16].astype(BF16)
    for place in range(per):
        at = lanes(place)
        for k, (out, group) in enumerate(((grad_up, 2), (grad_down, 7))):
            xs = [early[source][group, :, at] for source in range(count)]
            es = [late[source][k, :, at] for source in range(count)]
            out[0, place] = ((grads[k, place] + outer(xs, es)) * scale).astype(BF16)


def call(body, operands, spaces, outs, scratch, after=(), cost=LIGHT):
    taken = len(operands)

    def kernel(*refs):
        body(*refs[:taken], *refs[taken + len(after):])

    return pl.pallas_call(
        kernel,
        out_shape=outs,
        in_specs=[pl.BlockSpec(memory_space=space) for space in spaces] + [pl.BlockSpec(memory_space=pl.ANY)] * len(after),
        out_specs=[pl.BlockSpec(memory_space=pltpu.VMEM)] * len(outs),
        scratch_shapes=scratch,
        compiler_params=pltpu.CompilerParams(vmem_limit_bytes=LIMIT),
        cost_estimate=pl.CostEstimate(flops=cost, bytes_accessed=cost // 100, transcendentals=0),
    )(*operands, *after)


def on_device(w_up, up_index, w_down, down_index, tick_order, values_in, score_grad_in, tangent_in, state_adjoint_in,
              saved_back, saved_tan, saved_second, saved_second_tan, saved_second_grad):
    count = lax.axis_size("dp")
    blocks = w_up.shape[1]
    per = blocks // count
    width = values_in.shape[2]
    part = per * BLOCK
    scale = 1.0 / (values_in.shape[1] * count)
    shape = jax.ShapeDtypeStruct
    pair = shape((16, width), BF16)
    vmem, smem = pltpu.VMEM, pltpu.SMEM

    def body(f, *args):
        def kernel(*refs):
            f(*args, *refs)
        return kernel

    def to_replicas(parts):
        return [parts[0]] + [lax.ppermute(parts[step], "dp", swap_route(step, count)) for step in range(1, count)]

    rows = (score_grad_in, state_adjoint_in, saved_back, saved_second, saved_second_tan, saved_second_grad)
    ten = shape((10, 16, part), BF16)
    (token,) = call(open_launch, (), [], [shape((8, BLOCK), F32)], [], cost=WORK)
    near, far, keep, keep_tan, *early = call(
        body(first_tick, count, per),
        (up_index, down_index, tick_order, w_up, w_down) + rows + (values_in, tangent_in, saved_tan),
        [smem] * 3 + [vmem] * 11,
        [pair, pair, shape((blocks, 24, BLOCK), F32), shape((blocks, 8, BLOCK), F32)] + [ten] * count,
        [vmem((2, 16, width), BF16), vmem((blocks, 32, BLOCK), F32), vmem((blocks, 16, BLOCK), F32),
         vmem((blocks, 48, BLOCK), BF16), vmem((blocks, 16, BLOCK), BF16)],
        after=(token,), cost=WORK)
    near, far = swap_sections(near, far)
    early = to_replicas(early)
    near, far, *late = call(
        body(second_tick, count, per), (up_index, down_index, w_up, w_down, near, far, keep, keep_tan),
        [smem] * 2 + [vmem] * 6,
        [pair, pair] + [shape((2, 16, part), BF16)] * count,
        [vmem((2, 16, width), BF16), vmem((2, 16, width), BF16), vmem((blocks, 16, BLOCK), F32),
         vmem((blocks, 16, BLOCK), F32), vmem((blocks, 16, BLOCK), BF16)])
    near, far = swap_sections(near, far)
    two = shape((2, 16, part), BF16)
    grads, *late = call(
        body(early_grads, count, per), (*early, *late), [vmem] * (2 * count),
        [shape((2, per, BLOCK, BLOCK), F32)] + [two] * count, [])
    late = to_replicas(late)
    stream = shape((1,) + values_in.shape[1:], BF16)
    grad = shape((1, per, BLOCK, BLOCK), BF16)
    return tuple(call(
        body(finish, count, per, scale), (near, far, grads, *early, *late), [vmem] * (3 + 2 * count),
        [stream, stream, stream, stream, grad, grad], [vmem((2, 16, width), BF16)]))


def solution(mesh):
    layer = P("section", None, None, None)
    table = P("section", None)
    stream = P("section", "dp", None)
    saved = P("section", None, "dp", None)
    return jax.shard_map(
        on_device,
        mesh=mesh,
        in_specs=(layer, table, layer, table, table) + (stream,) * 4 + (saved,) * 5,
        out_specs=(stream,) * 4 + (P("section", "dp", None, None),) * 2,
        check_vma=False,
    )
```

```python
import jax
import jax.numpy as jnp
from jax import lax
from jax.experimental import pallas as pl
from jax.experimental.pallas import tpu as pltpu
from jax.sharding import PartitionSpec as P

BLOCK = 128
F32 = jnp.float32
BF16 = jnp.bfloat16
LIMIT = 40 * 1024 * 1024
WORK = 10 ** 10
LIGHT = 10 ** 9


def partner(me, step, count):
    if count & (count - 1) == 0:
        return me ^ step
    return lax.rem(me + step, count)


def swap_route(step, count):
    if count & (count - 1) == 0:
        return [(i, i ^ step) for i in range(count)]
    return [(i, (i + step) % count) for i in range(count)]


def swap_sections(near, far):
    count = lax.axis_size("section")
    far = lax.ppermute(far, "section", [(i, (i + 2 * (i % 2) - 1) % count) for i in range(count)])
    near = lax.ppermute(near, "section", [(i, i ^ 1) for i in range(count)])
    return near, far


def times(rows, weight):
    return lax.dot_general(rows, weight, (((1,), (0,)), ((), ())), preferred_element_type=F32)


def times_transposed(rows, weight):
    return lax.dot_general(rows, weight, (((1,), (1,)), ((), ())), preferred_element_type=F32)


def outer(xs, es):
    return lax.dot_general(jnp.concatenate(xs, 0), jnp.concatenate(es, 0), (((0,), (0,)), ((), ())),
                           preferred_element_type=F32)


def sigmoid(z):
    return 1.0 / (1.0 + jnp.exp(-z))


def slope_of(z, s):
    return s * (1.0 + z * (1.0 - s))


def lanes(block):
    if isinstance(block, int):
        return pl.ds(block * BLOCK, BLOCK)
    return pl.ds(pl.multiple_of(block * BLOCK, BLOCK), BLOCK)


def stack(parts):
    return jnp.concatenate([part.astype(F32) for part in parts], 0)


def send_order(me, count, per):
    for step in range(count):
        base = partner(me, step, count) * per
        for place in range(per):
            yield step, place, base + place


def odd_section():
    return lax.rem(lax.axis_index("section"), 2)


def hand_out(packs, near, far):
    odd = odd_section()
    near[...] = packs[odd]
    far[...] = packs[1 - odd]


def take_in(near, far, packs):
    odd = odd_section()
    packs[1 - odd] = near[...]
    packs[odd] = far[...]


def open_launch(token):
    token[...] = jnp.zeros(token.shape, F32)


def back_first(count, per, up_idx, down_idx, order, w_up, w_down, g_ref, a_ref, back, second, second_tan,
               second_grad, pack, keep, sends, pulled, returned, hidden):
    blocks = count * per
    me = lax.axis_index("dp")
    for b in range(blocks):
        pulled[b] = jnp.zeros(pulled.shape[1:], F32)
    m0 = order[0, 0]
    m1 = order[0, 1]
    for b in range(blocks):
        returned[b] = stack([g_ref[0, :, lanes(b)], a_ref[0, :, lanes(b)]])
    for step, place, i in send_order(me, count, per):
        at = lanes(i)
        c = stack([g_ref[0, :, at], a_ref[0, :, at], second_grad[0, m0, :, at], second_grad[0, m1, :, at]]).astype(BF16)
        sends[step][8, :, lanes(place)] = c[0:16]
        sends[step][9, :, lanes(place)] = c[16:32]
        target = down_idx[0, i]
        pulled[target] = pulled[target] + times_transposed(c, w_down[0, i])
    for step, place, j in send_order(me, count, per):
        u = up_idx[0, j]
        at = lanes(u)
        x = stack([back[0, m0, :, at], second[0, m0, :, at], second_tan[0, m0, :, at],
                   second_tan[0, m1, :, at], back[0, m1, :, at], second[0, m1, :, at]]).astype(BF16)
        out = sends[step]
        here = lanes(place)
        for group in range(3):
            out[group, :, here] = x[16 * group:16 * group + 16]
        z = times(x, w_up[0, j])
        zb0, za0, ta0, ta1, zb1, za1 = (z[8 * k:8 * k + 8] for k in range(6))
        pg, pa, ga0, ga1 = (pulled[j, 8 * k:8 * k + 8] for k in range(4))
        sb0, sa0, sb1, sa1 = sigmoid(zb0), sigmoid(za0), sigmoid(zb1), sigmoid(za1)
        slope_a0 = slope_of(za0, sa0)
        slope_a1 = slope_of(za1, sa1)
        curve_a0 = sa0 * (1.0 - sa0) * (2.0 + za0 * (1.0 - 2.0 * sa0))
        curve_a1 = sa1 * (1.0 - sa1) * (2.0 + za1 * (1.0 - 2.0 * sa1))
        push = slope_a0 * pa + curve_a0 * ga0 * ta0
        e = jnp.concatenate([slope_of(zb0, sb0) * pg, push], 0).astype(BF16)
        out[3, :, here] = e
        out[4, :, here] = jnp.concatenate([slope_a0 * ga0, slope_a1 * ga1], 0).astype(BF16)
        hidden[j] = jnp.concatenate(
            [zb0 * sb0, za0 * sa0, slope_a0 * ta0, slope_a1 * ta1, zb1 * sb1, za1 * sa1], 0).astype(BF16)
        keep[j] = jnp.concatenate([slope_of(zb1, sb1), slope_a1, curve_a1 * ga1 * ta1], 0)
        returned[u] = returned[u] + times_transposed(e, w_up[0, j])
    for b in range(blocks):
        pack[:, lanes(b)] = returned[b].astype(BF16)
    for step, place, i in send_order(me, count, per):
        y = hidden[down_idx[0, i]]
        for group in range(3):
            sends[step][5 + group, :, lanes(place)] = y[16 * group:16 * group + 16]


def forward_first(blocks, up_idx, down_idx, order, w_up, w_down, v_ref, t_ref, tan, pack, keep, hidden):
    m0 = order[0, 0]
    m1 = order[0, 1]
    for j in range(blocks):
        at = lanes(up_idx[0, j])
        x = stack([v_ref[0, :, at], t_ref[0, :, at], tan[0, m0, :, at], tan[0, m1, :, at]]).astype(BF16)
        z = times(x, w_up[0, j])
        zv, zt, z0, z1 = (z[8 * k:8 * k + 8] for k in range(4))
        hidden[j] = jnp.concatenate([zv * sigmoid(zv), slope_of(z0, sigmoid(z0)) * zt], 0).astype(BF16)
        keep[j] = slope_of(z1, sigmoid(z1))
    for i in range(blocks):
        at = lanes(i)
        moved = stack([v_ref[0, :, at], t_ref[0, :, at]]) + times(hidden[down_idx[0, i]], w_down[0, i])
        pack[:, at] = moved.astype(BF16)


def first_tick(count, per, up_idx, down_idx, order, w_up, w_down, g_ref, a_ref, back, second, second_tan, second_grad,
               v_ref, t_ref, tan, near, far, keep, keep_tan, *refs):
    sends, (packs, pulled, returned, hidden, hidden_fwd) = refs[:count], refs[count:]
    back_first(count, per, up_idx, down_idx, order, w_up, w_down, g_ref, a_ref, back, second, second_tan,
               second_grad, packs.at[1], keep, sends, pulled, returned, hidden)
    forward_first(count * per, up_idx, down_idx, order, w_up, w_down, v_ref, t_ref, tan, packs.at[0], keep_tan, hidden_fwd)
    hand_out(packs, near, far)


def back_second(count, per, up_idx, down_idx, w_up, w_down, rows, keep, pack, sends, pulled, returned):
    blocks = count * per
    me = lax.axis_index("dp")
    for b in range(blocks):
        pulled[b] = jnp.zeros(pulled.shape[1:], F32)
        returned[b] = rows[:, lanes(b)].astype(F32)
    for step, place, i in send_order(me, count, per):
        c = rows[:, lanes(i)]
        sends[step][1, :, lanes(place)] = c
        target = down_idx[0, i]
        pulled[target] = pulled[target] + times_transposed(c, w_down[0, i])
    for step, place, j in send_order(me, count, per):
        u = up_idx[0, j]
        slope_b, slope_a, push = (keep[j, 8 * k:8 * k + 8] for k in range(3))
        e = jnp.concatenate([slope_b * pulled[j, 0:8], slope_a * pulled[j, 8:16] + push], 0).astype(BF16)
        sends[step][0, :, lanes(place)] = e
        returned[u] = returned[u] + times_transposed(e, w_up[0, j])
    for b in range(blocks):
        pack[:, lanes(b)] = returned[b].astype(BF16)


def forward_second(blocks, up_idx, down_idx, w_up, w_down, rows, keep, pack, hidden):
    for j in range(blocks):
        z = times(rows[:, lanes(up_idx[0, j])], w_up[0, j])
        zv, zt = z[0:8], z[8:16]
        hidden[j] = jnp.concatenate([zv * sigmoid(zv), keep[j] * zt], 0).astype(BF16)
    for i in range(blocks):
        at = lanes(i)
        pack[:, at] = (rows[:, at].astype(F32) + times(hidden[down_idx[0, i]], w_down[0, i])).astype(BF16)


def second_tick(count, per, up_idx, down_idx, w_up, w_down, near_in, far_in, keep, keep_tan, near, far, *refs):
    sends, (came, packs, pulled, returned, hidden) = refs[:count], refs[count:]
    take_in(near_in, far_in, came)
    back_second(count, per, up_idx, down_idx, w_up, w_down, came.at[1], keep, packs.at[1], sends, pulled, returned)
    forward_second(count * per, up_idx, down_idx, w_up, w_down, came.at[0], keep_tan, packs.at[0], hidden)
    hand_out(packs, near, far)


def early_grads(count, per, *refs):
    early, grads = refs[:count], refs[count]
    for place in range(per):
        at = lanes(place)
        for out, left, right in ((0, 0, 3), (1, 5, 8)):
            xs = [early[source][left + k, :, at] for source in range(count) for k in range(2)]
            es = [early[source][right + k, :, at] for source in range(count) for k in range(2)]
            grads[out, place] = outer(xs, es)


def finish(count, per, scale, near, far, grads, *rest):
    early, late = rest[:count], rest[count:2 * count]
    values, score, tangent, adjoint, grad_up, grad_down, came = rest[2 * count:]
    take_in(near, far, came)
    moved = came[0].astype(F32)
    values[0] = moved[0:8].astype(BF16)
    tangent[0] = moved[8:16].astype(BF16)
    moved = came[1].astype(F32)
    score[0] = moved[0:8].astype(BF16)
    adjoint[0] = moved[8:16].astype(BF16)
    for place in range(per):
        at = lanes(place)
        for k, (out, group) in enumerate(((grad_up, 2), (grad_down, 7))):
            xs = [early[source][group, :, at] for source in range(count)]
            es = [late[source][k, :, at] for source in range(count)]
            out[0, place] = ((grads[k, place] + outer(xs, es)) * scale).astype(BF16)


def call(body, operands, spaces, outs, scratch, after=(), cost=LIGHT):
    taken = len(operands)

    def kernel(*refs):
        body(*refs[:taken], *refs[taken + len(after):])

    return pl.pallas_call(
        kernel,
        out_shape=outs,
        in_specs=[pl.BlockSpec(memory_space=space) for space in spaces] + [pl.BlockSpec(memory_space=pl.ANY)] * len(after),
        out_specs=[pl.BlockSpec(memory_space=pltpu.VMEM)] * len(outs),
        scratch_shapes=scratch,
        compiler_params=pltpu.CompilerParams(vmem_limit_bytes=LIMIT),
        cost_estimate=pl.CostEstimate(flops=cost, bytes_accessed=cost // 100, transcendentals=0),
    )(*operands, *after)


def hold(arrays, until):
    def kernel(*refs):
        del refs

    return pl.pallas_call(
        kernel,
        out_shape=[jax.ShapeDtypeStruct(x.shape, x.dtype) for x in arrays],
        in_specs=[pl.BlockSpec(memory_space=pl.ANY)] * (len(arrays) + 1),
        out_specs=[pl.BlockSpec(memory_space=pl.ANY)] * len(arrays),
        input_output_aliases={k: k for k in range(len(arrays))},
        cost_estimate=pl.CostEstimate(flops=LIGHT, bytes_accessed=LIGHT // 100, transcendentals=0),
    )(*arrays, until)


def on_device(w_up, up_index, w_down, down_index, tick_order, values_in, score_grad_in, tangent_in, state_adjoint_in,
              saved_back, saved_tan, saved_second, saved_second_tan, saved_second_grad):
    count = lax.axis_size("dp")
    blocks = w_up.shape[1]
    per = blocks // count
    width = values_in.shape[2]
    part = per * BLOCK
    scale = 1.0 / (values_in.shape[1] * count)
    shape = jax.ShapeDtypeStruct
    pair = shape((16, width), BF16)
    vmem, smem = pltpu.VMEM, pltpu.SMEM

    def body(f, *args):
        def kernel(*refs):
            f(*args, *refs)
        return kernel

    def to_replicas(parts):
        return [parts[0]] + [lax.ppermute(parts[step], "dp", swap_route(step, count)) for step in range(1, count)]

    rows = (score_grad_in, state_adjoint_in, saved_back, saved_second, saved_second_tan, saved_second_grad)
    ten = shape((10, 16, part), BF16)
    (token,) = call(open_launch, (), [], [shape((8, BLOCK), F32)], [], cost=WORK)
    near, far, keep, keep_tan, *early = call(
        body(first_tick, count, per),
        (up_index, down_index, tick_order, w_up, w_down) + rows + (values_in, tangent_in, saved_tan),
        [smem] * 3 + [vmem] * 11,
        [pair, pair, shape((blocks, 24, BLOCK), F32), shape((blocks, 8, BLOCK), F32)] + [ten] * count,
        [vmem((2, 16, width), BF16), vmem((blocks, 32, BLOCK), F32), vmem((blocks, 16, BLOCK), F32),
         vmem((blocks, 48, BLOCK), BF16), vmem((blocks, 16, BLOCK), BF16)],
        after=(token,), cost=WORK)
    near, far = swap_sections(near, far)
    early = to_replicas(early)
    near, far, *late = call(
        body(second_tick, count, per), (up_index, down_index, w_up, w_down, near, far, keep, keep_tan),
        [smem] * 2 + [vmem] * 6,
        [pair, pair] + [shape((2, 16, part), BF16)] * count,
        [vmem((2, 16, width), BF16), vmem((2, 16, width), BF16), vmem((blocks, 16, BLOCK), F32),
         vmem((blocks, 16, BLOCK), F32), vmem((blocks, 16, BLOCK), BF16)])
    near, far = swap_sections(near, far)
    late = hold(late, near)
    late = to_replicas(late)
    (grads,) = call(
        body(early_grads, count, per), tuple(early), [vmem] * count, [shape((2, per, BLOCK, BLOCK), F32)], [])
    stream = shape((1,) + values_in.shape[1:], BF16)
    grad = shape((1, per, BLOCK, BLOCK), BF16)
    return tuple(call(
        body(finish, count, per, scale), (near, far, grads, *early, *late), [vmem] * (3 + 2 * count),
        [stream, stream, stream, stream, grad, grad], [vmem((2, 16, width), BF16)]))


def solution(mesh):
    layer = P("section", None, None, None)
    table = P("section", None)
    stream = P("section", "dp", None)
    saved = P("section", None, "dp", None)
    return jax.shard_map(
        on_device,
        mesh=mesh,
        in_specs=(layer, table, layer, table, table) + (stream,) * 4 + (saved,) * 5,
        out_specs=(stream,) * 4 + (P("section", "dp", None, None),) * 2,
        check_vma=False,
    )
```

```python
import jax
import jax.numpy as jnp
from jax import lax
from jax.experimental import pallas as pl
from jax.experimental.pallas import tpu as pltpu
from jax.sharding import PartitionSpec as P

BLOCK = 128
F32 = jnp.float32
BF16 = jnp.bfloat16
LIMIT = 40 * 1024 * 1024
WORK = 10 ** 10
LIGHT = 10 ** 9


def partner(me, step, count):
    if count & (count - 1) == 0:
        return me ^ step
    return lax.rem(me + step, count)


def swap_route(step, count):
    if count & (count - 1) == 0:
        return [(i, i ^ step) for i in range(count)]
    return [(i, (i + step) % count) for i in range(count)]


def swap_sections(near, far):
    count = lax.axis_size("section")
    far = lax.ppermute(far, "section", [(i, (i + 2 * (i % 2) - 1) % count) for i in range(count)])
    near = lax.ppermute(near, "section", [(i, i ^ 1) for i in range(count)])
    return near, far


def times(rows, weight):
    return lax.dot_general(rows, weight, (((1,), (0,)), ((), ())), preferred_element_type=F32)


def times_transposed(rows, weight):
    return lax.dot_general(rows, weight, (((1,), (1,)), ((), ())), preferred_element_type=F32)


def outer(xs, es):
    return lax.dot_general(jnp.concatenate(xs, 0), jnp.concatenate(es, 0), (((0,), (0,)), ((), ())),
                           preferred_element_type=F32)


def sigmoid(z):
    return 1.0 / (1.0 + jnp.exp(-z))


def slope_of(z, s):
    return s * (1.0 + z * (1.0 - s))


def lanes(block):
    if isinstance(block, int):
        return pl.ds(block * BLOCK, BLOCK)
    return pl.ds(pl.multiple_of(block * BLOCK, BLOCK), BLOCK)


def stack(parts):
    return jnp.concatenate([part.astype(F32) for part in parts], 0)


def send_order(me, count, per):
    for step in range(count):
        base = partner(me, step, count) * per
        for place in range(per):
            yield step, place, base + place


def odd_section():
    return lax.rem(lax.axis_index("section"), 2)


def hand_out(packs, near, far):
    odd = odd_section()
    near[...] = packs[odd]
    far[...] = packs[1 - odd]


def take_in(near, far, packs):
    odd = odd_section()
    packs[1 - odd] = near[...]
    packs[odd] = far[...]


def open_launch(token):
    token[...] = jnp.zeros(token.shape, F32)


def back_first(count, per, up_idx, down_idx, order, w_up, w_down, g_ref, a_ref, back, second, second_tan,
               second_grad, pack, keep, sends, pulled, returned, hidden):
    blocks = count * per
    me = lax.axis_index("dp")
    for b in range(blocks):
        pulled[b] = jnp.zeros(pulled.shape[1:], F32)
    m0 = order[0, 0]
    m1 = order[0, 1]
    for b in range(blocks):
        returned[b] = stack([g_ref[0, :, lanes(b)], a_ref[0, :, lanes(b)]])
    for step, place, i in send_order(me, count, per):
        at = lanes(i)
        c = stack([g_ref[0, :, at], a_ref[0, :, at], second_grad[0, m0, :, at], second_grad[0, m1, :, at]]).astype(BF16)
        sends[step][8, :, lanes(place)] = c[0:16]
        sends[step][9, :, lanes(place)] = c[16:32]
        target = down_idx[0, i]
        pulled[target] = pulled[target] + times_transposed(c, w_down[0, i])
    for step, place, j in send_order(me, count, per):
        u = up_idx[0, j]
        at = lanes(u)
        x = stack([back[0, m0, :, at], second[0, m0, :, at], second_tan[0, m0, :, at],
                   second_tan[0, m1, :, at], back[0, m1, :, at], second[0, m1, :, at]]).astype(BF16)
        out = sends[step]
        here = lanes(place)
        for group in range(3):
            out[group, :, here] = x[16 * group:16 * group + 16]
        z = times(x, w_up[0, j])
        zb0, za0, ta0, ta1, zb1, za1 = (z[8 * k:8 * k + 8] for k in range(6))
        pg, pa, ga0, ga1 = (pulled[j, 8 * k:8 * k + 8] for k in range(4))
        sb0, sa0, sb1, sa1 = sigmoid(zb0), sigmoid(za0), sigmoid(zb1), sigmoid(za1)
        slope_a0 = slope_of(za0, sa0)
        slope_a1 = slope_of(za1, sa1)
        curve_a0 = sa0 * (1.0 - sa0) * (2.0 + za0 * (1.0 - 2.0 * sa0))
        curve_a1 = sa1 * (1.0 - sa1) * (2.0 + za1 * (1.0 - 2.0 * sa1))
        push = slope_a0 * pa + curve_a0 * ga0 * ta0
        e = jnp.concatenate([slope_of(zb0, sb0) * pg, push], 0).astype(BF16)
        out[3, :, here] = e
        out[4, :, here] = jnp.concatenate([slope_a0 * ga0, slope_a1 * ga1], 0).astype(BF16)
        hidden[j] = jnp.concatenate(
            [zb0 * sb0, za0 * sa0, slope_a0 * ta0, slope_a1 * ta1, zb1 * sb1, za1 * sa1], 0).astype(BF16)
        keep[j] = jnp.concatenate([slope_of(zb1, sb1), slope_a1, curve_a1 * ga1 * ta1], 0)
        returned[u] = returned[u] + times_transposed(e, w_up[0, j])
    for b in range(blocks):
        pack[:, lanes(b)] = returned[b].astype(BF16)
    for step, place, i in send_order(me, count, per):
        y = hidden[down_idx[0, i]]
        for group in range(3):
            sends[step][5 + group, :, lanes(place)] = y[16 * group:16 * group + 16]


def forward_first(blocks, up_idx, down_idx, order, w_up, w_down, v_ref, t_ref, tan, pack, keep, hidden):
    m0 = order[0, 0]
    m1 = order[0, 1]
    for j in range(blocks):
        at = lanes(up_idx[0, j])
        x = stack([v_ref[0, :, at], t_ref[0, :, at], tan[0, m0, :, at], tan[0, m1, :, at]]).astype(BF16)
        z = times(x, w_up[0, j])
        zv, zt, z0, z1 = (z[8 * k:8 * k + 8] for k in range(4))
        hidden[j] = jnp.concatenate([zv * sigmoid(zv), slope_of(z0, sigmoid(z0)) * zt], 0).astype(BF16)
        keep[j] = slope_of(z1, sigmoid(z1))
    for i in range(blocks):
        at = lanes(i)
        moved = stack([v_ref[0, :, at], t_ref[0, :, at]]) + times(hidden[down_idx[0, i]], w_down[0, i])
        pack[:, at] = moved.astype(BF16)


def first_tick(count, per, up_idx, down_idx, order, w_up, w_down, g_ref, a_ref, back, second, second_tan, second_grad,
               v_ref, t_ref, tan, near, far, keep, keep_tan, *refs):
    sends, (packs, pulled, returned, hidden, hidden_fwd) = refs[:count], refs[count:]
    back_first(count, per, up_idx, down_idx, order, w_up, w_down, g_ref, a_ref, back, second, second_tan,
               second_grad, packs.at[1], keep, sends, pulled, returned, hidden)
    forward_first(count * per, up_idx, down_idx, order, w_up, w_down, v_ref, t_ref, tan, packs.at[0], keep_tan, hidden_fwd)
    hand_out(packs, near, far)


def back_second(count, per, up_idx, down_idx, w_up, w_down, rows, keep, pack, sends, pulled, returned):
    blocks = count * per
    me = lax.axis_index("dp")
    for b in range(blocks):
        pulled[b] = jnp.zeros(pulled.shape[1:], F32)
        returned[b] = rows[:, lanes(b)].astype(F32)
    for step, place, i in send_order(me, count, per):
        c = rows[:, lanes(i)]
        sends[step][1, :, lanes(place)] = c
        target = down_idx[0, i]
        pulled[target] = pulled[target] + times_transposed(c, w_down[0, i])
    for step, place, j in send_order(me, count, per):
        u = up_idx[0, j]
        slope_b, slope_a, push = (keep[j, 8 * k:8 * k + 8] for k in range(3))
        e = jnp.concatenate([slope_b * pulled[j, 0:8], slope_a * pulled[j, 8:16] + push], 0).astype(BF16)
        sends[step][0, :, lanes(place)] = e
        returned[u] = returned[u] + times_transposed(e, w_up[0, j])
    for b in range(blocks):
        pack[:, lanes(b)] = returned[b].astype(BF16)


def forward_second(blocks, up_idx, down_idx, w_up, w_down, rows, keep, pack, hidden):
    for j in range(blocks):
        z = times(rows[:, lanes(up_idx[0, j])], w_up[0, j])
        zv, zt = z[0:8], z[8:16]
        hidden[j] = jnp.concatenate([zv * sigmoid(zv), keep[j] * zt], 0).astype(BF16)
    for i in range(blocks):
        at = lanes(i)
        pack[:, at] = (rows[:, at].astype(F32) + times(hidden[down_idx[0, i]], w_down[0, i])).astype(BF16)


def second_tick(count, per, up_idx, down_idx, w_up, w_down, near_in, far_in, keep, keep_tan, near, far, *refs):
    sends, (came, packs, pulled, returned, hidden) = refs[:count], refs[count:]
    take_in(near_in, far_in, came)
    back_second(count, per, up_idx, down_idx, w_up, w_down, came.at[1], keep, packs.at[1], sends, pulled, returned)
    forward_second(count * per, up_idx, down_idx, w_up, w_down, came.at[0], keep_tan, packs.at[0], hidden)
    hand_out(packs, near, far)


def early_grads(count, per, *refs):
    early, grads = refs[:count], refs[count]
    for place in range(per):
        at = lanes(place)
        for out, left, right in ((0, 0, 3), (1, 5, 8)):
            xs = [early[source][left + k, :, at] for source in range(count) for k in range(2)]
            es = [early[source][right + k, :, at] for source in range(count) for k in range(2)]
            grads[out, place] = outer(xs, es)


def finish(count, per, scale, near, far, grads, *rest):
    early, late = rest[:count], rest[count:2 * count]
    values, score, tangent, adjoint, grad_up, grad_down, came = rest[2 * count:]
    take_in(near, far, came)
    moved = came[0].astype(F32)
    values[0] = moved[0:8].astype(BF16)
    tangent[0] = moved[8:16].astype(BF16)
    moved = came[1].astype(F32)
    score[0] = moved[0:8].astype(BF16)
    adjoint[0] = moved[8:16].astype(BF16)
    for place in range(per):
        at = lanes(place)
        for k, (out, group) in enumerate(((grad_up, 2), (grad_down, 7))):
            xs = [early[source][group, :, at] for source in range(count)]
            es = [late[source][k, :, at] for source in range(count)]
            out[0, place] = ((grads[k, place] + outer(xs, es)) * scale).astype(BF16)


def call(body, operands, spaces, outs, scratch, after=(), cost=LIGHT):
    taken = len(operands)

    def kernel(*refs):
        body(*refs[:taken], *refs[taken + len(after):])

    return pl.pallas_call(
        kernel,
        out_shape=outs,
        in_specs=[pl.BlockSpec(memory_space=space) for space in spaces] + [pl.BlockSpec(memory_space=pl.ANY)] * len(after),
        out_specs=[pl.BlockSpec(memory_space=pltpu.VMEM)] * len(outs),
        scratch_shapes=scratch,
        compiler_params=pltpu.CompilerParams(vmem_limit_bytes=LIMIT),
        cost_estimate=pl.CostEstimate(flops=cost, bytes_accessed=cost // 100, transcendentals=0),
    )(*operands, *after)


def hand_on(*refs):
    half = len(refs) // 2
    for source, target in zip(refs[:half], refs[half:]):
        target[...] = source[...]


def on_device(w_up, up_index, w_down, down_index, tick_order, values_in, score_grad_in, tangent_in, state_adjoint_in,
              saved_back, saved_tan, saved_second, saved_second_tan, saved_second_grad):
    count = lax.axis_size("dp")
    blocks = w_up.shape[1]
    per = blocks // count
    width = values_in.shape[2]
    part = per * BLOCK
    scale = 1.0 / (values_in.shape[1] * count)
    shape = jax.ShapeDtypeStruct
    pair = shape((16, width), BF16)
    vmem, smem = pltpu.VMEM, pltpu.SMEM

    def body(f, *args):
        def kernel(*refs):
            f(*args, *refs)
        return kernel

    def to_replicas(parts):
        return [parts[0]] + [lax.ppermute(parts[step], "dp", swap_route(step, count)) for step in range(1, count)]

    rows = (score_grad_in, state_adjoint_in, saved_back, saved_second, saved_second_tan, saved_second_grad)
    ten = shape((10, 16, part), BF16)
    (token,) = call(open_launch, (), [], [shape((8, BLOCK), F32)], [], cost=WORK)
    near, far, keep, keep_tan, *early = call(
        body(first_tick, count, per),
        (up_index, down_index, tick_order, w_up, w_down) + rows + (values_in, tangent_in, saved_tan),
        [smem] * 3 + [vmem] * 11,
        [pair, pair, shape((blocks, 24, BLOCK), F32), shape((blocks, 8, BLOCK), F32)] + [ten] * count,
        [vmem((2, 16, width), BF16), vmem((blocks, 32, BLOCK), F32), vmem((blocks, 16, BLOCK), F32),
         vmem((blocks, 48, BLOCK), BF16), vmem((blocks, 16, BLOCK), BF16)],
        after=(token,), cost=WORK)
    near, far = swap_sections(near, far)
    early = to_replicas(early)
    near, far, *late = call(
        body(second_tick, count, per), (up_index, down_index, w_up, w_down, near, far, keep, keep_tan),
        [smem] * 2 + [vmem] * 6,
        [pair, pair] + [shape((2, 16, part), BF16)] * count,
        [vmem((2, 16, width), BF16), vmem((2, 16, width), BF16), vmem((blocks, 16, BLOCK), F32),
         vmem((blocks, 16, BLOCK), F32), vmem((blocks, 16, BLOCK), BF16)])
    near, far = swap_sections(near, far)
    two = shape((2, 16, part), BF16)
    held = call(hand_on, tuple(late[1:]), [vmem] * (count - 1), [two] * (count - 1), [], after=(near,))
    late = to_replicas(late[:1] + list(held))
    (grads,) = call(
        body(early_grads, count, per), tuple(early), [vmem] * count, [shape((2, per, BLOCK, BLOCK), F32)], [])
    stream = shape((1,) + values_in.shape[1:], BF16)
    grad = shape((1, per, BLOCK, BLOCK), BF16)
    return tuple(call(
        body(finish, count, per, scale), (near, far, grads, *early, *late), [vmem] * (3 + 2 * count),
        [stream, stream, stream, stream, grad, grad], [vmem((2, 16, width), BF16)]))


def solution(mesh):
    layer = P("section", None, None, None)
    table = P("section", None)
    stream = P("section", "dp", None)
    saved = P("section", None, "dp", None)
    return jax.shard_map(
        on_device,
        mesh=mesh,
        in_specs=(layer, table, layer, table, table) + (stream,) * 4 + (saved,) * 5,
        out_specs=(stream,) * 4 + (P("section", "dp", None, None),) * 2,
        check_vma=False,
    )
```

```python
import jax
import jax.numpy as jnp
from jax import lax
from jax.experimental import pallas as pl
from jax.experimental.pallas import tpu as pltpu
from jax.sharding import PartitionSpec as P

BLOCK = 128
F32 = jnp.float32
BF16 = jnp.bfloat16
LIMIT = 40 * 1024 * 1024
WORK = 10 ** 10
LIGHT = 10 ** 4


def partner(me, step, count):
    if count & (count - 1) == 0:
        return me ^ step
    return lax.rem(me + step, count)


def swap_route(step, count):
    if count & (count - 1) == 0:
        return [(i, i ^ step) for i in range(count)]
    return [(i, (i + step) % count) for i in range(count)]


def swap_sections(near, far):
    count = lax.axis_size("section")
    far = lax.ppermute(far, "section", [(i, (i + 2 * (i % 2) - 1) % count) for i in range(count)])
    near = lax.ppermute(near, "section", [(i, i ^ 1) for i in range(count)])
    return near, far


def times(rows, weight):
    return lax.dot_general(rows, weight, (((1,), (0,)), ((), ())), preferred_element_type=F32)


def times_transposed(rows, weight):
    return lax.dot_general(rows, weight, (((1,), (1,)), ((), ())), preferred_element_type=F32)


def outer(xs, es):
    return lax.dot_general(jnp.concatenate(xs, 0), jnp.concatenate(es, 0), (((0,), (0,)), ((), ())),
                           preferred_element_type=F32)


def sigmoid(z):
    return 1.0 / (1.0 + jnp.exp(-z))


def slope_of(z, s):
    return s * (1.0 + z * (1.0 - s))


def lanes(block):
    if isinstance(block, int):
        return pl.ds(block * BLOCK, BLOCK)
    return pl.ds(pl.multiple_of(block * BLOCK, BLOCK), BLOCK)


def stack(parts):
    return jnp.concatenate([part.astype(F32) for part in parts], 0)


def send_order(me, count, per):
    for step in range(count):
        base = partner(me, step, count) * per
        for place in range(per):
            yield step, place, base + place


def odd_section():
    return lax.rem(lax.axis_index("section"), 2)


def hand_out(packs, near, far):
    odd = odd_section()
    near[...] = packs[odd]
    far[...] = packs[1 - odd]


def take_in(near, far, packs):
    odd = odd_section()
    packs[1 - odd] = near[...]
    packs[odd] = far[...]


def open_launch(token):
    token[...] = jnp.zeros(token.shape, F32)


def back_first(count, per, up_idx, down_idx, order, w_up, w_down, g_ref, a_ref, back, second, second_tan,
               second_grad, pack, keep, sends, pulled, returned, hidden):
    blocks = count * per
    me = lax.axis_index("dp")
    for b in range(blocks):
        pulled[b] = jnp.zeros(pulled.shape[1:], F32)
    m0 = order[0, 0]
    m1 = order[0, 1]
    for b in range(blocks):
        returned[b] = stack([g_ref[0, :, lanes(b)], a_ref[0, :, lanes(b)]])
    for step, place, i in send_order(me, count, per):
        at = lanes(i)
        c = stack([g_ref[0, :, at], a_ref[0, :, at], second_grad[0, m0, :, at], second_grad[0, m1, :, at]]).astype(BF16)
        sends[step][8, :, lanes(place)] = c[0:16]
        sends[step][9, :, lanes(place)] = c[16:32]
        target = down_idx[0, i]
        pulled[target] = pulled[target] + times_transposed(c, w_down[0, i])
    for step, place, j in send_order(me, count, per):
        u = up_idx[0, j]
        at = lanes(u)
        x = stack([back[0, m0, :, at], second[0, m0, :, at], second_tan[0, m0, :, at],
                   second_tan[0, m1, :, at], back[0, m1, :, at], second[0, m1, :, at]]).astype(BF16)
        out = sends[step]
        here = lanes(place)
        for group in range(3):
            out[group, :, here] = x[16 * group:16 * group + 16]
        z = times(x, w_up[0, j])
        zb0, za0, ta0, ta1, zb1, za1 = (z[8 * k:8 * k + 8] for k in range(6))
        pg, pa, ga0, ga1 = (pulled[j, 8 * k:8 * k + 8] for k in range(4))
        sb0, sa0, sb1, sa1 = sigmoid(zb0), sigmoid(za0), sigmoid(zb1), sigmoid(za1)
        slope_a0 = slope_of(za0, sa0)
        slope_a1 = slope_of(za1, sa1)
        curve_a0 = sa0 * (1.0 - sa0) * (2.0 + za0 * (1.0 - 2.0 * sa0))
        curve_a1 = sa1 * (1.0 - sa1) * (2.0 + za1 * (1.0 - 2.0 * sa1))
        push = slope_a0 * pa + curve_a0 * ga0 * ta0
        e = jnp.concatenate([slope_of(zb0, sb0) * pg, push], 0).astype(BF16)
        out[3, :, here] = e
        out[4, :, here] = jnp.concatenate([slope_a0 * ga0, slope_a1 * ga1], 0).astype(BF16)
        hidden[j] = jnp.concatenate(
            [zb0 * sb0, za0 * sa0, slope_a0 * ta0, slope_a1 * ta1, zb1 * sb1, za1 * sa1], 0).astype(BF16)
        keep[j] = jnp.concatenate([slope_of(zb1, sb1), slope_a1, curve_a1 * ga1 * ta1], 0)
        returned[u] = returned[u] + times_transposed(e, w_up[0, j])
    for b in range(blocks):
        pack[:, lanes(b)] = returned[b].astype(BF16)
    for step, place, i in send_order(me, count, per):
        y = hidden[down_idx[0, i]]
        for group in range(3):
            sends[step][5 + group, :, lanes(place)] = y[16 * group:16 * group + 16]


def forward_first(blocks, up_idx, down_idx, order, w_up, w_down, v_ref, t_ref, tan, pack, keep, hidden):
    m0 = order[0, 0]
    m1 = order[0, 1]
    for j in range(blocks):
        at = lanes(up_idx[0, j])
        x = stack([v_ref[0, :, at], t_ref[0, :, at], tan[0, m0, :, at], tan[0, m1, :, at]]).astype(BF16)
        z = times(x, w_up[0, j])
        zv, zt, z0, z1 = (z[8 * k:8 * k + 8] for k in range(4))
        hidden[j] = jnp.concatenate([zv * sigmoid(zv), slope_of(z0, sigmoid(z0)) * zt], 0).astype(BF16)
        keep[j] = slope_of(z1, sigmoid(z1))
    for i in range(blocks):
        at = lanes(i)
        moved = stack([v_ref[0, :, at], t_ref[0, :, at]]) + times(hidden[down_idx[0, i]], w_down[0, i])
        pack[:, at] = moved.astype(BF16)


def first_tick(count, per, up_idx, down_idx, order, w_up, w_down, g_ref, a_ref, back, second, second_tan, second_grad,
               v_ref, t_ref, tan, near, far, keep, keep_tan, *refs):
    sends, (packs, pulled, returned, hidden, hidden_fwd) = refs[:count], refs[count:]
    back_first(count, per, up_idx, down_idx, order, w_up, w_down, g_ref, a_ref, back, second, second_tan,
               second_grad, packs.at[1], keep, sends, pulled, returned, hidden)
    forward_first(count * per, up_idx, down_idx, order, w_up, w_down, v_ref, t_ref, tan, packs.at[0], keep_tan, hidden_fwd)
    hand_out(packs, near, far)


def back_second(count, per, up_idx, down_idx, w_up, w_down, rows, keep, pack, sends, pulled, returned):
    blocks = count * per
    me = lax.axis_index("dp")
    for b in range(blocks):
        pulled[b] = jnp.zeros(pulled.shape[1:], F32)
        returned[b] = rows[:, lanes(b)].astype(F32)
    for step, place, i in send_order(me, count, per):
        c = rows[:, lanes(i)]
        sends[step][1, :, lanes(place)] = c
        target = down_idx[0, i]
        pulled[target] = pulled[target] + times_transposed(c, w_down[0, i])
    for step, place, j in send_order(me, count, per):
        u = up_idx[0, j]
        slope_b, slope_a, push = (keep[j, 8 * k:8 * k + 8] for k in range(3))
        e = jnp.concatenate([slope_b * pulled[j, 0:8], slope_a * pulled[j, 8:16] + push], 0).astype(BF16)
        sends[step][0, :, lanes(place)] = e
        returned[u] = returned[u] + times_transposed(e, w_up[0, j])
    for b in range(blocks):
        pack[:, lanes(b)] = returned[b].astype(BF16)


def forward_second(blocks, up_idx, down_idx, w_up, w_down, rows, keep, pack, hidden):
    for j in range(blocks):
        z = times(rows[:, lanes(up_idx[0, j])], w_up[0, j])
        zv, zt = z[0:8], z[8:16]
        hidden[j] = jnp.concatenate([zv * sigmoid(zv), keep[j] * zt], 0).astype(BF16)
    for i in range(blocks):
        at = lanes(i)
        pack[:, at] = (rows[:, at].astype(F32) + times(hidden[down_idx[0, i]], w_down[0, i])).astype(BF16)


def second_tick(count, per, up_idx, down_idx, w_up, w_down, near_in, far_in, keep, keep_tan, near, far, *refs):
    sends, (came, packs, pulled, returned, hidden) = refs[:count], refs[count:]
    take_in(near_in, far_in, came)
    back_second(count, per, up_idx, down_idx, w_up, w_down, came.at[1], keep, packs.at[1], sends, pulled, returned)
    forward_second(count * per, up_idx, down_idx, w_up, w_down, came.at[0], keep_tan, packs.at[0], hidden)
    hand_out(packs, near, far)


def early_grads(count, per, *refs):
    early, grads = refs[:count], refs[count]
    for place in range(per):
        at = lanes(place)
        for out, left, right in ((0, 0, 3), (1, 5, 8)):
            xs = [early[source][left + k, :, at] for source in range(count) for k in range(2)]
            es = [early[source][right + k, :, at] for source in range(count) for k in range(2)]
            grads[out, place] = outer(xs, es)


def finish(count, per, scale, near, far, grads, *rest):
    early, late = rest[:count], rest[count:2 * count]
    values, score, tangent, adjoint, grad_up, grad_down, came = rest[2 * count:]
    take_in(near, far, came)
    moved = came[0].astype(F32)
    values[0] = moved[0:8].astype(BF16)
    tangent[0] = moved[8:16].astype(BF16)
    moved = came[1].astype(F32)
    score[0] = moved[0:8].astype(BF16)
    adjoint[0] = moved[8:16].astype(BF16)
    for place in range(per):
        at = lanes(place)
        for k, (out, group) in enumerate(((grad_up, 2), (grad_down, 7))):
            xs = [early[source][group, :, at] for source in range(count)]
            es = [late[source][k, :, at] for source in range(count)]
            out[0, place] = ((grads[k, place] + outer(xs, es)) * scale).astype(BF16)


def call(body, operands, spaces, outs, scratch, after=(), cost=LIGHT):
    taken = len(operands)

    def kernel(*refs):
        body(*refs[:taken], *refs[taken + len(after):])

    return pl.pallas_call(
        kernel,
        out_shape=outs,
        in_specs=[pl.BlockSpec(memory_space=space) for space in spaces] + [pl.BlockSpec(memory_space=pl.ANY)] * len(after),
        out_specs=[pl.BlockSpec(memory_space=pltpu.VMEM)] * len(outs),
        scratch_shapes=scratch,
        compiler_params=pltpu.CompilerParams(vmem_limit_bytes=LIMIT),
        cost_estimate=pl.CostEstimate(flops=cost, bytes_accessed=cost // 100, transcendentals=0),
    )(*operands, *after)


def hand_on(*refs):
    half = len(refs) // 2
    for source, target in zip(refs[:half], refs[half:]):
        target[...] = source[...]


def on_device(w_up, up_index, w_down, down_index, tick_order, values_in, score_grad_in, tangent_in, state_adjoint_in,
              saved_back, saved_tan, saved_second, saved_second_tan, saved_second_grad):
    count = lax.axis_size("dp")
    blocks = w_up.shape[1]
    per = blocks // count
    width = values_in.shape[2]
    part = per * BLOCK
    scale = 1.0 / (values_in.shape[1] * count)
    shape = jax.ShapeDtypeStruct
    pair = shape((16, width), BF16)
    vmem, smem = pltpu.VMEM, pltpu.SMEM

    def body(f, *args):
        def kernel(*refs):
            f(*args, *refs)
        return kernel

    def to_replicas(parts):
        steps = [count - 1] + list(range(1, count - 1))
        return [parts[0]] + [lax.ppermute(parts[step], "dp", swap_route(step, count)) for step in steps]

    rows = (score_grad_in, state_adjoint_in, saved_back, saved_second, saved_second_tan, saved_second_grad)
    ten = shape((10, 16, part), BF16)
    (token,) = call(open_launch, (), [], [shape((8, BLOCK), F32)], [], cost=WORK)
    near, far, keep, keep_tan, *early = call(
        body(first_tick, count, per),
        (up_index, down_index, tick_order, w_up, w_down) + rows + (values_in, tangent_in, saved_tan),
        [smem] * 3 + [vmem] * 11,
        [pair, pair, shape((blocks, 24, BLOCK), F32), shape((blocks, 8, BLOCK), F32)] + [ten] * count,
        [vmem((2, 16, width), BF16), vmem((blocks, 32, BLOCK), F32), vmem((blocks, 16, BLOCK), F32),
         vmem((blocks, 48, BLOCK), BF16), vmem((blocks, 16, BLOCK), BF16)],
        after=(token,), cost=WORK)
    near, far = swap_sections(near, far)
    early = to_replicas(early)
    near, far, *late = call(
        body(second_tick, count, per), (up_index, down_index, w_up, w_down, near, far, keep, keep_tan),
        [smem] * 2 + [vmem] * 6,
        [pair, pair] + [shape((2, 16, part), BF16)] * count,
        [vmem((2, 16, width), BF16), vmem((2, 16, width), BF16), vmem((blocks, 16, BLOCK), F32),
         vmem((blocks, 16, BLOCK), F32), vmem((blocks, 16, BLOCK), BF16)])
    near, far = swap_sections(near, far)
    two = shape((2, 16, part), BF16)
    held = call(hand_on, tuple(late[1:]), [vmem] * (count - 1), [two] * (count - 1), [], after=(near,))
    late = to_replicas(late[:1] + list(held))
    (grads,) = call(
        body(early_grads, count, per), tuple(early), [vmem] * count, [shape((2, per, BLOCK, BLOCK), F32)], [])
    stream = shape((1,) + values_in.shape[1:], BF16)
    grad = shape((1, per, BLOCK, BLOCK), BF16)
    return tuple(call(
        body(finish, count, per, scale), (near, far, grads, *early, *late), [vmem] * (3 + 2 * count),
        [stream, stream, stream, stream, grad, grad], [vmem((2, 16, width), BF16)]))


def solution(mesh):
    layer = P("section", None, None, None)
    table = P("section", None)
    stream = P("section", "dp", None)
    saved = P("section", None, "dp", None)
    return jax.shard_map(
        on_device,
        mesh=mesh,
        in_specs=(layer, table, layer, table, table) + (stream,) * 4 + (saved,) * 5,
        out_specs=(stream,) * 4 + (P("section", "dp", None, None),) * 2,
        check_vma=False,
    )
```

```python
import jax
import jax.numpy as jnp
from jax import lax
from jax.experimental import pallas as pl
from jax.experimental.pallas import tpu as pltpu
from jax.sharding import PartitionSpec as P

BLOCK = 128
F32 = jnp.float32
BF16 = jnp.bfloat16
LIMIT = 40 * 1024 * 1024
WORK = 10 ** 10
LIGHT = 10 ** 4
STREAMS = LIGHT


def partner(me, step, count):
    if count & (count - 1) == 0:
        return me ^ step
    return lax.rem(me + step, count)


def swap_route(step, count):
    if count & (count - 1) == 0:
        return [(i, i ^ step) for i in range(count)]
    return [(i, (i + step) % count) for i in range(count)]


def swap_sections(near, far):
    count = lax.axis_size("section")
    far = lax.ppermute(far, "section", [(i, (i + 2 * (i % 2) - 1) % count) for i in range(count)])
    near = lax.ppermute(near, "section", [(i, i ^ 1) for i in range(count)])
    return near, far


def times(rows, weight):
    return lax.dot_general(rows, weight, (((1,), (0,)), ((), ())), preferred_element_type=F32)


def times_transposed(rows, weight):
    return lax.dot_general(rows, weight, (((1,), (1,)), ((), ())), preferred_element_type=F32)


def outer(xs, es):
    return lax.dot_general(jnp.concatenate(xs, 0), jnp.concatenate(es, 0), (((0,), (0,)), ((), ())),
                           preferred_element_type=F32)


def sigmoid(z):
    return 1.0 / (1.0 + jnp.exp(-z))


def slope_of(z, s):
    return s * (1.0 + z * (1.0 - s))


def lanes(block):
    if isinstance(block, int):
        return pl.ds(block * BLOCK, BLOCK)
    return pl.ds(pl.multiple_of(block * BLOCK, BLOCK), BLOCK)


def stack(parts):
    return jnp.concatenate([part.astype(F32) for part in parts], 0)


def send_order(me, count, per):
    for step in range(count):
        base = partner(me, step, count) * per
        for place in range(per):
            yield step, place, base + place


def odd_section():
    return lax.rem(lax.axis_index("section"), 2)


def hand_out(packs, near, far):
    odd = odd_section()
    near[...] = packs[odd]
    far[...] = packs[1 - odd]


def take_in(near, far, packs):
    odd = odd_section()
    packs[1 - odd] = near[...]
    packs[odd] = far[...]


def open_launch(token):
    token[...] = jnp.zeros(token.shape, F32)


def first_rows(count, per, up_idx, down_idx, order, w_up, w_down, g_ref, a_ref, back, second, second_tan, second_grad,
               keep, pushes, *refs):
    sends, (pulled, hidden) = refs[:count], refs[count:]
    blocks = count * per
    me = lax.axis_index("dp")
    for b in range(blocks):
        pulled[b] = jnp.zeros(pulled.shape[1:], F32)
    m0 = order[0, 0]
    m1 = order[0, 1]
    for step, place, i in send_order(me, count, per):
        at = lanes(i)
        c = stack([g_ref[0, :, at], a_ref[0, :, at], second_grad[0, m0, :, at], second_grad[0, m1, :, at]]).astype(BF16)
        sends[step][8, :, lanes(place)] = c[0:16]
        sends[step][9, :, lanes(place)] = c[16:32]
        target = down_idx[0, i]
        pulled[target] = pulled[target] + times_transposed(c, w_down[0, i])
    for step, place, j in send_order(me, count, per):
        u = up_idx[0, j]
        at = lanes(u)
        x = stack([back[0, m0, :, at], second[0, m0, :, at], second_tan[0, m0, :, at],
                   second_tan[0, m1, :, at], back[0, m1, :, at], second[0, m1, :, at]]).astype(BF16)
        out = sends[step]
        here = lanes(place)
        for group in range(3):
            out[group, :, here] = x[16 * group:16 * group + 16]
        z = times(x, w_up[0, j])
        zb0, za0, ta0, ta1, zb1, za1 = (z[8 * k:8 * k + 8] for k in range(6))
        pg, pa, ga0, ga1 = (pulled[j, 8 * k:8 * k + 8] for k in range(4))
        sb0, sa0, sb1, sa1 = sigmoid(zb0), sigmoid(za0), sigmoid(zb1), sigmoid(za1)
        slope_a0 = slope_of(za0, sa0)
        slope_a1 = slope_of(za1, sa1)
        curve_a0 = sa0 * (1.0 - sa0) * (2.0 + za0 * (1.0 - 2.0 * sa0))
        curve_a1 = sa1 * (1.0 - sa1) * (2.0 + za1 * (1.0 - 2.0 * sa1))
        push = slope_a0 * pa + curve_a0 * ga0 * ta0
        e = jnp.concatenate([slope_of(zb0, sb0) * pg, push], 0).astype(BF16)
        out[3, :, here] = e
        out[4, :, here] = jnp.concatenate([slope_a0 * ga0, slope_a1 * ga1], 0).astype(BF16)
        hidden[j] = jnp.concatenate(
            [zb0 * sb0, za0 * sa0, slope_a0 * ta0, slope_a1 * ta1, zb1 * sb1, za1 * sa1], 0).astype(BF16)
        keep[j] = jnp.concatenate([slope_of(zb1, sb1), slope_a1, curve_a1 * ga1 * ta1], 0)
        pushes[:, lanes(j)] = e
    for step, place, i in send_order(me, count, per):
        y = hidden[down_idx[0, i]]
        for group in range(3):
            sends[step][5 + group, :, lanes(place)] = y[16 * group:16 * group + 16]


def forward_first(blocks, up_idx, down_idx, order, w_up, w_down, v_ref, t_ref, tan, pack, keep, hidden):
    m0 = order[0, 0]
    m1 = order[0, 1]
    for j in range(blocks):
        at = lanes(up_idx[0, j])
        x = stack([v_ref[0, :, at], t_ref[0, :, at], tan[0, m0, :, at], tan[0, m1, :, at]]).astype(BF16)
        z = times(x, w_up[0, j])
        zv, zt, z0, z1 = (z[8 * k:8 * k + 8] for k in range(4))
        hidden[j] = jnp.concatenate([zv * sigmoid(zv), slope_of(z0, sigmoid(z0)) * zt], 0).astype(BF16)
        keep[j] = slope_of(z1, sigmoid(z1))
    for i in range(blocks):
        at = lanes(i)
        moved = stack([v_ref[0, :, at], t_ref[0, :, at]]) + times(hidden[down_idx[0, i]], w_down[0, i])
        pack[:, at] = moved.astype(BF16)


def first_streams(count, per, up_idx, down_idx, order, w_up, w_down, g_ref, a_ref, pushes, v_ref, t_ref, tan,
                  near, far, keep_tan, packs, returned, hidden):
    blocks = count * per
    for b in range(blocks):
        returned[b] = stack([g_ref[0, :, lanes(b)], a_ref[0, :, lanes(b)]])
    for j in range(blocks):
        u = up_idx[0, j]
        returned[u] = returned[u] + times_transposed(pushes[:, lanes(j)], w_up[0, j])
    for b in range(blocks):
        packs[1, :, lanes(b)] = returned[b].astype(BF16)
    forward_first(blocks, up_idx, down_idx, order, w_up, w_down, v_ref, t_ref, tan, packs.at[0], keep_tan, hidden)
    hand_out(packs, near, far)


def back_second(count, per, up_idx, down_idx, w_up, w_down, rows, keep, pack, sends, pulled, returned):
    blocks = count * per
    me = lax.axis_index("dp")
    for b in range(blocks):
        pulled[b] = jnp.zeros(pulled.shape[1:], F32)
        returned[b] = rows[:, lanes(b)].astype(F32)
    for step, place, i in send_order(me, count, per):
        c = rows[:, lanes(i)]
        sends[step][1, :, lanes(place)] = c
        target = down_idx[0, i]
        pulled[target] = pulled[target] + times_transposed(c, w_down[0, i])
    for step, place, j in send_order(me, count, per):
        u = up_idx[0, j]
        slope_b, slope_a, push = (keep[j, 8 * k:8 * k + 8] for k in range(3))
        e = jnp.concatenate([slope_b * pulled[j, 0:8], slope_a * pulled[j, 8:16] + push], 0).astype(BF16)
        sends[step][0, :, lanes(place)] = e
        returned[u] = returned[u] + times_transposed(e, w_up[0, j])
    for b in range(blocks):
        pack[:, lanes(b)] = returned[b].astype(BF16)


def forward_second(blocks, up_idx, down_idx, w_up, w_down, rows, keep, pack, hidden):
    for j in range(blocks):
        z = times(rows[:, lanes(up_idx[0, j])], w_up[0, j])
        zv, zt = z[0:8], z[8:16]
        hidden[j] = jnp.concatenate([zv * sigmoid(zv), keep[j] * zt], 0).astype(BF16)
    for i in range(blocks):
        at = lanes(i)
        pack[:, at] = (rows[:, at].astype(F32) + times(hidden[down_idx[0, i]], w_down[0, i])).astype(BF16)


def near_phase(count, per, up_idx, down_idx, w_up, w_down, near_in, keep, keep_tan, far, *refs):
    sends, (pulled, returned, hidden) = refs[:count], refs[count:]
    odd = odd_section()

    @pl.when(odd == 0)
    def _():
        back_second(count, per, up_idx, down_idx, w_up, w_down, near_in, keep, far, sends, pulled, returned)

    @pl.when(odd == 1)
    def _():
        forward_second(count * per, up_idx, down_idx, w_up, w_down, near_in, keep_tan, far, hidden)


def far_phase(count, per, up_idx, down_idx, w_up, w_down, far_in, keep, keep_tan, *refs):
    done, near, refs = refs[:count], refs[count], refs[count + 1:]
    sends, (pulled, returned, hidden) = refs[:count], refs[count:]
    odd = odd_section()

    @pl.when(odd == 0)
    def _():
        for source, target in zip(done, sends):
            target[...] = source[...]
        forward_second(count * per, up_idx, down_idx, w_up, w_down, far_in, keep_tan, near, hidden)

    @pl.when(odd == 1)
    def _():
        back_second(count, per, up_idx, down_idx, w_up, w_down, far_in, keep, near, sends, pulled, returned)


def early_grads(count, per, *refs):
    early, grads = refs[:count], refs[count]
    for place in range(per):
        at = lanes(place)
        for out, left, right in ((0, 0, 3), (1, 5, 8)):
            xs = [early[source][left + k, :, at] for source in range(count) for k in range(2)]
            es = [early[source][right + k, :, at] for source in range(count) for k in range(2)]
            grads[out, place] = outer(xs, es)


def finish(count, per, scale, far, near, grads, *rest):
    early, late = rest[:count], rest[count:2 * count]
    values, score, tangent, adjoint, grad_up, grad_down, came = rest[2 * count:]
    take_in(near, far, came)
    moved = came[0].astype(F32)
    values[0] = moved[0:8].astype(BF16)
    tangent[0] = moved[8:16].astype(BF16)
    moved = came[1].astype(F32)
    score[0] = moved[0:8].astype(BF16)
    adjoint[0] = moved[8:16].astype(BF16)
    for place in range(per):
        at = lanes(place)
        for k, (out, group) in enumerate(((grad_up, 2), (grad_down, 7))):
            xs = [early[source][group, :, at] for source in range(count)]
            es = [late[source][k, :, at] for source in range(count)]
            out[0, place] = ((grads[k, place] + outer(xs, es)) * scale).astype(BF16)


def call(body, operands, spaces, outs, scratch, after=(), cost=LIGHT):
    taken = len(operands)

    def kernel(*refs):
        body(*refs[:taken], *refs[taken + len(after):])

    return pl.pallas_call(
        kernel,
        out_shape=outs,
        in_specs=[pl.BlockSpec(memory_space=space) for space in spaces] + [pl.BlockSpec(memory_space=pl.ANY)] * len(after),
        out_specs=[pl.BlockSpec(memory_space=pltpu.VMEM)] * len(outs),
        scratch_shapes=scratch,
        compiler_params=pltpu.CompilerParams(vmem_limit_bytes=LIMIT),
        cost_estimate=pl.CostEstimate(flops=cost, bytes_accessed=cost // 100, transcendentals=0),
    )(*operands, *after)


def on_device(w_up, up_index, w_down, down_index, tick_order, values_in, score_grad_in, tangent_in, state_adjoint_in,
              saved_back, saved_tan, saved_second, saved_second_tan, saved_second_grad):
    count = lax.axis_size("dp")
    blocks = w_up.shape[1]
    per = blocks // count
    width = values_in.shape[2]
    part = per * BLOCK
    scale = 1.0 / (values_in.shape[1] * count)
    shape = jax.ShapeDtypeStruct
    pair = shape((16, width), BF16)
    vmem, smem = pltpu.VMEM, pltpu.SMEM

    def body(f, *args):
        def kernel(*refs):
            f(*args, *refs)
        return kernel

    def to_replicas(parts):
        steps = [count - 1] + list(range(1, count - 1))
        return [parts[0]] + [lax.ppermute(parts[step], "dp", swap_route(step, count)) for step in steps]

    rows = (score_grad_in, state_adjoint_in, saved_back, saved_second, saved_second_tan, saved_second_grad)
    ten = shape((10, 16, part), BF16)
    (token,) = call(open_launch, (), [], [shape((8, BLOCK), F32)], [], cost=WORK)
    tables = (up_index, down_index, tick_order, w_up, w_down)
    keep, pushes, *early = call(
        body(first_rows, count, per), tables + rows, [smem] * 3 + [vmem] * 8,
        [shape((blocks, 24, BLOCK), F32), pair] + [ten] * count,
        [vmem((blocks, 32, BLOCK), F32), vmem((blocks, 48, BLOCK), BF16)],
        after=(token,), cost=WORK)
    near, far, keep_tan = call(
        body(first_streams, count, per),
        tables + (score_grad_in, state_adjoint_in, pushes, values_in, tangent_in, saved_tan), [smem] * 3 + [vmem] * 8,
        [pair, pair, shape((blocks, 8, BLOCK), F32)],
        [vmem((2, 16, width), BF16), vmem((blocks, 16, BLOCK), F32), vmem((blocks, 16, BLOCK), BF16)], cost=STREAMS)
    near, far = swap_sections(near, far)
    early = to_replicas(early)
    tables = (up_index, down_index, w_up, w_down)
    two = [shape((2, 16, part), BF16)] * count
    scratch = [vmem((blocks, 16, BLOCK), F32), vmem((blocks, 16, BLOCK), F32), vmem((blocks, 16, BLOCK), BF16)]
    far_out, *late = call(
        body(near_phase, count, per), tables + (near, keep, keep_tan), [smem] * 2 + [vmem] * 5, [pair] + two, scratch)
    near_out, *late = call(
        body(far_phase, count, per), tables + (far, keep, keep_tan, *late), [smem] * 2 + [vmem] * (5 + count),
        [pair] + two, scratch)
    near, far = swap_sections(near_out, far_out)
    late = to_replicas(late)
    (grads,) = call(
        body(early_grads, count, per), tuple(early), [vmem] * count, [shape((2, per, BLOCK, BLOCK), F32)], [],
        after=(far,))
    stream = shape((1,) + values_in.shape[1:], BF16)
    grad = shape((1, per, BLOCK, BLOCK), BF16)
    return tuple(call(
        body(finish, count, per, scale), (far, near, grads, *early, *late), [vmem] * (3 + 2 * count),
        [stream, stream, stream, stream, grad, grad], [vmem((2, 16, width), BF16)]))


def solution(mesh):
    layer = P("section", None, None, None)
    table = P("section", None)
    stream = P("section", "dp", None)
    saved = P("section", None, "dp", None)
    return jax.shard_map(
        on_device,
        mesh=mesh,
        in_specs=(layer, table, layer, table, table) + (stream,) * 4 + (saved,) * 5,
        out_specs=(stream,) * 4 + (P("section", "dp", None, None),) * 2,
        check_vma=False,
    )
```

```python
import jax
import jax.numpy as jnp
from jax import lax
from jax.experimental import pallas as pl
from jax.experimental.pallas import tpu as pltpu
from jax.sharding import PartitionSpec as P

BLOCK = 128
F32 = jnp.float32
BF16 = jnp.bfloat16
LIMIT = 40 * 1024 * 1024
WORK = 10 ** 10
LIGHT = 10 ** 4
PAD = BLOCK


def partner(me, step, count):
    if count & (count - 1) == 0:
        return me ^ step
    return lax.rem(me + step, count)


def swap_route(step, count):
    if count & (count - 1) == 0:
        return [(i, i ^ step) for i in range(count)]
    return [(i, (i + step) % count) for i in range(count)]


def swap_sections(near, far):
    count = lax.axis_size("section")
    far = lax.ppermute(far, "section", [(i, (i + 2 * (i % 2) - 1) % count) for i in range(count)])
    near = lax.ppermute(near, "section", [(i, i ^ 1) for i in range(count)])
    return near, far


def times(rows, weight):
    return lax.dot_general(rows, weight, (((1,), (0,)), ((), ())), preferred_element_type=F32)


def times_transposed(rows, weight):
    return lax.dot_general(rows, weight, (((1,), (1,)), ((), ())), preferred_element_type=F32)


def outer(xs, es):
    return lax.dot_general(jnp.concatenate(xs, 0), jnp.concatenate(es, 0), (((0,), (0,)), ((), ())),
                           preferred_element_type=F32)


def sigmoid(z):
    return 1.0 / (1.0 + jnp.exp(-z))


def slope_of(z, s):
    return s * (1.0 + z * (1.0 - s))


def lanes(block):
    if isinstance(block, int):
        return pl.ds(block * BLOCK, BLOCK)
    return pl.ds(pl.multiple_of(block * BLOCK, BLOCK), BLOCK)


def stack(parts):
    return jnp.concatenate([part.astype(F32) for part in parts], 0)


def send_order(me, count, per):
    for step in range(count):
        base = partner(me, step, count) * per
        for place in range(per):
            yield step, place, base + place


def odd_section():
    return lax.rem(lax.axis_index("section"), 2)


def take_in(near, far, packs):
    odd = odd_section()
    packs[1 - odd] = near[...]
    packs[odd] = far[:, :packs.shape[2]]


def open_launch(token):
    token[...] = jnp.zeros(token.shape, F32)


def first_rows(count, per, up_idx, down_idx, order, w_up, w_down, g_ref, a_ref, back, second, second_tan, second_grad,
               keep, pushes, *refs):
    sends, (pulled, hidden) = refs[:count], refs[count:]
    blocks = count * per
    me = lax.axis_index("dp")
    for b in range(blocks):
        pulled[b] = jnp.zeros(pulled.shape[1:], F32)
    m0 = order[0, 0]
    m1 = order[0, 1]
    for step, place, i in send_order(me, count, per):
        at = lanes(i)
        c = stack([g_ref[0, :, at], a_ref[0, :, at], second_grad[0, m0, :, at], second_grad[0, m1, :, at]]).astype(BF16)
        sends[step][8, :, lanes(place)] = c[0:16]
        sends[step][9, :, lanes(place)] = c[16:32]
        target = down_idx[0, i]
        pulled[target] = pulled[target] + times_transposed(c, w_down[0, i])
    for step, place, j in send_order(me, count, per):
        u = up_idx[0, j]
        at = lanes(u)
        x = stack([back[0, m0, :, at], second[0, m0, :, at], second_tan[0, m0, :, at],
                   second_tan[0, m1, :, at], back[0, m1, :, at], second[0, m1, :, at]]).astype(BF16)
        out = sends[step]
        here = lanes(place)
        for group in range(3):
            out[group, :, here] = x[16 * group:16 * group + 16]
        z = times(x, w_up[0, j])
        zb0, za0, ta0, ta1, zb1, za1 = (z[8 * k:8 * k + 8] for k in range(6))
        pg, pa, ga0, ga1 = (pulled[j, 8 * k:8 * k + 8] for k in range(4))
        sb0, sa0, sb1, sa1 = sigmoid(zb0), sigmoid(za0), sigmoid(zb1), sigmoid(za1)
        slope_a0 = slope_of(za0, sa0)
        slope_a1 = slope_of(za1, sa1)
        curve_a0 = sa0 * (1.0 - sa0) * (2.0 + za0 * (1.0 - 2.0 * sa0))
        curve_a1 = sa1 * (1.0 - sa1) * (2.0 + za1 * (1.0 - 2.0 * sa1))
        push = slope_a0 * pa + curve_a0 * ga0 * ta0
        e = jnp.concatenate([slope_of(zb0, sb0) * pg, push], 0).astype(BF16)
        out[3, :, here] = e
        out[4, :, here] = jnp.concatenate([slope_a0 * ga0, slope_a1 * ga1], 0).astype(BF16)
        hidden[j] = jnp.concatenate(
            [zb0 * sb0, za0 * sa0, slope_a0 * ta0, slope_a1 * ta1, zb1 * sb1, za1 * sa1], 0).astype(BF16)
        keep[j] = jnp.concatenate([slope_of(zb1, sb1), slope_a1, curve_a1 * ga1 * ta1], 0)
        pushes[:, lanes(j)] = e
    for step, place, i in send_order(me, count, per):
        y = hidden[down_idx[0, i]]
        for group in range(3):
            sends[step][5 + group, :, lanes(place)] = y[16 * group:16 * group + 16]


def forward_first(blocks, up_idx, down_idx, order, w_up, w_down, v_ref, t_ref, tan, pack, keep, hidden):
    m0 = order[0, 0]
    m1 = order[0, 1]
    for j in range(blocks):
        at = lanes(up_idx[0, j])
        x = stack([v_ref[0, :, at], t_ref[0, :, at], tan[0, m0, :, at], tan[0, m1, :, at]]).astype(BF16)
        z = times(x, w_up[0, j])
        zv, zt, z0, z1 = (z[8 * k:8 * k + 8] for k in range(4))
        hidden[j] = jnp.concatenate([zv * sigmoid(zv), slope_of(z0, sigmoid(z0)) * zt], 0).astype(BF16)
        keep[j] = slope_of(z1, sigmoid(z1))
    for i in range(blocks):
        at = lanes(i)
        moved = stack([v_ref[0, :, at], t_ref[0, :, at]]) + times(hidden[down_idx[0, i]], w_down[0, i])
        pack[:, at] = moved.astype(BF16)


def clear_pad(pack, blocks):
    if pack.shape[1] > blocks * BLOCK:
        pack[:, blocks * BLOCK:] = jnp.zeros((pack.shape[0], pack.shape[1] - blocks * BLOCK), BF16)


def back_streams(blocks, up_idx, w_up, g_ref, a_ref, pushes, pack, returned):
    for b in range(blocks):
        returned[b] = stack([g_ref[0, :, lanes(b)], a_ref[0, :, lanes(b)]])
    for j in range(blocks):
        u = up_idx[0, j]
        returned[u] = returned[u] + times_transposed(pushes[:, lanes(j)], w_up[0, j])
    for b in range(blocks):
        pack[:, lanes(b)] = returned[b].astype(BF16)


def first_streams(blocks, back_parity, up_idx, down_idx, order, w_up, w_down, g_ref, a_ref, pushes, v_ref, t_ref, tan,
                  pack, keep, returned, hidden):
    odd = odd_section()
    clear_pad(pack, blocks)

    @pl.when(odd == back_parity)
    def _():
        back_streams(blocks, up_idx, w_up, g_ref, a_ref, pushes, pack, returned)

    @pl.when(odd != back_parity)
    def _():
        forward_first(blocks, up_idx, down_idx, order, w_up, w_down, v_ref, t_ref, tan, pack, keep, hidden)


def back_second(count, per, up_idx, down_idx, w_up, w_down, rows, keep, pack, sends, pulled, returned):
    blocks = count * per
    me = lax.axis_index("dp")
    for b in range(blocks):
        pulled[b] = jnp.zeros(pulled.shape[1:], F32)
        returned[b] = rows[:, lanes(b)].astype(F32)
    for step, place, i in send_order(me, count, per):
        c = rows[:, lanes(i)]
        sends[step][1, :, lanes(place)] = c
        target = down_idx[0, i]
        pulled[target] = pulled[target] + times_transposed(c, w_down[0, i])
    for step, place, j in send_order(me, count, per):
        u = up_idx[0, j]
        slope_b, slope_a, push = (keep[j, 8 * k:8 * k + 8] for k in range(3))
        e = jnp.concatenate([slope_b * pulled[j, 0:8], slope_a * pulled[j, 8:16] + push], 0).astype(BF16)
        sends[step][0, :, lanes(place)] = e
        returned[u] = returned[u] + times_transposed(e, w_up[0, j])
    for b in range(blocks):
        pack[:, lanes(b)] = returned[b].astype(BF16)


def forward_second(blocks, up_idx, down_idx, w_up, w_down, rows, keep, pack, hidden):
    for j in range(blocks):
        z = times(rows[:, lanes(up_idx[0, j])], w_up[0, j])
        zv, zt = z[0:8], z[8:16]
        hidden[j] = jnp.concatenate([zv * sigmoid(zv), keep[j] * zt], 0).astype(BF16)
    for i in range(blocks):
        at = lanes(i)
        pack[:, at] = (rows[:, at].astype(F32) + times(hidden[down_idx[0, i]], w_down[0, i])).astype(BF16)


def near_phase(count, per, up_idx, down_idx, w_up, w_down, near_in, keep, keep_tan, far, *refs):
    sends, (pulled, returned, hidden) = refs[:count], refs[count:]
    odd = odd_section()
    clear_pad(far, count * per)

    @pl.when(odd == 0)
    def _():
        back_second(count, per, up_idx, down_idx, w_up, w_down, near_in, keep, far, sends, pulled, returned)

    @pl.when(odd == 1)
    def _():
        forward_second(count * per, up_idx, down_idx, w_up, w_down, near_in, keep_tan, far, hidden)


def far_phase(count, per, up_idx, down_idx, w_up, w_down, far_in, keep, keep_tan, *refs):
    done, near, refs = refs[:count], refs[count], refs[count + 1:]
    sends, (pulled, returned, hidden) = refs[:count], refs[count:]
    odd = odd_section()

    @pl.when(odd == 0)
    def _():
        for source, target in zip(done, sends):
            target[...] = source[...]
        forward_second(count * per, up_idx, down_idx, w_up, w_down, far_in, keep_tan, near, hidden)

    @pl.when(odd == 1)
    def _():
        back_second(count, per, up_idx, down_idx, w_up, w_down, far_in, keep, near, sends, pulled, returned)


def early_grads(count, per, *refs):
    early, grads = refs[:count], refs[count]
    for place in range(per):
        at = lanes(place)
        for out, left, right in ((0, 0, 3), (1, 5, 8)):
            xs = [early[source][left + k, :, at] for source in range(count) for k in range(2)]
            es = [early[source][right + k, :, at] for source in range(count) for k in range(2)]
            grads[out, place] = outer(xs, es)


def finish(count, per, scale, far, near, grads, *rest):
    early, late = rest[:count], rest[count:2 * count]
    values, score, tangent, adjoint, grad_up, grad_down, came = rest[2 * count:]
    take_in(near, far, came)
    moved = came[0].astype(F32)
    values[0] = moved[0:8].astype(BF16)
    tangent[0] = moved[8:16].astype(BF16)
    moved = came[1].astype(F32)
    score[0] = moved[0:8].astype(BF16)
    adjoint[0] = moved[8:16].astype(BF16)
    for place in range(per):
        at = lanes(place)
        for k, (out, group) in enumerate(((grad_up, 2), (grad_down, 7))):
            xs = [early[source][group, :, at] for source in range(count)]
            es = [late[source][k, :, at] for source in range(count)]
            out[0, place] = ((grads[k, place] + outer(xs, es)) * scale).astype(BF16)


def call(body, operands, spaces, outs, scratch, after=(), cost=LIGHT):
    taken = len(operands)

    def kernel(*refs):
        body(*refs[:taken], *refs[taken + len(after):])

    return pl.pallas_call(
        kernel,
        out_shape=outs,
        in_specs=[pl.BlockSpec(memory_space=space) for space in spaces] + [pl.BlockSpec(memory_space=pl.ANY)] * len(after),
        out_specs=[pl.BlockSpec(memory_space=pltpu.VMEM)] * len(outs),
        scratch_shapes=scratch,
        compiler_params=pltpu.CompilerParams(vmem_limit_bytes=LIMIT),
        cost_estimate=pl.CostEstimate(flops=cost, bytes_accessed=cost // 100, transcendentals=0),
    )(*operands, *after)


def on_device(w_up, up_index, w_down, down_index, tick_order, values_in, score_grad_in, tangent_in, state_adjoint_in,
              saved_back, saved_tan, saved_second, saved_second_tan, saved_second_grad):
    count = lax.axis_size("dp")
    blocks = w_up.shape[1]
    per = blocks // count
    width = values_in.shape[2]
    part = per * BLOCK
    scale = 1.0 / (values_in.shape[1] * count)
    shape = jax.ShapeDtypeStruct
    pair = shape((16, width), BF16)
    vmem, smem = pltpu.VMEM, pltpu.SMEM

    def body(f, *args):
        def kernel(*refs):
            f(*args, *refs)
        return kernel

    def to_replicas(parts):
        steps = [count - 1] + list(range(1, count - 1))
        return [parts[0]] + [lax.ppermute(parts[step], "dp", swap_route(step, count)) for step in steps]

    rows = (score_grad_in, state_adjoint_in, saved_back, saved_second, saved_second_tan, saved_second_grad)
    ten = shape((10, 16, part), BF16)
    (token,) = call(open_launch, (), [], [shape((8, BLOCK), F32)], [], cost=WORK)
    tables = (up_index, down_index, tick_order, w_up, w_down)
    keep, pushes, *early = call(
        body(first_rows, count, per), tables + rows, [smem] * 3 + [vmem] * 8,
        [shape((blocks, 24, BLOCK), F32), pair] + [ten] * count,
        [vmem((blocks, 32, BLOCK), F32), vmem((blocks, 48, BLOCK), BF16)],
        after=(token,), cost=WORK)
    taken = tables + (score_grad_in, state_adjoint_in, pushes, values_in, tangent_in, saved_tan)
    made = [shape((blocks, 8, BLOCK), F32)]
    long = shape((16, width + PAD), BF16)
    scratch = [vmem((blocks, 16, BLOCK), F32), vmem((blocks, 16, BLOCK), BF16)]
    far, far_keep = call(body(first_streams, blocks, 0), taken, [smem] * 3 + [vmem] * 8, [long] + made, scratch)
    near, near_keep = call(body(first_streams, blocks, 1), taken, [smem] * 3 + [vmem] * 8, [pair] + made, scratch,
                           after=(far,))
    near, far = swap_sections(near, far)
    early = to_replicas(early)
    tables = (up_index, down_index, w_up, w_down)
    two = [shape((2, 16, part), BF16)] * count
    scratch = [vmem((blocks, 16, BLOCK), F32), vmem((blocks, 16, BLOCK), F32), vmem((blocks, 16, BLOCK), BF16)]
    far_out, *late = call(
        body(near_phase, count, per), tables + (near, keep, far_keep), [smem] * 2 + [vmem] * 5, [long] + two, scratch)
    near_out, *late = call(
        body(far_phase, count, per), tables + (far, keep, near_keep, *late), [smem] * 2 + [vmem] * (5 + count),
        [pair] + two, scratch)
    near, far = swap_sections(near_out, far_out)
    late = to_replicas(late)
    (grads,) = call(
        body(early_grads, count, per), tuple(early), [vmem] * count, [shape((2, per, BLOCK, BLOCK), F32)], [])
    stream = shape((1,) + values_in.shape[1:], BF16)
    grad = shape((1, per, BLOCK, BLOCK), BF16)
    return tuple(call(
        body(finish, count, per, scale), (far, near, grads, *early, *late), [vmem] * (3 + 2 * count),
        [stream, stream, stream, stream, grad, grad], [vmem((2, 16, width), BF16)]))


def solution(mesh):
    layer = P("section", None, None, None)
    table = P("section", None)
    stream = P("section", "dp", None)
    saved = P("section", None, "dp", None)
    return jax.shard_map(
        on_device,
        mesh=mesh,
        in_specs=(layer, table, layer, table, table) + (stream,) * 4 + (saved,) * 5,
        out_specs=(stream,) * 4 + (P("section", "dp", None, None),) * 2,
        check_vma=False,
    )
```

```python
import jax
import jax.numpy as jnp
from jax import lax
from jax.experimental import pallas as pl
from jax.experimental.pallas import tpu as pltpu
from jax.sharding import PartitionSpec as P

BLOCK = 128
F32 = jnp.float32
BF16 = jnp.bfloat16
LIMIT = 40 * 1024 * 1024
WORK = 10 ** 10
LIGHT = 10 ** 4
PAD = BLOCK


def partner(me, step, count):
    if count & (count - 1) == 0:
        return me ^ step
    return lax.rem(me + step, count)


def swap_route(step, count):
    if count & (count - 1) == 0:
        return [(i, i ^ step) for i in range(count)]
    return [(i, (i + step) % count) for i in range(count)]


def swap_sections(near, far):
    count = lax.axis_size("section")
    far = lax.ppermute(far, "section", [(i, (i + 2 * (i % 2) - 1) % count) for i in range(count)])
    near = lax.ppermute(near, "section", [(i, i ^ 1) for i in range(count)])
    return near, far


def times(rows, weight):
    return lax.dot_general(rows, weight, (((1,), (0,)), ((), ())), preferred_element_type=F32)


def times_transposed(rows, weight):
    return lax.dot_general(rows, weight, (((1,), (1,)), ((), ())), preferred_element_type=F32)


def outer(xs, es):
    return lax.dot_general(jnp.concatenate(xs, 0), jnp.concatenate(es, 0), (((0,), (0,)), ((), ())),
                           preferred_element_type=F32)


def sigmoid(z):
    return 1.0 / (1.0 + jnp.exp(-z))


def slope_of(z, s):
    return s * (1.0 + z * (1.0 - s))


def lanes(block):
    if isinstance(block, int):
        return pl.ds(block * BLOCK, BLOCK)
    return pl.ds(pl.multiple_of(block * BLOCK, BLOCK), BLOCK)


def stack(parts):
    return jnp.concatenate([part.astype(F32) for part in parts], 0)


def send_order(me, count, per):
    for step in range(count):
        base = partner(me, step, count) * per
        for place in range(per):
            yield step, place, base + place


def odd_section():
    return lax.rem(lax.axis_index("section"), 2)


def take_in(near, far, packs):
    odd = odd_section()
    packs[1 - odd] = near[...]
    packs[odd] = far[:, :packs.shape[2]]


def open_launch(token):
    token[...] = jnp.zeros(token.shape, F32)


def first_rows(count, per, up_idx, down_idx, order, w_up, w_down, g_ref, a_ref, back, second, second_tan, second_grad,
               keep, pushes, *refs):
    sends, (pulled, products, hidden) = refs[:count], refs[count:]
    blocks = count * per
    me = lax.axis_index("dp")
    for b in range(blocks):
        pulled[b] = jnp.zeros(pulled.shape[1:], F32)
    m0 = order[0, 0]
    m1 = order[0, 1]
    for step, place, i in send_order(me, count, per):
        at = lanes(i)
        c = stack([g_ref[0, :, at], a_ref[0, :, at], second_grad[0, m0, :, at], second_grad[0, m1, :, at]]).astype(BF16)
        sends[step][8, :, lanes(place)] = c[0:16]
        sends[step][9, :, lanes(place)] = c[16:32]
        products[i] = times_transposed(c, w_down[0, i])
    add_at(pulled, products, down_idx)
    for step, place, j in send_order(me, count, per):
        u = up_idx[0, j]
        at = lanes(u)
        x = stack([back[0, m0, :, at], second[0, m0, :, at], second_tan[0, m0, :, at],
                   second_tan[0, m1, :, at], back[0, m1, :, at], second[0, m1, :, at]]).astype(BF16)
        out = sends[step]
        here = lanes(place)
        for group in range(3):
            out[group, :, here] = x[16 * group:16 * group + 16]
        z = times(x, w_up[0, j])
        zb0, za0, ta0, ta1, zb1, za1 = (z[8 * k:8 * k + 8] for k in range(6))
        pg, pa, ga0, ga1 = (pulled[j, 8 * k:8 * k + 8] for k in range(4))
        sb0, sa0, sb1, sa1 = sigmoid(zb0), sigmoid(za0), sigmoid(zb1), sigmoid(za1)
        slope_a0 = slope_of(za0, sa0)
        slope_a1 = slope_of(za1, sa1)
        curve_a0 = sa0 * (1.0 - sa0) * (2.0 + za0 * (1.0 - 2.0 * sa0))
        curve_a1 = sa1 * (1.0 - sa1) * (2.0 + za1 * (1.0 - 2.0 * sa1))
        push = slope_a0 * pa + curve_a0 * ga0 * ta0
        e = jnp.concatenate([slope_of(zb0, sb0) * pg, push], 0).astype(BF16)
        out[3, :, here] = e
        out[4, :, here] = jnp.concatenate([slope_a0 * ga0, slope_a1 * ga1], 0).astype(BF16)
        hidden[j] = jnp.concatenate(
            [zb0 * sb0, za0 * sa0, slope_a0 * ta0, slope_a1 * ta1, zb1 * sb1, za1 * sa1], 0).astype(BF16)
        keep[j] = jnp.concatenate([slope_of(zb1, sb1), slope_a1, curve_a1 * ga1 * ta1], 0)
        pushes[:, lanes(j)] = e
    for step, place, i in send_order(me, count, per):
        y = hidden[down_idx[0, i]]
        for group in range(3):
            sends[step][5 + group, :, lanes(place)] = y[16 * group:16 * group + 16]


def forward_first(blocks, up_idx, down_idx, order, w_up, w_down, v_ref, t_ref, tan, pack, keep, hidden):
    m0 = order[0, 0]
    m1 = order[0, 1]
    for j in range(blocks):
        at = lanes(up_idx[0, j])
        x = stack([v_ref[0, :, at], t_ref[0, :, at], tan[0, m0, :, at], tan[0, m1, :, at]]).astype(BF16)
        z = times(x, w_up[0, j])
        zv, zt, z0, z1 = (z[8 * k:8 * k + 8] for k in range(4))
        hidden[j] = jnp.concatenate([zv * sigmoid(zv), slope_of(z0, sigmoid(z0)) * zt], 0).astype(BF16)
        keep[j] = slope_of(z1, sigmoid(z1))
    for i in range(blocks):
        at = lanes(i)
        moved = stack([v_ref[0, :, at], t_ref[0, :, at]]) + times(hidden[down_idx[0, i]], w_down[0, i])
        pack[:, at] = moved.astype(BF16)


def add_at(totals, products, table):
    for k in range(products.shape[0]):
        target = table[0, k]
        totals[target] = totals[target] + products[k]


def clear_pad(pack, blocks):
    if pack.shape[1] > blocks * BLOCK:
        pack[:, blocks * BLOCK:] = jnp.zeros((pack.shape[0], pack.shape[1] - blocks * BLOCK), BF16)


def back_streams(blocks, up_idx, w_up, g_ref, a_ref, pushes, pack, returned, products):
    for b in range(blocks):
        returned[b] = stack([g_ref[0, :, lanes(b)], a_ref[0, :, lanes(b)]])
    for j in range(blocks):
        products[j] = times_transposed(pushes[:, lanes(j)], w_up[0, j])
    add_at(returned, products, up_idx)
    for b in range(blocks):
        pack[:, lanes(b)] = returned[b].astype(BF16)


def first_streams(blocks, back_parity, up_idx, down_idx, order, w_up, w_down, g_ref, a_ref, pushes, v_ref, t_ref, tan,
                  pack, keep, returned, products, hidden):
    odd = odd_section()
    clear_pad(pack, blocks)

    @pl.when(odd == back_parity)
    def _():
        back_streams(blocks, up_idx, w_up, g_ref, a_ref, pushes, pack, returned, products)

    @pl.when(odd != back_parity)
    def _():
        forward_first(blocks, up_idx, down_idx, order, w_up, w_down, v_ref, t_ref, tan, pack, keep, hidden)


def back_second(count, per, up_idx, down_idx, w_up, w_down, rows, keep, pack, sends, pulled, returned, products):
    blocks = count * per
    me = lax.axis_index("dp")
    for b in range(blocks):
        pulled[b] = jnp.zeros(pulled.shape[1:], F32)
        returned[b] = rows[:, lanes(b)].astype(F32)
    for step, place, i in send_order(me, count, per):
        c = rows[:, lanes(i)]
        sends[step][1, :, lanes(place)] = c
        products[i] = times_transposed(c, w_down[0, i])
    add_at(pulled, products, down_idx)
    for step, place, j in send_order(me, count, per):
        slope_b, slope_a, push = (keep[j, 8 * k:8 * k + 8] for k in range(3))
        e = jnp.concatenate([slope_b * pulled[j, 0:8], slope_a * pulled[j, 8:16] + push], 0).astype(BF16)
        sends[step][0, :, lanes(place)] = e
        products[j] = times_transposed(e, w_up[0, j])
    add_at(returned, products, up_idx)
    for b in range(blocks):
        pack[:, lanes(b)] = returned[b].astype(BF16)


def forward_second(blocks, up_idx, down_idx, w_up, w_down, rows, keep, pack, hidden):
    for j in range(blocks):
        z = times(rows[:, lanes(up_idx[0, j])], w_up[0, j])
        zv, zt = z[0:8], z[8:16]
        hidden[j] = jnp.concatenate([zv * sigmoid(zv), keep[j] * zt], 0).astype(BF16)
    for i in range(blocks):
        at = lanes(i)
        pack[:, at] = (rows[:, at].astype(F32) + times(hidden[down_idx[0, i]], w_down[0, i])).astype(BF16)


def near_phase(count, per, up_idx, down_idx, w_up, w_down, near_in, keep, keep_tan, far, *refs):
    sends, (pulled, returned, products, hidden) = refs[:count], refs[count:]
    odd = odd_section()
    clear_pad(far, count * per)

    @pl.when(odd == 0)
    def _():
        back_second(count, per, up_idx, down_idx, w_up, w_down, near_in, keep, far, sends, pulled, returned, products)

    @pl.when(odd == 1)
    def _():
        forward_second(count * per, up_idx, down_idx, w_up, w_down, near_in, keep_tan, far, hidden)


def far_phase(count, per, up_idx, down_idx, w_up, w_down, far_in, keep, keep_tan, *refs):
    done, near, refs = refs[:count], refs[count], refs[count + 1:]
    sends, (pulled, returned, products, hidden) = refs[:count], refs[count:]
    odd = odd_section()

    @pl.when(odd == 0)
    def _():
        for source, target in zip(done, sends):
            target[...] = source[...]
        forward_second(count * per, up_idx, down_idx, w_up, w_down, far_in, keep_tan, near, hidden)

    @pl.when(odd == 1)
    def _():
        back_second(count, per, up_idx, down_idx, w_up, w_down, far_in, keep, near, sends, pulled, returned, products)


def early_grads(count, per, *refs):
    early, grads = refs[:count], refs[count]
    for place in range(per):
        at = lanes(place)
        for out, left, right in ((0, 0, 3), (1, 5, 8)):
            xs = [early[source][left + k, :, at] for source in range(count) for k in range(2)]
            es = [early[source][right + k, :, at] for source in range(count) for k in range(2)]
            grads[out, place] = outer(xs, es)


def finish(count, per, scale, far, near, grads, *rest):
    early, late = rest[:count], rest[count:2 * count]
    outs, (came, streams, held, sems) = rest[2 * count:2 * count + 6], rest[2 * count + 6:]
    copies = []

    def leave(source, target):
        copies.append(pltpu.make_async_copy(source, target, sems.at[len(copies)]))
        copies[-1].start()

    take_in(near, far, came)
    forward = came[0].astype(F32)
    backward = came[1].astype(F32)
    for k, rows in enumerate((forward[0:8], backward[0:8], forward[8:16], backward[8:16])):
        streams[k] = rows.astype(BF16)
        leave(streams.at[k], outs[k].at[0])
    for place in range(per):
        at = lanes(place)
        for k, group in enumerate((2, 7)):
            xs = [early[source][group, :, at] for source in range(count)]
            es = [late[source][k, :, at] for source in range(count)]
            held[k, place] = ((grads[k, place] + outer(xs, es)) * scale).astype(BF16)
            leave(held.at[k, place], outs[4 + k].at[0, place])
    for copy in copies:
        copy.wait()


def call(body, operands, spaces, outs, scratch, after=(), cost=LIGHT, out_space=pltpu.VMEM):
    taken = len(operands)

    def kernel(*refs):
        body(*refs[:taken], *refs[taken + len(after):])

    return pl.pallas_call(
        kernel,
        out_shape=outs,
        in_specs=[pl.BlockSpec(memory_space=space) for space in spaces] + [pl.BlockSpec(memory_space=pl.ANY)] * len(after),
        out_specs=[pl.BlockSpec(memory_space=out_space)] * len(outs),
        scratch_shapes=scratch,
        compiler_params=pltpu.CompilerParams(vmem_limit_bytes=LIMIT),
        cost_estimate=pl.CostEstimate(flops=cost, bytes_accessed=cost // 100, transcendentals=0),
    )(*operands, *after)


def on_device(w_up, up_index, w_down, down_index, tick_order, values_in, score_grad_in, tangent_in, state_adjoint_in,
              saved_back, saved_tan, saved_second, saved_second_tan, saved_second_grad):
    count = lax.axis_size("dp")
    blocks = w_up.shape[1]
    per = blocks // count
    width = values_in.shape[2]
    part = per * BLOCK
    scale = 1.0 / (values_in.shape[1] * count)
    shape = jax.ShapeDtypeStruct
    pair = shape((16, width), BF16)
    vmem, smem = pltpu.VMEM, pltpu.SMEM

    def body(f, *args):
        def kernel(*refs):
            f(*args, *refs)
        return kernel

    def to_replicas(parts):
        steps = [count - 1] + list(range(1, count - 1))
        return [parts[0]] + [lax.ppermute(parts[step], "dp", swap_route(step, count)) for step in steps]

    rows = (score_grad_in, state_adjoint_in, saved_back, saved_second, saved_second_tan, saved_second_grad)
    ten = shape((10, 16, part), BF16)
    (token,) = call(open_launch, (), [], [shape((8, BLOCK), F32)], [], cost=WORK)
    tables = (up_index, down_index, tick_order, w_up, w_down)
    keep, pushes, *early = call(
        body(first_rows, count, per), tables + rows, [smem] * 3 + [vmem] * 8,
        [shape((blocks, 24, BLOCK), F32), pair] + [ten] * count,
        [vmem((blocks, 32, BLOCK), F32), vmem((blocks, 32, BLOCK), F32), vmem((blocks, 48, BLOCK), BF16)],
        after=(token,), cost=WORK)
    taken = tables + (score_grad_in, state_adjoint_in, pushes, values_in, tangent_in, saved_tan)
    made = [shape((blocks, 8, BLOCK), F32)]
    long = shape((16, width + PAD), BF16)
    scratch = [vmem((blocks, 16, BLOCK), F32), vmem((blocks, 16, BLOCK), F32), vmem((blocks, 16, BLOCK), BF16)]
    far, far_keep = call(body(first_streams, blocks, 0), taken, [smem] * 3 + [vmem] * 8, [long] + made, scratch)
    near, near_keep = call(body(first_streams, blocks, 1), taken, [smem] * 3 + [vmem] * 8, [pair] + made, scratch,
                           after=(far,))
    near, far = swap_sections(near, far)
    early = to_replicas(early)
    tables = (up_index, down_index, w_up, w_down)
    two = [shape((2, 16, part), BF16)] * count
    scratch = [vmem((blocks, 16, BLOCK), F32)] + scratch
    far_out, *late = call(
        body(near_phase, count, per), tables + (near, keep, far_keep), [smem] * 2 + [vmem] * 5, [long] + two, scratch)
    near_out, *late = call(
        body(far_phase, count, per), tables + (far, keep, near_keep, *late), [smem] * 2 + [vmem] * (5 + count),
        [pair] + two, scratch)
    near, far = swap_sections(near_out, far_out)
    late = to_replicas(late)
    (grads,) = call(
        body(early_grads, count, per), tuple(early), [vmem] * count, [shape((2, per, BLOCK, BLOCK), F32)], [])
    stream = shape((1,) + values_in.shape[1:], BF16)
    grad = shape((1, per, BLOCK, BLOCK), BF16)
    return tuple(call(
        body(finish, count, per, scale), (far, near, grads, *early, *late), [vmem] * (3 + 2 * count),
        [stream] * 4 + [grad] * 2,
        [vmem((2, 16, width), BF16), vmem((4,) + values_in.shape[1:], BF16), vmem((2, per, BLOCK, BLOCK), BF16),
         pltpu.SemaphoreType.DMA((4 + 2 * per,))], out_space=pl.ANY))


def solution(mesh):
    layer = P("section", None, None, None)
    table = P("section", None)
    stream = P("section", "dp", None)
    saved = P("section", None, "dp", None)
    return jax.shard_map(
        on_device,
        mesh=mesh,
        in_specs=(layer, table, layer, table, table) + (stream,) * 4 + (saved,) * 5,
        out_specs=(stream,) * 4 + (P("section", "dp", None, None),) * 2,
        check_vma=False,
    )
```

```python
import jax
import jax.numpy as jnp
from jax import lax
from jax.experimental import pallas as pl
from jax.experimental.pallas import tpu as pltpu
from jax.sharding import PartitionSpec as P

BLOCK = 128
F32 = jnp.float32
BF16 = jnp.bfloat16
LIMIT = 40 * 1024 * 1024
WORK = 10 ** 10
LIGHT = 10 ** 4
PAD = BLOCK
C_FAR = LIGHT
C_NEAR = LIGHT
C_NEAR_PHASE = LIGHT
C_FAR_PHASE = 147 * 10 ** 7


def partner(me, step, count):
    if count & (count - 1) == 0:
        return me ^ step
    return lax.rem(me + step, count)


def swap_route(step, count):
    if count & (count - 1) == 0:
        return [(i, i ^ step) for i in range(count)]
    return [(i, (i + step) % count) for i in range(count)]


def swap_sections(near, far):
    count = lax.axis_size("section")
    far = lax.ppermute(far, "section", [(i, (i + 2 * (i % 2) - 1) % count) for i in range(count)])
    near = lax.ppermute(near, "section", [(i, i ^ 1) for i in range(count)])
    return near, far


def times(rows, weight):
    return lax.dot_general(rows, weight, (((1,), (0,)), ((), ())), preferred_element_type=F32)


def times_transposed(rows, weight):
    return lax.dot_general(rows, weight, (((1,), (1,)), ((), ())), preferred_element_type=F32)


def outer(xs, es):
    return lax.dot_general(jnp.concatenate(xs, 0), jnp.concatenate(es, 0), (((0,), (0,)), ((), ())),
                           preferred_element_type=F32)


def sigmoid(z):
    return 1.0 / (1.0 + jnp.exp(-z))


def slope_of(z, s):
    return s * (1.0 + z * (1.0 - s))


def lanes(block):
    if isinstance(block, int):
        return pl.ds(block * BLOCK, BLOCK)
    return pl.ds(pl.multiple_of(block * BLOCK, BLOCK), BLOCK)


def stack(parts):
    return jnp.concatenate([part.astype(F32) for part in parts], 0)


def send_order(me, count, per):
    for step in range(count):
        base = partner(me, step, count) * per
        for place in range(per):
            yield step, place, base + place


def odd_section():
    return lax.rem(lax.axis_index("section"), 2)


def take_in(near, far, packs):
    odd = odd_section()
    packs[1 - odd] = near[...]
    packs[odd] = far[:, :packs.shape[2]]


def open_launch(token):
    token[...] = jnp.zeros(token.shape, F32)


def first_rows(count, per, up_idx, down_idx, order, w_up, w_down, g_ref, a_ref, back, second, second_tan, second_grad,
               keep, pushes, *refs):
    sends, (pulled, hidden) = refs[:count], refs[count:]
    clear_pad(sends[-1], 10 * per)
    blocks = count * per
    me = lax.axis_index("dp")
    for b in range(blocks):
        pulled[b] = jnp.zeros(pulled.shape[1:], F32)
    m0 = order[0, 0]
    m1 = order[0, 1]
    for step, place, i in send_order(me, count, per):
        at = lanes(i)
        c = stack([g_ref[0, :, at], a_ref[0, :, at], second_grad[0, m0, :, at], second_grad[0, m1, :, at]]).astype(BF16)
        sends[step][:, lanes(8 * per + place)] = c[0:16]
        sends[step][:, lanes(9 * per + place)] = c[16:32]
        target = down_idx[0, i]
        pulled[target] = pulled[target] + times_transposed(c, w_down[0, i])
    for step, place, j in send_order(me, count, per):
        u = up_idx[0, j]
        at = lanes(u)
        x = stack([back[0, m0, :, at], second[0, m0, :, at], second_tan[0, m0, :, at],
                   second_tan[0, m1, :, at], back[0, m1, :, at], second[0, m1, :, at]]).astype(BF16)
        out = sends[step]
        for group in range(3):
            out[:, lanes(group * per + place)] = x[16 * group:16 * group + 16]
        z = times(x, w_up[0, j])
        zb0, za0, ta0, ta1, zb1, za1 = (z[8 * k:8 * k + 8] for k in range(6))
        pg, pa, ga0, ga1 = (pulled[j, 8 * k:8 * k + 8] for k in range(4))
        sb0, sa0, sb1, sa1 = sigmoid(zb0), sigmoid(za0), sigmoid(zb1), sigmoid(za1)
        slope_a0 = slope_of(za0, sa0)
        slope_a1 = slope_of(za1, sa1)
        curve_a0 = sa0 * (1.0 - sa0) * (2.0 + za0 * (1.0 - 2.0 * sa0))
        curve_a1 = sa1 * (1.0 - sa1) * (2.0 + za1 * (1.0 - 2.0 * sa1))
        push = slope_a0 * pa + curve_a0 * ga0 * ta0
        e = jnp.concatenate([slope_of(zb0, sb0) * pg, push], 0).astype(BF16)
        out[:, lanes(3 * per + place)] = e
        out[:, lanes(4 * per + place)] = jnp.concatenate([slope_a0 * ga0, slope_a1 * ga1], 0).astype(BF16)
        hidden[j] = jnp.concatenate(
            [zb0 * sb0, za0 * sa0, slope_a0 * ta0, slope_a1 * ta1, zb1 * sb1, za1 * sa1], 0).astype(BF16)
        keep[j] = jnp.concatenate([slope_of(zb1, sb1), slope_a1, curve_a1 * ga1 * ta1], 0)
        pushes[:, lanes(j)] = e
    for step, place, i in send_order(me, count, per):
        y = hidden[down_idx[0, i]]
        for group in range(3):
            sends[step][:, lanes((5 + group) * per + place)] = y[16 * group:16 * group + 16]


def forward_first(blocks, up_idx, down_idx, order, w_up, w_down, v_ref, t_ref, tan, pack, keep, hidden):
    m0 = order[0, 0]
    m1 = order[0, 1]
    for j in range(blocks):
        at = lanes(up_idx[0, j])
        x = stack([v_ref[0, :, at], t_ref[0, :, at], tan[0, m0, :, at], tan[0, m1, :, at]]).astype(BF16)
        z = times(x, w_up[0, j])
        zv, zt, z0, z1 = (z[8 * k:8 * k + 8] for k in range(4))
        hidden[j] = jnp.concatenate([zv * sigmoid(zv), slope_of(z0, sigmoid(z0)) * zt], 0).astype(BF16)
        keep[j] = slope_of(z1, sigmoid(z1))
    for i in range(blocks):
        at = lanes(i)
        moved = stack([v_ref[0, :, at], t_ref[0, :, at]]) + times(hidden[down_idx[0, i]], w_down[0, i])
        pack[:, at] = moved.astype(BF16)


def clear_pad(pack, blocks):
    if pack.shape[1] > blocks * BLOCK:
        pack[:, blocks * BLOCK:] = jnp.zeros((pack.shape[0], pack.shape[1] - blocks * BLOCK), BF16)


def back_streams(blocks, up_idx, w_up, g_ref, a_ref, pushes, pack, returned):
    for b in range(blocks):
        returned[b] = stack([g_ref[0, :, lanes(b)], a_ref[0, :, lanes(b)]])
    for j in range(blocks):
        u = up_idx[0, j]
        returned[u] = returned[u] + times_transposed(pushes[:, lanes(j)], w_up[0, j])
    for b in range(blocks):
        pack[:, lanes(b)] = returned[b].astype(BF16)


def first_streams(blocks, back_parity, held, up_idx, down_idx, order, w_up, w_down, g_ref, a_ref, pushes, v_ref, t_ref,
                  tan, *refs):
    pack, keep = refs[held:held + 2]
    returned, hidden = refs[2 * held + 2:]
    for source, target in zip(refs[:held], refs[held + 2:2 * held + 2]):
        target[...] = source[...]
    odd = odd_section()
    clear_pad(pack, blocks)

    @pl.when(odd == back_parity)
    def _():
        back_streams(blocks, up_idx, w_up, g_ref, a_ref, pushes, pack, returned)

    @pl.when(odd != back_parity)
    def _():
        forward_first(blocks, up_idx, down_idx, order, w_up, w_down, v_ref, t_ref, tan, pack, keep, hidden)


def back_second(count, per, up_idx, down_idx, w_up, w_down, rows, keep, pack, sends, pulled, returned):
    blocks = count * per
    me = lax.axis_index("dp")
    for b in range(blocks):
        pulled[b] = jnp.zeros(pulled.shape[1:], F32)
        returned[b] = rows[:, lanes(b)].astype(F32)
    for step, place, i in send_order(me, count, per):
        c = rows[:, lanes(i)]
        sends[step][:, lanes(per + place)] = c
        target = down_idx[0, i]
        pulled[target] = pulled[target] + times_transposed(c, w_down[0, i])
    for step, place, j in send_order(me, count, per):
        u = up_idx[0, j]
        slope_b, slope_a, push = (keep[j, 8 * k:8 * k + 8] for k in range(3))
        e = jnp.concatenate([slope_b * pulled[j, 0:8], slope_a * pulled[j, 8:16] + push], 0).astype(BF16)
        sends[step][:, lanes(place)] = e
        returned[u] = returned[u] + times_transposed(e, w_up[0, j])
    for b in range(blocks):
        pack[:, lanes(b)] = returned[b].astype(BF16)


def forward_second(blocks, up_idx, down_idx, w_up, w_down, rows, keep, pack, hidden):
    for j in range(blocks):
        z = times(rows[:, lanes(up_idx[0, j])], w_up[0, j])
        zv, zt = z[0:8], z[8:16]
        hidden[j] = jnp.concatenate([zv * sigmoid(zv), keep[j] * zt], 0).astype(BF16)
    for i in range(blocks):
        at = lanes(i)
        pack[:, at] = (rows[:, at].astype(F32) + times(hidden[down_idx[0, i]], w_down[0, i])).astype(BF16)


def near_phase(count, per, up_idx, down_idx, w_up, w_down, near_in, keep, keep_tan, far, *refs):
    sends, (pulled, returned, hidden) = refs[:count], refs[count:]
    odd = odd_section()
    clear_pad(far, count * per)

    @pl.when(odd == 0)
    def _():
        back_second(count, per, up_idx, down_idx, w_up, w_down, near_in, keep, far, sends, pulled, returned)

    @pl.when(odd == 1)
    def _():
        forward_second(count * per, up_idx, down_idx, w_up, w_down, near_in, keep_tan, far, hidden)


def far_phase(count, per, up_idx, down_idx, w_up, w_down, far_in, keep, keep_tan, *refs):
    done, near, refs = refs[:count], refs[count], refs[count + 1:]
    sends, (pulled, returned, hidden) = refs[:count], refs[count:]
    odd = odd_section()

    @pl.when(odd == 0)
    def _():
        for source, target in zip(done, sends):
            target[...] = source[...]
        forward_second(count * per, up_idx, down_idx, w_up, w_down, far_in, keep_tan, near, hidden)

    @pl.when(odd == 1)
    def _():
        back_second(count, per, up_idx, down_idx, w_up, w_down, far_in, keep, near, sends, pulled, returned)


def early_grads(count, per, *refs):
    early, grads = refs[:count], refs[count]
    for place in range(per):
        for out, left, right in ((0, 0, 3), (1, 5, 8)):
            xs = [early[source][:, lanes((left + k) * per + place)] for source in range(count) for k in range(2)]
            es = [early[source][:, lanes((right + k) * per + place)] for source in range(count) for k in range(2)]
            grads[out, place] = outer(xs, es)


def finish(count, per, scale, far, near, grads, *rest):
    early, late = rest[:count], rest[count:2 * count]
    values, score, tangent, adjoint, grad_up, grad_down, came = rest[2 * count:]
    take_in(near, far, came)
    moved = came[0].astype(F32)
    values[0] = moved[0:8].astype(BF16)
    tangent[0] = moved[8:16].astype(BF16)
    moved = came[1].astype(F32)
    score[0] = moved[0:8].astype(BF16)
    adjoint[0] = moved[8:16].astype(BF16)
    for place in range(per):
        for k, (out, group) in enumerate(((grad_up, 2), (grad_down, 7))):
            xs = [early[source][:, lanes(group * per + place)] for source in range(count)]
            es = [late[source][:, lanes(k * per + place)] for source in range(count)]
            out[0, place] = ((grads[k, place] + outer(xs, es)) * scale).astype(BF16)


def call(body, operands, spaces, outs, scratch, after=(), cost=LIGHT):
    taken = len(operands)

    def kernel(*refs):
        body(*refs[:taken], *refs[taken + len(after):])

    return pl.pallas_call(
        kernel,
        out_shape=outs,
        in_specs=[pl.BlockSpec(memory_space=space) for space in spaces] + [pl.BlockSpec(memory_space=pl.ANY)] * len(after),
        out_specs=[pl.BlockSpec(memory_space=pltpu.VMEM)] * len(outs),
        scratch_shapes=scratch,
        compiler_params=pltpu.CompilerParams(vmem_limit_bytes=LIMIT),
        cost_estimate=pl.CostEstimate(flops=cost, bytes_accessed=cost // 100, transcendentals=0),
    )(*operands, *after)


def on_device(w_up, up_index, w_down, down_index, tick_order, values_in, score_grad_in, tangent_in, state_adjoint_in,
              saved_back, saved_tan, saved_second, saved_second_tan, saved_second_grad):
    count = lax.axis_size("dp")
    blocks = w_up.shape[1]
    per = blocks // count
    width = values_in.shape[2]
    part = per * BLOCK
    scale = 1.0 / (values_in.shape[1] * count)
    shape = jax.ShapeDtypeStruct
    pair = shape((16, width), BF16)
    vmem, smem = pltpu.VMEM, pltpu.SMEM

    def body(f, *args):
        def kernel(*refs):
            f(*args, *refs)
        return kernel

    def to_replicas(parts):
        steps = [count - 1] + list(range(1, count - 1))
        return [parts[0]] + [lax.ppermute(parts[step], "dp", swap_route(step, count)) for step in steps]

    rows = (score_grad_in, state_adjoint_in, saved_back, saved_second, saved_second_tan, saved_second_grad)
    ten = [shape((16, 10 * part), BF16)] * (count - 1) + [shape((16, 10 * part + 4 * PAD), BF16)]
    (token,) = call(open_launch, (), [], [shape((8, BLOCK), F32)], [], cost=WORK)
    tables = (up_index, down_index, tick_order, w_up, w_down)
    keep, pushes, *early = call(
        body(first_rows, count, per), tables + rows, [smem] * 3 + [vmem] * 8,
        [shape((blocks, 24, BLOCK), F32), pair] + ten,
        [vmem((blocks, 32, BLOCK), F32), vmem((blocks, 48, BLOCK), BF16)],
        after=(token,), cost=WORK)
    taken = tables + (score_grad_in, state_adjoint_in, pushes, values_in, tangent_in, saved_tan)
    made = [shape((blocks, 8, BLOCK), F32)]
    long = shape((16, width + PAD), BF16)
    scratch = [vmem((blocks, 16, BLOCK), F32), vmem((blocks, 16, BLOCK), BF16)]
    far, far_keep = call(
        body(first_streams, blocks, 0, 0), taken, [smem] * 3 + [vmem] * 8, [long] + made, scratch, cost=C_FAR)
    neighbours = early[1:count - 1]
    near, near_keep, *neighbours = call(
        body(first_streams, blocks, 1, len(neighbours)), taken + tuple(neighbours),
        [smem] * 3 + [vmem] * (8 + len(neighbours)), [pair] + made + ten[:len(neighbours)], scratch, after=(far,),
        cost=C_NEAR)
    early = [early[0], *neighbours, early[count - 1]]
    near, far = swap_sections(near, far)
    early = to_replicas(early)
    tables = (up_index, down_index, w_up, w_down)
    two = [shape((16, 2 * part), BF16)] * count
    scratch = [vmem((blocks, 16, BLOCK), F32), vmem((blocks, 16, BLOCK), F32), vmem((blocks, 16, BLOCK), BF16)]
    far_out, *late = call(
        body(near_phase, count, per), tables + (near, keep, far_keep), [smem] * 2 + [vmem] * 5, [long] + two, scratch,
        cost=C_NEAR_PHASE)
    near_out, *late = call(
        body(far_phase, count, per), tables + (far, keep, near_keep, *late), [smem] * 2 + [vmem] * (5 + count),
        [pair] + two, scratch, cost=C_FAR_PHASE)
    near, far = swap_sections(near_out, far_out)
    late = to_replicas(late)
    (grads,) = call(
        body(early_grads, count, per), tuple(early), [vmem] * count, [shape((2, per, BLOCK, BLOCK), F32)], [])
    stream = shape((1,) + values_in.shape[1:], BF16)
    grad = shape((1, per, BLOCK, BLOCK), BF16)
    return tuple(call(
        body(finish, count, per, scale), (far, near, grads, *early, *late), [vmem] * (3 + 2 * count),
        [stream, stream, stream, stream, grad, grad], [vmem((2, 16, width), BF16)]))


def solution(mesh):
    layer = P("section", None, None, None)
    table = P("section", None)
    stream = P("section", "dp", None)
    saved = P("section", None, "dp", None)
    return jax.shard_map(
        on_device,
        mesh=mesh,
        in_specs=(layer, table, layer, table, table) + (stream,) * 4 + (saved,) * 5,
        out_specs=(stream,) * 4 + (P("section", "dp", None, None),) * 2,
        check_vma=False,
    )
```

```python
import jax
import jax.numpy as jnp
from jax import lax
from jax.experimental import pallas as pl
from jax.experimental.pallas import tpu as pltpu
from jax.sharding import PartitionSpec as P

BLOCK = 128
F32 = jnp.float32
BF16 = jnp.bfloat16
LIMIT = 40 * 1024 * 1024
WORK = 10 ** 10
LIGHT = 10 ** 4
PAD = BLOCK
C_FAR = LIGHT
C_NEAR = LIGHT
C_NEAR_PHASE = LIGHT
C_FAR_PHASE = 200 * 10 ** 7


def partner(me, step, count):
    if count & (count - 1) == 0:
        return me ^ step
    return lax.rem(me + step, count)


def swap_route(step, count):
    if count & (count - 1) == 0:
        return [(i, i ^ step) for i in range(count)]
    return [(i, (i + step) % count) for i in range(count)]


def swap_sections(near, far):
    count = lax.axis_size("section")
    far = lax.ppermute(far, "section", [(i, (i + 2 * (i % 2) - 1) % count) for i in range(count)])
    near = lax.ppermute(near, "section", [(i, i ^ 1) for i in range(count)])
    return near, far


def times(rows, weight):
    return lax.dot_general(rows, weight, (((1,), (0,)), ((), ())), preferred_element_type=F32)


def times_transposed(rows, weight):
    return lax.dot_general(rows, weight, (((1,), (1,)), ((), ())), preferred_element_type=F32)


def outer(xs, es):
    return lax.dot_general(jnp.concatenate(xs, 0), jnp.concatenate(es, 0), (((0,), (0,)), ((), ())),
                           preferred_element_type=F32)


def sigmoid(z):
    return 1.0 / (1.0 + jnp.exp(-z))


def slope_of(z, s):
    return s * (1.0 + z * (1.0 - s))


def lanes(block):
    if isinstance(block, int):
        return pl.ds(block * BLOCK, BLOCK)
    return pl.ds(pl.multiple_of(block * BLOCK, BLOCK), BLOCK)


def stack(parts):
    return jnp.concatenate([part.astype(F32) for part in parts], 0)


def send_order(me, count, per):
    for step in range(count):
        base = partner(me, step, count) * per
        for place in range(per):
            yield step, place, base + place


def odd_section():
    return lax.rem(lax.axis_index("section"), 2)


def take_in(near, far, packs):
    odd = odd_section()
    packs[1 - odd] = near[...]
    packs[odd] = far[:, :packs.shape[2]]


def open_launch(token):
    token[...] = jnp.zeros(token.shape, F32)


def first_rows(count, per, up_idx, down_idx, order, w_up, w_down, g_ref, a_ref, back, second, second_tan, second_grad,
               keep, pushes, *refs):
    sends, (pulled, hidden) = refs[:count], refs[count:]
    blocks = count * per
    me = lax.axis_index("dp")
    for b in range(blocks):
        pulled[b] = jnp.zeros(pulled.shape[1:], F32)
    m0 = order[0, 0]
    m1 = order[0, 1]
    for step, place, i in send_order(me, count, per):
        at = lanes(i)
        c = stack([g_ref[0, :, at], a_ref[0, :, at], second_grad[0, m0, :, at], second_grad[0, m1, :, at]]).astype(BF16)
        sends[step][:, lanes(8 * per + place)] = c[0:16]
        sends[step][:, lanes(9 * per + place)] = c[16:32]
        target = down_idx[0, i]
        pulled[target] = pulled[target] + times_transposed(c, w_down[0, i])
    for step, place, j in send_order(me, count, per):
        u = up_idx[0, j]
        at = lanes(u)
        x = stack([back[0, m0, :, at], second[0, m0, :, at], second_tan[0, m0, :, at],
                   second_tan[0, m1, :, at], back[0, m1, :, at], second[0, m1, :, at]]).astype(BF16)
        out = sends[step]
        for group in range(3):
            out[:, lanes(group * per + place)] = x[16 * group:16 * group + 16]
        z = times(x, w_up[0, j])
        zb0, za0, ta0, ta1, zb1, za1 = (z[8 * k:8 * k + 8] for k in range(6))
        pg, pa, ga0, ga1 = (pulled[j, 8 * k:8 * k + 8] for k in range(4))
        sb0, sa0, sb1, sa1 = sigmoid(zb0), sigmoid(za0), sigmoid(zb1), sigmoid(za1)
        slope_a0 = slope_of(za0, sa0)
        slope_a1 = slope_of(za1, sa1)
        curve_a0 = sa0 * (1.0 - sa0) * (2.0 + za0 * (1.0 - 2.0 * sa0))
        curve_a1 = sa1 * (1.0 - sa1) * (2.0 + za1 * (1.0 - 2.0 * sa1))
        push = slope_a0 * pa + curve_a0 * ga0 * ta0
        e = jnp.concatenate([slope_of(zb0, sb0) * pg, push], 0).astype(BF16)
        out[:, lanes(3 * per + place)] = e
        out[:, lanes(4 * per + place)] = jnp.concatenate([slope_a0 * ga0, slope_a1 * ga1], 0).astype(BF16)
        hidden[j] = jnp.concatenate(
            [zb0 * sb0, za0 * sa0, slope_a0 * ta0, slope_a1 * ta1, zb1 * sb1, za1 * sa1], 0).astype(BF16)
        keep[j] = jnp.concatenate([slope_of(zb1, sb1), slope_a1, curve_a1 * ga1 * ta1], 0)
        pushes[:, lanes(j)] = e
    for step, place, i in send_order(me, count, per):
        y = hidden[down_idx[0, i]]
        for group in range(3):
            sends[step][:, lanes((5 + group) * per + place)] = y[16 * group:16 * group + 16]


def forward_first(blocks, up_idx, down_idx, order, w_up, w_down, v_ref, t_ref, tan, pack, keep, hidden):
    m0 = order[0, 0]
    m1 = order[0, 1]
    for j in range(blocks):
        at = lanes(up_idx[0, j])
        x = stack([v_ref[0, :, at], t_ref[0, :, at], tan[0, m0, :, at], tan[0, m1, :, at]]).astype(BF16)
        z = times(x, w_up[0, j])
        zv, zt, z0, z1 = (z[8 * k:8 * k + 8] for k in range(4))
        hidden[j] = jnp.concatenate([zv * sigmoid(zv), slope_of(z0, sigmoid(z0)) * zt], 0).astype(BF16)
        keep[j] = slope_of(z1, sigmoid(z1))
    for i in range(blocks):
        at = lanes(i)
        moved = stack([v_ref[0, :, at], t_ref[0, :, at]]) + times(hidden[down_idx[0, i]], w_down[0, i])
        pack[:, at] = moved.astype(BF16)


def clear_pad(pack, blocks):
    if pack.shape[1] > blocks * BLOCK:
        pack[:, blocks * BLOCK:] = jnp.zeros((pack.shape[0], pack.shape[1] - blocks * BLOCK), BF16)


def back_streams(blocks, up_idx, w_up, g_ref, a_ref, pushes, pack, returned):
    for b in range(blocks):
        returned[b] = stack([g_ref[0, :, lanes(b)], a_ref[0, :, lanes(b)]])
    for j in range(blocks):
        u = up_idx[0, j]
        returned[u] = returned[u] + times_transposed(pushes[:, lanes(j)], w_up[0, j])
    for b in range(blocks):
        pack[:, lanes(b)] = returned[b].astype(BF16)


def first_streams(blocks, back_parity, held, up_idx, down_idx, order, w_up, w_down, g_ref, a_ref, pushes, v_ref, t_ref,
                  tan, *refs):
    pack, keep = refs[held:held + 2]
    returned, hidden = refs[2 * held + 2:]
    for source, target in zip(refs[:held], refs[held + 2:2 * held + 2]):
        target[...] = source[...]
    odd = odd_section()
    clear_pad(pack, blocks)

    @pl.when(odd == back_parity)
    def _():
        back_streams(blocks, up_idx, w_up, g_ref, a_ref, pushes, pack, returned)

    @pl.when(odd != back_parity)
    def _():
        forward_first(blocks, up_idx, down_idx, order, w_up, w_down, v_ref, t_ref, tan, pack, keep, hidden)


def back_second(count, per, up_idx, down_idx, w_up, w_down, rows, keep, pack, sends, pulled, returned):
    blocks = count * per
    me = lax.axis_index("dp")
    for b in range(blocks):
        pulled[b] = jnp.zeros(pulled.shape[1:], F32)
        returned[b] = rows[:, lanes(b)].astype(F32)
    for step, place, i in send_order(me, count, per):
        c = rows[:, lanes(i)]
        sends[step][:, lanes(per + place)] = c
        target = down_idx[0, i]
        pulled[target] = pulled[target] + times_transposed(c, w_down[0, i])
    for step, place, j in send_order(me, count, per):
        u = up_idx[0, j]
        slope_b, slope_a, push = (keep[j, 8 * k:8 * k + 8] for k in range(3))
        e = jnp.concatenate([slope_b * pulled[j, 0:8], slope_a * pulled[j, 8:16] + push], 0).astype(BF16)
        sends[step][:, lanes(place)] = e
        returned[u] = returned[u] + times_transposed(e, w_up[0, j])
    for b in range(blocks):
        pack[:, lanes(b)] = returned[b].astype(BF16)


def forward_second(blocks, up_idx, down_idx, w_up, w_down, rows, keep, pack, hidden):
    for j in range(blocks):
        z = times(rows[:, lanes(up_idx[0, j])], w_up[0, j])
        zv, zt = z[0:8], z[8:16]
        hidden[j] = jnp.concatenate([zv * sigmoid(zv), keep[j] * zt], 0).astype(BF16)
    for i in range(blocks):
        at = lanes(i)
        pack[:, at] = (rows[:, at].astype(F32) + times(hidden[down_idx[0, i]], w_down[0, i])).astype(BF16)


def near_phase(count, per, up_idx, down_idx, w_up, w_down, near_in, keep, keep_tan, far, *refs):
    sends, (pulled, returned, hidden) = refs[:count], refs[count:]
    odd = odd_section()
    clear_pad(far, count * per)

    @pl.when(odd == 0)
    def _():
        back_second(count, per, up_idx, down_idx, w_up, w_down, near_in, keep, far, sends, pulled, returned)

    @pl.when(odd == 1)
    def _():
        forward_second(count * per, up_idx, down_idx, w_up, w_down, near_in, keep_tan, far, hidden)


def far_phase(count, per, up_idx, down_idx, w_up, w_down, far_in, keep, keep_tan, *refs):
    done, near, refs = refs[:count], refs[count], refs[count + 1:]
    sends, (pulled, returned, hidden) = refs[:count], refs[count:]
    odd = odd_section()

    @pl.when(odd == 0)
    def _():
        for source, target in zip(done, sends):
            target[...] = source[...]
        forward_second(count * per, up_idx, down_idx, w_up, w_down, far_in, keep_tan, near, hidden)

    @pl.when(odd == 1)
    def _():
        back_second(count, per, up_idx, down_idx, w_up, w_down, far_in, keep, near, sends, pulled, returned)


def early_grads(count, per, *refs):
    early, grads = refs[:count], refs[count]
    for place in range(per):
        for out, left, right in ((0, 0, 3), (1, 5, 8)):
            xs = [early[source][:, lanes((left + k) * per + place)] for source in range(count) for k in range(2)]
            es = [early[source][:, lanes((right + k) * per + place)] for source in range(count) for k in range(2)]
            grads[out, place] = outer(xs, es)


def finish(count, per, scale, far, near, grads, *rest):
    early, late = rest[:count], rest[count:2 * count]
    values, score, tangent, adjoint, grad_up, grad_down, came = rest[2 * count:]
    take_in(near, far, came)
    moved = came[0].astype(F32)
    values[0] = moved[0:8].astype(BF16)
    tangent[0] = moved[8:16].astype(BF16)
    moved = came[1].astype(F32)
    score[0] = moved[0:8].astype(BF16)
    adjoint[0] = moved[8:16].astype(BF16)
    for place in range(per):
        for k, (out, group) in enumerate(((grad_up, 2), (grad_down, 7))):
            xs = [early[source][:, lanes(group * per + place)] for source in range(count)]
            es = [late[source][:, lanes(k * per + place)] for source in range(count)]
            out[0, place] = ((grads[k, place] + outer(xs, es)) * scale).astype(BF16)


def call(body, operands, spaces, outs, scratch, after=(), cost=LIGHT):
    taken = len(operands)

    def kernel(*refs):
        body(*refs[:taken], *refs[taken + len(after):])

    return pl.pallas_call(
        kernel,
        out_shape=outs,
        in_specs=[pl.BlockSpec(memory_space=space) for space in spaces] + [pl.BlockSpec(memory_space=pl.ANY)] * len(after),
        out_specs=[pl.BlockSpec(memory_space=pltpu.VMEM)] * len(outs),
        scratch_shapes=scratch,
        compiler_params=pltpu.CompilerParams(vmem_limit_bytes=LIMIT),
        cost_estimate=pl.CostEstimate(flops=cost, bytes_accessed=cost // 100, transcendentals=0),
    )(*operands, *after)


def on_device(w_up, up_index, w_down, down_index, tick_order, values_in, score_grad_in, tangent_in, state_adjoint_in,
              saved_back, saved_tan, saved_second, saved_second_tan, saved_second_grad):
    count = lax.axis_size("dp")
    blocks = w_up.shape[1]
    per = blocks // count
    width = values_in.shape[2]
    part = per * BLOCK
    scale = 1.0 / (values_in.shape[1] * count)
    shape = jax.ShapeDtypeStruct
    pair = shape((16, width), BF16)
    vmem, smem = pltpu.VMEM, pltpu.SMEM

    def body(f, *args):
        def kernel(*refs):
            f(*args, *refs)
        return kernel

    def to_replicas(parts):
        steps = [count - 1] + list(range(1, count - 1))
        return [parts[0]] + [lax.ppermute(parts[step], "dp", swap_route(step, count)) for step in steps]

    rows = (score_grad_in, state_adjoint_in, saved_back, saved_second, saved_second_tan, saved_second_grad)
    ten = [shape((16, 10 * part), BF16)] * (count - 1) + [shape((16, 10 * part), BF16)]
    (token,) = call(open_launch, (), [], [shape((8, BLOCK), F32)], [], cost=WORK)
    tables = (up_index, down_index, tick_order, w_up, w_down)
    keep, pushes, *early = call(
        body(first_rows, count, per), tables + rows, [smem] * 3 + [vmem] * 8,
        [shape((blocks, 24, BLOCK), F32), pair] + ten,
        [vmem((blocks, 32, BLOCK), F32), vmem((blocks, 48, BLOCK), BF16)],
        after=(token,), cost=WORK)
    taken = tables + (score_grad_in, state_adjoint_in, pushes, values_in, tangent_in, saved_tan)
    made = [shape((blocks, 8, BLOCK), F32)]
    long = shape((16, width + PAD), BF16)
    scratch = [vmem((blocks, 16, BLOCK), F32), vmem((blocks, 16, BLOCK), BF16)]
    far, far_keep = call(
        body(first_streams, blocks, 0, 0), taken, [smem] * 3 + [vmem] * 8, [long] + made, scratch, cost=C_FAR)
    neighbours = early[1:count - 1]
    near, near_keep, *neighbours = call(
        body(first_streams, blocks, 1, len(neighbours)), taken + tuple(neighbours),
        [smem] * 3 + [vmem] * (8 + len(neighbours)), [pair] + made + ten[:len(neighbours)], scratch, after=(far,),
        cost=C_NEAR)
    early = [early[0], *neighbours, early[count - 1]]
    near, far = swap_sections(near, far)
    early = to_replicas(early)
    tables = (up_index, down_index, w_up, w_down)
    two = [shape((16, 2 * part), BF16)] * count
    scratch = [vmem((blocks, 16, BLOCK), F32), vmem((blocks, 16, BLOCK), F32), vmem((blocks, 16, BLOCK), BF16)]
    far_out, *late = call(
        body(near_phase, count, per), tables + (near, keep, far_keep), [smem] * 2 + [vmem] * 5, [long] + two, scratch,
        cost=C_NEAR_PHASE)
    near_out, *late = call(
        body(far_phase, count, per), tables + (far, keep, near_keep, *late), [smem] * 2 + [vmem] * (5 + count),
        [pair] + two, scratch, cost=C_FAR_PHASE, after=(early[1],))
    near, far = swap_sections(near_out, far_out)
    late = to_replicas(late)
    (grads,) = call(
        body(early_grads, count, per), tuple(early), [vmem] * count, [shape((2, per, BLOCK, BLOCK), F32)], [])
    stream = shape((1,) + values_in.shape[1:], BF16)
    grad = shape((1, per, BLOCK, BLOCK), BF16)
    return tuple(call(
        body(finish, count, per, scale), (far, near, grads, *early, *late), [vmem] * (3 + 2 * count),
        [stream, stream, stream, stream, grad, grad], [vmem((2, 16, width), BF16)]))


def solution(mesh):
    layer = P("section", None, None, None)
    table = P("section", None)
    stream = P("section", "dp", None)
    saved = P("section", None, "dp", None)
    return jax.shard_map(
        on_device,
        mesh=mesh,
        in_specs=(layer, table, layer, table, table) + (stream,) * 4 + (saved,) * 5,
        out_specs=(stream,) * 4 + (P("section", "dp", None, None),) * 2,
        check_vma=False,
    )
```

```python
import jax
import jax.numpy as jnp
from jax import lax
from jax.experimental import pallas as pl
from jax.experimental.pallas import tpu as pltpu
from jax.sharding import PartitionSpec as P

BLOCK = 128
F32 = jnp.float32
BF16 = jnp.bfloat16
LIMIT = 40 * 1024 * 1024
WORK = 10 ** 10
LIGHT = 10 ** 4
PAD = BLOCK
C_FAR = LIGHT
C_NEAR = LIGHT
C_NEAR_PHASE = LIGHT
C_FAR_PHASE = 144 * 10 ** 7


def partner(me, step, count):
    if count & (count - 1) == 0:
        return me ^ step
    return lax.rem(me + step, count)


def swap_route(step, count):
    if count & (count - 1) == 0:
        return [(i, i ^ step) for i in range(count)]
    return [(i, (i + step) % count) for i in range(count)]


def swap_sections(near, far):
    count = lax.axis_size("section")
    far = lax.ppermute(far, "section", [(i, (i + 2 * (i % 2) - 1) % count) for i in range(count)])
    near = lax.ppermute(near, "section", [(i, i ^ 1) for i in range(count)])
    return near, far


def times(rows, weight):
    return lax.dot_general(rows, weight, (((1,), (0,)), ((), ())), preferred_element_type=F32)


def times_transposed(rows, weight):
    return lax.dot_general(rows, weight, (((1,), (1,)), ((), ())), preferred_element_type=F32)


def outer(xs, es):
    return lax.dot_general(jnp.concatenate(xs, 0), jnp.concatenate(es, 0), (((0,), (0,)), ((), ())),
                           preferred_element_type=F32)


def sigmoid(z):
    return 1.0 / (1.0 + jnp.exp(-z))


def slope_of(z, s):
    return s * (1.0 + z * (1.0 - s))


def lanes(block):
    if isinstance(block, int):
        return pl.ds(block * BLOCK, BLOCK)
    return pl.ds(pl.multiple_of(block * BLOCK, BLOCK), BLOCK)


def stack(parts):
    return jnp.concatenate([part.astype(F32) for part in parts], 0)


def send_order(me, count, per):
    for step in range(count):
        base = partner(me, step, count) * per
        for place in range(per):
            yield step, place, base + place


def odd_section():
    return lax.rem(lax.axis_index("section"), 2)


def take_in(near, far, packs):
    odd = odd_section()
    packs[1 - odd] = near[...]
    packs[odd] = far[:, :packs.shape[2]]


def open_launch(token):
    token[...] = jnp.zeros(token.shape, F32)


def first_rows(count, per, up_idx, down_idx, order, w_up, w_down, g_ref, a_ref, back, second, second_tan, second_grad,
               keep, pushes, *refs):
    sends, (pulled, hidden) = refs[:count], refs[count:]
    clear_pad(sends[1], 10 * per)
    blocks = count * per
    me = lax.axis_index("dp")
    for b in range(blocks):
        pulled[b] = jnp.zeros(pulled.shape[1:], F32)
    m0 = order[0, 0]
    m1 = order[0, 1]
    for step, place, i in send_order(me, count, per):
        at = lanes(i)
        c = stack([g_ref[0, :, at], a_ref[0, :, at], second_grad[0, m0, :, at], second_grad[0, m1, :, at]]).astype(BF16)
        sends[step][:, lanes(8 * per + place)] = c[0:16]
        sends[step][:, lanes(9 * per + place)] = c[16:32]
        target = down_idx[0, i]
        pulled[target] = pulled[target] + times_transposed(c, w_down[0, i])
    for step, place, j in send_order(me, count, per):
        u = up_idx[0, j]
        at = lanes(u)
        x = stack([back[0, m0, :, at], second[0, m0, :, at], second_tan[0, m0, :, at],
                   second_tan[0, m1, :, at], back[0, m1, :, at], second[0, m1, :, at]]).astype(BF16)
        out = sends[step]
        for group in range(3):
            out[:, lanes(group * per + place)] = x[16 * group:16 * group + 16]
        z = times(x, w_up[0, j])
        zb0, za0, ta0, ta1, zb1, za1 = (z[8 * k:8 * k + 8] for k in range(6))
        pg, pa, ga0, ga1 = (pulled[j, 8 * k:8 * k + 8] for k in range(4))
        sb0, sa0, sb1, sa1 = sigmoid(zb0), sigmoid(za0), sigmoid(zb1), sigmoid(za1)
        slope_a0 = slope_of(za0, sa0)
        slope_a1 = slope_of(za1, sa1)
        curve_a0 = sa0 * (1.0 - sa0) * (2.0 + za0 * (1.0 - 2.0 * sa0))
        curve_a1 = sa1 * (1.0 - sa1) * (2.0 + za1 * (1.0 - 2.0 * sa1))
        push = slope_a0 * pa + curve_a0 * ga0 * ta0
        e = jnp.concatenate([slope_of(zb0, sb0) * pg, push], 0).astype(BF16)
        out[:, lanes(3 * per + place)] = e
        out[:, lanes(4 * per + place)] = jnp.concatenate([slope_a0 * ga0, slope_a1 * ga1], 0).astype(BF16)
        hidden[j] = jnp.concatenate(
            [zb0 * sb0, za0 * sa0, slope_a0 * ta0, slope_a1 * ta1, zb1 * sb1, za1 * sa1], 0).astype(BF16)
        keep[j] = jnp.concatenate([slope_of(zb1, sb1), slope_a1, curve_a1 * ga1 * ta1], 0)
        pushes[:, lanes(j)] = e
    for step, place, i in send_order(me, count, per):
        y = hidden[down_idx[0, i]]
        for group in range(3):
            sends[step][:, lanes((5 + group) * per + place)] = y[16 * group:16 * group + 16]


def forward_first(blocks, up_idx, down_idx, order, w_up, w_down, v_ref, t_ref, tan, pack, keep, hidden):
    m0 = order[0, 0]
    m1 = order[0, 1]
    for j in range(blocks):
        at = lanes(up_idx[0, j])
        x = stack([v_ref[0, :, at], t_ref[0, :, at], tan[0, m0, :, at], tan[0, m1, :, at]]).astype(BF16)
        z = times(x, w_up[0, j])
        zv, zt, z0, z1 = (z[8 * k:8 * k + 8] for k in range(4))
        hidden[j] = jnp.concatenate([zv * sigmoid(zv), slope_of(z0, sigmoid(z0)) * zt], 0).astype(BF16)
        keep[j] = slope_of(z1, sigmoid(z1))
    for i in range(blocks):
        at = lanes(i)
        moved = stack([v_ref[0, :, at], t_ref[0, :, at]]) + times(hidden[down_idx[0, i]], w_down[0, i])
        pack[:, at] = moved.astype(BF16)


def clear_pad(pack, blocks):
    if pack.shape[1] > blocks * BLOCK:
        pack[:, blocks * BLOCK:] = jnp.zeros((pack.shape[0], pack.shape[1] - blocks * BLOCK), BF16)


def back_streams(blocks, up_idx, w_up, g_ref, a_ref, pushes, pack, returned):
    for b in range(blocks):
        returned[b] = stack([g_ref[0, :, lanes(b)], a_ref[0, :, lanes(b)]])
    for j in range(blocks):
        u = up_idx[0, j]
        returned[u] = returned[u] + times_transposed(pushes[:, lanes(j)], w_up[0, j])
    for b in range(blocks):
        pack[:, lanes(b)] = returned[b].astype(BF16)


def first_streams(blocks, back_parity, held, up_idx, down_idx, order, w_up, w_down, g_ref, a_ref, pushes, v_ref, t_ref,
                  tan, *refs):
    pack, keep = refs[held:held + 2]
    returned, hidden = refs[2 * held + 2:]
    for source, target in zip(refs[:held], refs[held + 2:2 * held + 2]):
        target[...] = source[...]
    odd = odd_section()
    clear_pad(pack, blocks)

    @pl.when(odd == back_parity)
    def _():
        back_streams(blocks, up_idx, w_up, g_ref, a_ref, pushes, pack, returned)

    @pl.when(odd != back_parity)
    def _():
        forward_first(blocks, up_idx, down_idx, order, w_up, w_down, v_ref, t_ref, tan, pack, keep, hidden)


def back_second(count, per, up_idx, down_idx, w_up, w_down, rows, keep, pack, sends, pulled, returned):
    blocks = count * per
    me = lax.axis_index("dp")
    for b in range(blocks):
        pulled[b] = jnp.zeros(pulled.shape[1:], F32)
        returned[b] = rows[:, lanes(b)].astype(F32)
    for step, place, i in send_order(me, count, per):
        c = rows[:, lanes(i)]
        sends[step][:, lanes(per + place)] = c
        target = down_idx[0, i]
        pulled[target] = pulled[target] + times_transposed(c, w_down[0, i])
    for step, place, j in send_order(me, count, per):
        u = up_idx[0, j]
        slope_b, slope_a, push = (keep[j, 8 * k:8 * k + 8] for k in range(3))
        e = jnp.concatenate([slope_b * pulled[j, 0:8], slope_a * pulled[j, 8:16] + push], 0).astype(BF16)
        sends[step][:, lanes(place)] = e
        returned[u] = returned[u] + times_transposed(e, w_up[0, j])
    for b in range(blocks):
        pack[:, lanes(b)] = returned[b].astype(BF16)


def forward_second(blocks, up_idx, down_idx, w_up, w_down, rows, keep, pack, hidden):
    for j in range(blocks):
        z = times(rows[:, lanes(up_idx[0, j])], w_up[0, j])
        zv, zt = z[0:8], z[8:16]
        hidden[j] = jnp.concatenate([zv * sigmoid(zv), keep[j] * zt], 0).astype(BF16)
    for i in range(blocks):
        at = lanes(i)
        pack[:, at] = (rows[:, at].astype(F32) + times(hidden[down_idx[0, i]], w_down[0, i])).astype(BF16)


def near_phase(count, per, up_idx, down_idx, w_up, w_down, near_in, keep, keep_tan, far, *refs):
    sends, (pulled, returned, hidden) = refs[:count], refs[count:]
    odd = odd_section()
    clear_pad(far, count * per)

    @pl.when(odd == 0)
    def _():
        back_second(count, per, up_idx, down_idx, w_up, w_down, near_in, keep, far, sends, pulled, returned)

    @pl.when(odd == 1)
    def _():
        forward_second(count * per, up_idx, down_idx, w_up, w_down, near_in, keep_tan, far, hidden)


def far_phase(count, per, up_idx, down_idx, w_up, w_down, far_in, keep, keep_tan, *refs):
    done, near, refs = refs[:count], refs[count], refs[count + 1:]
    sends, (pulled, returned, hidden) = refs[:count], refs[count:]
    odd = odd_section()

    @pl.when(odd == 0)
    def _():
        for source, target in zip(done, sends):
            target[...] = source[...]
        forward_second(count * per, up_idx, down_idx, w_up, w_down, far_in, keep_tan, near, hidden)

    @pl.when(odd == 1)
    def _():
        back_second(count, per, up_idx, down_idx, w_up, w_down, far_in, keep, near, sends, pulled, returned)


def early_grads(count, per, *refs):
    early, grads = refs[:count], refs[count]
    for place in range(per):
        for out, left, right in ((0, 0, 3), (1, 5, 8)):
            xs = [early[source][:, lanes((left + k) * per + place)] for source in range(count) for k in range(2)]
            es = [early[source][:, lanes((right + k) * per + place)] for source in range(count) for k in range(2)]
            grads[out, place] = outer(xs, es)


def finish(count, per, scale, far, near, grads, *rest):
    early, late = rest[:count], rest[count:2 * count]
    values, score, tangent, adjoint, grad_up, grad_down, came = rest[2 * count:]
    take_in(near, far, came)
    moved = came[0].astype(F32)
    values[0] = moved[0:8].astype(BF16)
    tangent[0] = moved[8:16].astype(BF16)
    moved = came[1].astype(F32)
    score[0] = moved[0:8].astype(BF16)
    adjoint[0] = moved[8:16].astype(BF16)
    for place in range(per):
        for k, (out, group) in enumerate(((grad_up, 2), (grad_down, 7))):
            xs = [early[source][:, lanes(group * per + place)] for source in range(count)]
            es = [late[source][:, lanes(k * per + place)] for source in range(count)]
            out[0, place] = ((grads[k, place] + outer(xs, es)) * scale).astype(BF16)


def call(body, operands, spaces, outs, scratch, after=(), cost=LIGHT):
    taken = len(operands)

    def kernel(*refs):
        body(*refs[:taken], *refs[taken + len(after):])

    return pl.pallas_call(
        kernel,
        out_shape=outs,
        in_specs=[pl.BlockSpec(memory_space=space) for space in spaces] + [pl.BlockSpec(memory_space=pl.ANY)] * len(after),
        out_specs=[pl.BlockSpec(memory_space=pltpu.VMEM)] * len(outs),
        scratch_shapes=scratch,
        compiler_params=pltpu.CompilerParams(vmem_limit_bytes=LIMIT),
        cost_estimate=pl.CostEstimate(flops=cost, bytes_accessed=cost // 100, transcendentals=0),
    )(*operands, *after)


def on_device(w_up, up_index, w_down, down_index, tick_order, values_in, score_grad_in, tangent_in, state_adjoint_in,
              saved_back, saved_tan, saved_second, saved_second_tan, saved_second_grad):
    count = lax.axis_size("dp")
    blocks = w_up.shape[1]
    per = blocks // count
    width = values_in.shape[2]
    part = per * BLOCK
    scale = 1.0 / (values_in.shape[1] * count)
    shape = jax.ShapeDtypeStruct
    pair = shape((16, width), BF16)
    vmem, smem = pltpu.VMEM, pltpu.SMEM

    def body(f, *args):
        def kernel(*refs):
            f(*args, *refs)
        return kernel

    def to_replicas(parts):
        steps = [count - 1] + list(range(1, count - 1))
        return [parts[0]] + [lax.ppermute(parts[step], "dp", swap_route(step, count)) for step in steps]

    rows = (score_grad_in, state_adjoint_in, saved_back, saved_second, saved_second_tan, saved_second_grad)
    ten = [shape((16, 10 * part + (4 * PAD if step == 1 else 0)), BF16) for step in range(count)]
    (token,) = call(open_launch, (), [], [shape((8, BLOCK), F32)], [], cost=WORK)
    tables = (up_index, down_index, tick_order, w_up, w_down)
    keep, pushes, *early = call(
        body(first_rows, count, per), tables + rows, [smem] * 3 + [vmem] * 8,
        [shape((blocks, 24, BLOCK), F32), pair] + ten,
        [vmem((blocks, 32, BLOCK), F32), vmem((blocks, 48, BLOCK), BF16)],
        after=(token,), cost=WORK)
    taken = tables + (score_grad_in, state_adjoint_in, pushes, values_in, tangent_in, saved_tan)
    made = [shape((blocks, 8, BLOCK), F32)]
    long = shape((16, width + PAD), BF16)
    scratch = [vmem((blocks, 16, BLOCK), F32), vmem((blocks, 16, BLOCK), BF16)]
    far, far_keep = call(
        body(first_streams, blocks, 0, 0), taken, [smem] * 3 + [vmem] * 8, [long] + made, scratch, cost=C_FAR)
    neighbours = early[2:count - 1]
    near, near_keep, *neighbours = call(
        body(first_streams, blocks, 1, len(neighbours)), taken + tuple(neighbours),
        [smem] * 3 + [vmem] * (8 + len(neighbours)), [pair] + made + [ten[0]] * len(neighbours), scratch, after=(far,),
        cost=C_NEAR)
    early = [*early[:2], *neighbours, early[count - 1]]
    near, far = swap_sections(near, far)
    early = to_replicas(early)
    tables = (up_index, down_index, w_up, w_down)
    two = [shape((16, 2 * part), BF16)] * count
    scratch = [vmem((blocks, 16, BLOCK), F32), vmem((blocks, 16, BLOCK), F32), vmem((blocks, 16, BLOCK), BF16)]
    far_out, *late = call(
        body(near_phase, count, per), tables + (near, keep, far_keep), [smem] * 2 + [vmem] * 5, [long] + two, scratch,
        cost=C_NEAR_PHASE)
    near_out, *late = call(
        body(far_phase, count, per), tables + (far, keep, near_keep, *late), [smem] * 2 + [vmem] * (5 + count),
        [pair] + two, scratch, cost=C_FAR_PHASE, after=(early[1],))
    near, far = swap_sections(near_out, far_out)
    late = to_replicas(late)
    (grads,) = call(
        body(early_grads, count, per), tuple(early), [vmem] * count, [shape((2, per, BLOCK, BLOCK), F32)], [])
    stream = shape((1,) + values_in.shape[1:], BF16)
    grad = shape((1, per, BLOCK, BLOCK), BF16)
    return tuple(call(
        body(finish, count, per, scale), (far, near, grads, *early, *late), [vmem] * (3 + 2 * count),
        [stream, stream, stream, stream, grad, grad], [vmem((2, 16, width), BF16)]))


def solution(mesh):
    layer = P("section", None, None, None)
    table = P("section", None)
    stream = P("section", "dp", None)
    saved = P("section", None, "dp", None)
    return jax.shard_map(
        on_device,
        mesh=mesh,
        in_specs=(layer, table, layer, table, table) + (stream,) * 4 + (saved,) * 5,
        out_specs=(stream,) * 4 + (P("section", "dp", None, None),) * 2,
        check_vma=False,
    )
```

```python
import jax
import jax.numpy as jnp
from jax import lax
from jax.experimental import pallas as pl
from jax.experimental.pallas import tpu as pltpu
from jax.sharding import PartitionSpec as P

BLOCK = 128
F32 = jnp.float32
BF16 = jnp.bfloat16
LIMIT = 40 * 1024 * 1024
WORK = 10 ** 10
LIGHT = 10 ** 4
PAD = BLOCK
C_STREAMS = LIGHT
C_NEAR_PHASE = 5 * 10 ** 8
C_FAR_PHASE = LIGHT


def partner(me, step, count):
    if count & (count - 1) == 0:
        return me ^ step
    return lax.rem(me + step, count)


def swap_route(step, count):
    if count & (count - 1) == 0:
        return [(i, i ^ step) for i in range(count)]
    return [(i, (i + step) % count) for i in range(count)]


def swap_sections(near, far):
    count = lax.axis_size("section")
    far = lax.ppermute(far, "section", [(i, (i + 2 * (i % 2) - 1) % count) for i in range(count)])
    near = lax.ppermute(near, "section", [(i, i ^ 1) for i in range(count)])
    return near, far


def times(rows, weight):
    return lax.dot_general(rows, weight, (((1,), (0,)), ((), ())), preferred_element_type=F32)


def times_transposed(rows, weight):
    return lax.dot_general(rows, weight, (((1,), (1,)), ((), ())), preferred_element_type=F32)


def outer(xs, es):
    return lax.dot_general(jnp.concatenate(xs, 0), jnp.concatenate(es, 0), (((0,), (0,)), ((), ())),
                           preferred_element_type=F32)


def sigmoid(z):
    return 1.0 / (1.0 + jnp.exp(-z))


def slope_of(z, s):
    return s * (1.0 + z * (1.0 - s))


def lanes(block):
    if isinstance(block, int):
        return pl.ds(block * BLOCK, BLOCK)
    return pl.ds(pl.multiple_of(block * BLOCK, BLOCK), BLOCK)


def stack(parts):
    return jnp.concatenate([part.astype(F32) for part in parts], 0)


def send_order(me, count, per):
    for step in range(count):
        base = partner(me, step, count) * per
        for place in range(per):
            yield step, place, base + place


def odd_section():
    return lax.rem(lax.axis_index("section"), 2)


def take_in(near, far, packs):
    odd = odd_section()
    packs[1 - odd] = near[...]
    packs[odd] = far[:, :packs.shape[2]]


def open_launch(token):
    token[...] = jnp.zeros(token.shape, F32)


def first_rows(count, per, up_idx, down_idx, order, w_up, w_down, g_ref, a_ref, back, second, second_tan, second_grad,
               keep, pushes, *refs):
    sends, (pulled, hidden) = refs[:count], refs[count:]
    blocks = count * per
    me = lax.axis_index("dp")
    for b in range(blocks):
        pulled[b] = jnp.zeros(pulled.shape[1:], F32)
    m0 = order[0, 0]
    m1 = order[0, 1]
    for step, place, i in send_order(me, count, per):
        at = lanes(i)
        c = stack([g_ref[0, :, at], a_ref[0, :, at], second_grad[0, m0, :, at], second_grad[0, m1, :, at]]).astype(BF16)
        sends[step][8, :, lanes(place)] = c[0:16]
        sends[step][9, :, lanes(place)] = c[16:32]
        target = down_idx[0, i]
        pulled[target] = pulled[target] + times_transposed(c, w_down[0, i])
    for step, place, j in send_order(me, count, per):
        u = up_idx[0, j]
        at = lanes(u)
        x = stack([back[0, m0, :, at], second[0, m0, :, at], second_tan[0, m0, :, at],
                   second_tan[0, m1, :, at], back[0, m1, :, at], second[0, m1, :, at]]).astype(BF16)
        out = sends[step]
        here = lanes(place)
        for group in range(3):
            out[group, :, here] = x[16 * group:16 * group + 16]
        z = times(x, w_up[0, j])
        zb0, za0, ta0, ta1, zb1, za1 = (z[8 * k:8 * k + 8] for k in range(6))
        pg, pa, ga0, ga1 = (pulled[j, 8 * k:8 * k + 8] for k in range(4))
        sb0, sa0, sb1, sa1 = sigmoid(zb0), sigmoid(za0), sigmoid(zb1), sigmoid(za1)
        slope_a0 = slope_of(za0, sa0)
        slope_a1 = slope_of(za1, sa1)
        curve_a0 = sa0 * (1.0 - sa0) * (2.0 + za0 * (1.0 - 2.0 * sa0))
        curve_a1 = sa1 * (1.0 - sa1) * (2.0 + za1 * (1.0 - 2.0 * sa1))
        push = slope_a0 * pa + curve_a0 * ga0 * ta0
        e = jnp.concatenate([slope_of(zb0, sb0) * pg, push], 0).astype(BF16)
        out[3, :, here] = e
        out[4, :, here] = jnp.concatenate([slope_a0 * ga0, slope_a1 * ga1], 0).astype(BF16)
        hidden[j] = jnp.concatenate(
            [zb0 * sb0, za0 * sa0, slope_a0 * ta0, slope_a1 * ta1, zb1 * sb1, za1 * sa1], 0).astype(BF16)
        keep[j] = jnp.concatenate([slope_of(zb1, sb1), slope_a1, curve_a1 * ga1 * ta1], 0)
        pushes[:, lanes(j)] = e
    for step, place, i in send_order(me, count, per):
        y = hidden[down_idx[0, i]]
        for group in range(3):
            sends[step][5 + group, :, lanes(place)] = y[16 * group:16 * group + 16]


def forward_first(blocks, up_idx, down_idx, order, w_up, w_down, v_ref, t_ref, tan, pack, keep, hidden):
    m0 = order[0, 0]
    m1 = order[0, 1]
    for j in range(blocks):
        at = lanes(up_idx[0, j])
        x = stack([v_ref[0, :, at], t_ref[0, :, at], tan[0, m0, :, at], tan[0, m1, :, at]]).astype(BF16)
        z = times(x, w_up[0, j])
        zv, zt, z0, z1 = (z[8 * k:8 * k + 8] for k in range(4))
        hidden[j] = jnp.concatenate([zv * sigmoid(zv), slope_of(z0, sigmoid(z0)) * zt], 0).astype(BF16)
        keep[j] = slope_of(z1, sigmoid(z1))
    for i in range(blocks):
        at = lanes(i)
        moved = stack([v_ref[0, :, at], t_ref[0, :, at]]) + times(hidden[down_idx[0, i]], w_down[0, i])
        pack[:, at] = moved.astype(BF16)


def clear_pad(pack, blocks):
    if pack.shape[1] > blocks * BLOCK:
        pack[:, blocks * BLOCK:] = jnp.zeros((pack.shape[0], pack.shape[1] - blocks * BLOCK), BF16)


def back_streams(blocks, up_idx, w_up, g_ref, a_ref, pushes, pack, returned):
    for b in range(blocks):
        returned[b] = stack([g_ref[0, :, lanes(b)], a_ref[0, :, lanes(b)]])
    for j in range(blocks):
        u = up_idx[0, j]
        returned[u] = returned[u] + times_transposed(pushes[:, lanes(j)], w_up[0, j])
    for b in range(blocks):
        pack[:, lanes(b)] = returned[b].astype(BF16)


def first_streams(blocks, up_idx, down_idx, order, w_up, w_down, g_ref, a_ref, pushes, v_ref, t_ref, tan,
                  near, far, keep, packs, returned, hidden):
    odd = odd_section()
    clear_pad(far, blocks)
    back_streams(blocks, up_idx, w_up, g_ref, a_ref, pushes, packs.at[1], returned)
    forward_first(blocks, up_idx, down_idx, order, w_up, w_down, v_ref, t_ref, tan, packs.at[0], keep, hidden)
    near[...] = packs[odd]
    far[:, :packs.shape[2]] = packs[1 - odd]


def back_second(count, per, up_idx, down_idx, w_up, w_down, rows, keep, pack, sends, pulled, returned):
    blocks = count * per
    me = lax.axis_index("dp")
    for b in range(blocks):
        pulled[b] = jnp.zeros(pulled.shape[1:], F32)
        returned[b] = rows[:, lanes(b)].astype(F32)
    for step, place, i in send_order(me, count, per):
        c = rows[:, lanes(i)]
        sends[step][1, :, lanes(place)] = c
        target = down_idx[0, i]
        pulled[target] = pulled[target] + times_transposed(c, w_down[0, i])
    for step, place, j in send_order(me, count, per):
        u = up_idx[0, j]
        slope_b, slope_a, push = (keep[j, 8 * k:8 * k + 8] for k in range(3))
        e = jnp.concatenate([slope_b * pulled[j, 0:8], slope_a * pulled[j, 8:16] + push], 0).astype(BF16)
        sends[step][0, :, lanes(place)] = e
        returned[u] = returned[u] + times_transposed(e, w_up[0, j])
    for b in range(blocks):
        pack[:, lanes(b)] = returned[b].astype(BF16)


def forward_second(blocks, up_idx, down_idx, w_up, w_down, rows, keep, pack, hidden):
    for j in range(blocks):
        z = times(rows[:, lanes(up_idx[0, j])], w_up[0, j])
        zv, zt = z[0:8], z[8:16]
        hidden[j] = jnp.concatenate([zv * sigmoid(zv), keep[j] * zt], 0).astype(BF16)
    for i in range(blocks):
        at = lanes(i)
        pack[:, at] = (rows[:, at].astype(F32) + times(hidden[down_idx[0, i]], w_down[0, i])).astype(BF16)


def near_phase(count, per, up_idx, down_idx, w_up, w_down, near_in, keep, keep_tan, far, *refs):
    sends, (pulled, returned, hidden) = refs[:count], refs[count:]
    odd = odd_section()
    clear_pad(far, count * per)

    @pl.when(odd == 0)
    def _():
        back_second(count, per, up_idx, down_idx, w_up, w_down, near_in, keep, far, sends, pulled, returned)

    @pl.when(odd == 1)
    def _():
        forward_second(count * per, up_idx, down_idx, w_up, w_down, near_in, keep_tan, far, hidden)


def far_phase(count, per, up_idx, down_idx, w_up, w_down, far_in, keep, keep_tan, *refs):
    done, near, refs = refs[:count], refs[count], refs[count + 1:]
    sends, (pulled, returned, hidden) = refs[:count], refs[count:]
    odd = odd_section()

    @pl.when(odd == 0)
    def _():
        for source, target in zip(done, sends):
            target[...] = source[...]
        forward_second(count * per, up_idx, down_idx, w_up, w_down, far_in, keep_tan, near, hidden)

    @pl.when(odd == 1)
    def _():
        back_second(count, per, up_idx, down_idx, w_up, w_down, far_in, keep, near, sends, pulled, returned)


def early_grads(count, per, *refs):
    early, grads = refs[:count], refs[count]
    for place in range(per):
        at = lanes(place)
        for out, left, right in ((0, 0, 3), (1, 5, 8)):
            xs = [early[source][left + k, :, at] for source in range(count) for k in range(2)]
            es = [early[source][right + k, :, at] for source in range(count) for k in range(2)]
            grads[out, place] = outer(xs, es)


def finish(count, per, scale, far, near, grads, *rest):
    early, late = rest[:count], rest[count:2 * count]
    values, score, tangent, adjoint, grad_up, grad_down, came = rest[2 * count:]
    take_in(near, far, came)
    moved = came[0].astype(F32)
    values[0] = moved[0:8].astype(BF16)
    tangent[0] = moved[8:16].astype(BF16)
    moved = came[1].astype(F32)
    score[0] = moved[0:8].astype(BF16)
    adjoint[0] = moved[8:16].astype(BF16)
    for place in range(per):
        at = lanes(place)
        for k, (out, group) in enumerate(((grad_up, 2), (grad_down, 7))):
            xs = [early[source][group, :, at] for source in range(count)]
            es = [late[source][k, :, at] for source in range(count)]
            out[0, place] = ((grads[k, place] + outer(xs, es)) * scale).astype(BF16)


def call(body, operands, spaces, outs, scratch, after=(), cost=LIGHT):
    taken = len(operands)

    def kernel(*refs):
        body(*refs[:taken], *refs[taken + len(after):])

    return pl.pallas_call(
        kernel,
        out_shape=outs,
        in_specs=[pl.BlockSpec(memory_space=space) for space in spaces] + [pl.BlockSpec(memory_space=pl.ANY)] * len(after),
        out_specs=[pl.BlockSpec(memory_space=pltpu.VMEM)] * len(outs),
        scratch_shapes=scratch,
        compiler_params=pltpu.CompilerParams(vmem_limit_bytes=LIMIT),
        cost_estimate=pl.CostEstimate(flops=cost, bytes_accessed=cost // 100, transcendentals=0),
    )(*operands, *after)


def on_device(w_up, up_index, w_down, down_index, tick_order, values_in, score_grad_in, tangent_in, state_adjoint_in,
              saved_back, saved_tan, saved_second, saved_second_tan, saved_second_grad):
    count = lax.axis_size("dp")
    blocks = w_up.shape[1]
    per = blocks // count
    width = values_in.shape[2]
    part = per * BLOCK
    scale = 1.0 / (values_in.shape[1] * count)
    shape = jax.ShapeDtypeStruct
    pair = shape((16, width), BF16)
    vmem, smem = pltpu.VMEM, pltpu.SMEM

    def body(f, *args):
        def kernel(*refs):
            f(*args, *refs)
        return kernel

    def to_replicas(parts):
        steps = [count - 1] + list(range(1, count - 1))
        return [parts[0]] + [lax.ppermute(parts[step], "dp", swap_route(step, count)) for step in steps]

    rows = (score_grad_in, state_adjoint_in, saved_back, saved_second, saved_second_tan, saved_second_grad)
    ten = shape((10, 16, part), BF16)
    (token,) = call(open_launch, (), [], [shape((8, BLOCK), F32)], [], cost=WORK)
    tables = (up_index, down_index, tick_order, w_up, w_down)
    keep, pushes, *early = call(
        body(first_rows, count, per), tables + rows, [smem] * 3 + [vmem] * 8,
        [shape((blocks, 24, BLOCK), F32), pair] + [ten] * count,
        [vmem((blocks, 32, BLOCK), F32), vmem((blocks, 48, BLOCK), BF16)],
        after=(token,), cost=WORK)
    taken = tables + (score_grad_in, state_adjoint_in, pushes, values_in, tangent_in, saved_tan)
    long = shape((16, width + PAD), BF16)
    near, far, keep_tan = call(
        body(first_streams, blocks), taken, [smem] * 3 + [vmem] * 8, [pair, long, shape((blocks, 8, BLOCK), F32)],
        [vmem((2, 16, width), BF16), vmem((blocks, 16, BLOCK), F32), vmem((blocks, 16, BLOCK), BF16)], cost=C_STREAMS)
    near, far = swap_sections(near, far)
    early = to_replicas(early)
    tables = (up_index, down_index, w_up, w_down)
    two = [shape((2, 16, part), BF16)] * count
    scratch = [vmem((blocks, 16, BLOCK), F32), vmem((blocks, 16, BLOCK), F32), vmem((blocks, 16, BLOCK), BF16)]
    far_out, *late = call(
        body(near_phase, count, per), tables + (near, keep, keep_tan), [smem] * 2 + [vmem] * 5, [long] + two, scratch,
        cost=C_NEAR_PHASE)
    near_out, *late = call(
        body(far_phase, count, per), tables + (far, keep, keep_tan, *late), [smem] * 2 + [vmem] * (5 + count),
        [pair] + two, scratch, cost=C_FAR_PHASE)
    near, far = swap_sections(near_out, far_out)
    late = to_replicas(late)
    (grads,) = call(
        body(early_grads, count, per), tuple(early), [vmem] * count, [shape((2, per, BLOCK, BLOCK), F32)], [])
    stream = shape((1,) + values_in.shape[1:], BF16)
    grad = shape((1, per, BLOCK, BLOCK), BF16)
    return tuple(call(
        body(finish, count, per, scale), (far, near, grads, *early, *late), [vmem] * (3 + 2 * count),
        [stream, stream, stream, stream, grad, grad], [vmem((2, 16, width), BF16)]))


def solution(mesh):
    layer = P("section", None, None, None)
    table = P("section", None)
    stream = P("section", "dp", None)
    saved = P("section", None, "dp", None)
    return jax.shard_map(
        on_device,
        mesh=mesh,
        in_specs=(layer, table, layer, table, table) + (stream,) * 4 + (saved,) * 5,
        out_specs=(stream,) * 4 + (P("section", "dp", None, None),) * 2,
        check_vma=False,
    )
```

```python
import jax
import jax.numpy as jnp
from jax import lax
from jax.experimental import pallas as pl
from jax.experimental.pallas import tpu as pltpu
from jax.sharding import PartitionSpec as P

BLOCK = 128
F32 = jnp.float32
BF16 = jnp.bfloat16
LIMIT = 40 * 1024 * 1024
WORK = 10 ** 10
LIGHT = 10 ** 4
PAD = BLOCK
C_STREAMS = LIGHT
C_NEAR_PHASE = LIGHT
C_FAR_PHASE = LIGHT


def partner(me, step, count):
    if count & (count - 1) == 0:
        return me ^ step
    return lax.rem(me + step, count)


def swap_route(step, count):
    if count & (count - 1) == 0:
        return [(i, i ^ step) for i in range(count)]
    return [(i, (i + step) % count) for i in range(count)]


def swap_sections(near, far):
    count = lax.axis_size("section")
    far = lax.ppermute(far, "section", [(i, (i + 2 * (i % 2) - 1) % count) for i in range(count)])
    near = lax.ppermute(near, "section", [(i, i ^ 1) for i in range(count)])
    return near, far


def times(rows, weight):
    return lax.dot_general(rows, weight, (((1,), (0,)), ((), ())), preferred_element_type=F32)


def times_transposed(rows, weight):
    return lax.dot_general(rows, weight, (((1,), (1,)), ((), ())), preferred_element_type=F32)


def outer(xs, es):
    return lax.dot_general(jnp.concatenate(xs, 0), jnp.concatenate(es, 0), (((0,), (0,)), ((), ())),
                           preferred_element_type=F32)


def sigmoid(z):
    return 1.0 / (1.0 + jnp.exp(-z))


def slope_of(z, s):
    return s * (1.0 + z * (1.0 - s))


def lanes(block):
    if isinstance(block, int):
        return pl.ds(block * BLOCK, BLOCK)
    return pl.ds(pl.multiple_of(block * BLOCK, BLOCK), BLOCK)


def stack(parts):
    return jnp.concatenate([part.astype(F32) for part in parts], 0)


def send_order(me, count, per):
    for step in range(count):
        base = partner(me, step, count) * per
        for place in range(per):
            yield step, place, base + place


def odd_section():
    return lax.rem(lax.axis_index("section"), 2)


def take_in(near, far, packs):
    odd = odd_section()
    packs[1 - odd] = near[...]
    packs[odd] = far[:, :packs.shape[2]]


def open_launch(token):
    token[...] = jnp.zeros(token.shape, F32)


def first_rows(count, per, up_idx, down_idx, order, w_up, w_down, g_ref, a_ref, back, second, second_tan, second_grad,
               keep, pushes, *refs):
    sends, (pulled, hidden) = refs[:count], refs[count:]
    blocks = count * per
    me = lax.axis_index("dp")
    for b in range(blocks):
        pulled[b] = jnp.zeros(pulled.shape[1:], F32)
    m0 = order[0, 0]
    m1 = order[0, 1]
    for step, place, i in send_order(me, count, per):
        at = lanes(i)
        c = stack([g_ref[0, :, at], a_ref[0, :, at], second_grad[0, m0, :, at], second_grad[0, m1, :, at]]).astype(BF16)
        sends[step][8, :, lanes(place)] = c[0:16]
        sends[step][9, :, lanes(place)] = c[16:32]
        target = down_idx[0, i]
        pulled[target] = pulled[target] + times_transposed(c, w_down[0, i])
    for step, place, j in send_order(me, count, per):
        u = up_idx[0, j]
        at = lanes(u)
        x = stack([back[0, m0, :, at], second[0, m0, :, at], second_tan[0, m0, :, at],
                   second_tan[0, m1, :, at], back[0, m1, :, at], second[0, m1, :, at]]).astype(BF16)
        out = sends[step]
        here = lanes(place)
        for group in range(3):
            out[group, :, here] = x[16 * group:16 * group + 16]
        z = times(x, w_up[0, j])
        zb0, za0, ta0, ta1, zb1, za1 = (z[8 * k:8 * k + 8] for k in range(6))
        pg, pa, ga0, ga1 = (pulled[j, 8 * k:8 * k + 8] for k in range(4))
        sb0, sa0, sb1, sa1 = sigmoid(zb0), sigmoid(za0), sigmoid(zb1), sigmoid(za1)
        slope_a0 = slope_of(za0, sa0)
        slope_a1 = slope_of(za1, sa1)
        curve_a0 = sa0 * (1.0 - sa0) * (2.0 + za0 * (1.0 - 2.0 * sa0))
        curve_a1 = sa1 * (1.0 - sa1) * (2.0 + za1 * (1.0 - 2.0 * sa1))
        push = slope_a0 * pa + curve_a0 * ga0 * ta0
        e = jnp.concatenate([slope_of(zb0, sb0) * pg, push], 0).astype(BF16)
        out[3, :, here] = e
        out[4, :, here] = jnp.concatenate([slope_a0 * ga0, slope_a1 * ga1], 0).astype(BF16)
        hidden[j] = jnp.concatenate(
            [zb0 * sb0, za0 * sa0, slope_a0 * ta0, slope_a1 * ta1, zb1 * sb1, za1 * sa1], 0).astype(BF16)
        keep[j] = jnp.concatenate([slope_of(zb1, sb1), slope_a1, curve_a1 * ga1 * ta1], 0)
        pushes[:, lanes(j)] = e
    for step, place, i in send_order(me, count, per):
        y = hidden[down_idx[0, i]]
        for group in range(3):
            sends[step][5 + group, :, lanes(place)] = y[16 * group:16 * group + 16]


def forward_first(blocks, up_idx, down_idx, order, w_up, w_down, v_ref, t_ref, tan, pack, keep, hidden):
    m0 = order[0, 0]
    m1 = order[0, 1]
    for j in range(blocks):
        at = lanes(up_idx[0, j])
        x = stack([v_ref[0, :, at], t_ref[0, :, at], tan[0, m0, :, at], tan[0, m1, :, at]]).astype(BF16)
        z = times(x, w_up[0, j])
        zv, zt, z0, z1 = (z[8 * k:8 * k + 8] for k in range(4))
        hidden[j] = jnp.concatenate([zv * sigmoid(zv), slope_of(z0, sigmoid(z0)) * zt], 0).astype(BF16)
        keep[j] = slope_of(z1, sigmoid(z1))
    for i in range(blocks):
        at = lanes(i)
        moved = stack([v_ref[0, :, at], t_ref[0, :, at]]) + times(hidden[down_idx[0, i]], w_down[0, i])
        pack[:, at] = moved.astype(BF16)


def clear_pad(pack, blocks):
    if pack.shape[1] > blocks * BLOCK:
        pack[:, blocks * BLOCK:] = jnp.zeros((pack.shape[0], pack.shape[1] - blocks * BLOCK), BF16)


def back_streams(blocks, up_idx, w_up, g_ref, a_ref, pushes, pack, returned):
    for b in range(blocks):
        returned[b] = stack([g_ref[0, :, lanes(b)], a_ref[0, :, lanes(b)]])
    for j in range(blocks):
        u = up_idx[0, j]
        returned[u] = returned[u] + times_transposed(pushes[:, lanes(j)], w_up[0, j])
    for b in range(blocks):
        pack[:, lanes(b)] = returned[b].astype(BF16)


def first_streams(blocks, up_idx, down_idx, order, w_up, w_down, g_ref, a_ref, pushes, v_ref, t_ref, tan,
                  near, far, keep, packs, returned, hidden):
    odd = odd_section()
    clear_pad(far, blocks)
    back_streams(blocks, up_idx, w_up, g_ref, a_ref, pushes, packs.at[1], returned)
    forward_first(blocks, up_idx, down_idx, order, w_up, w_down, v_ref, t_ref, tan, packs.at[0], keep, hidden)
    near[...] = packs[odd]
    far[:, :packs.shape[2]] = packs[1 - odd]


def back_second(count, per, up_idx, down_idx, w_up, w_down, rows, keep, pack, sends, pulled, returned):
    blocks = count * per
    me = lax.axis_index("dp")
    for b in range(blocks):
        pulled[b] = jnp.zeros(pulled.shape[1:], F32)
        returned[b] = rows[:, lanes(b)].astype(F32)
    for step, place, i in send_order(me, count, per):
        c = rows[:, lanes(i)]
        sends[step][1, :, lanes(place)] = c
        target = down_idx[0, i]
        pulled[target] = pulled[target] + times_transposed(c, w_down[0, i])
    for step, place, j in send_order(me, count, per):
        u = up_idx[0, j]
        slope_b, slope_a, push = (keep[j, 8 * k:8 * k + 8] for k in range(3))
        e = jnp.concatenate([slope_b * pulled[j, 0:8], slope_a * pulled[j, 8:16] + push], 0).astype(BF16)
        sends[step][0, :, lanes(place)] = e
        returned[u] = returned[u] + times_transposed(e, w_up[0, j])
    for b in range(blocks):
        pack[:, lanes(b)] = returned[b].astype(BF16)


def forward_second(blocks, up_idx, down_idx, w_up, w_down, rows, keep, pack, hidden):
    for j in range(blocks):
        z = times(rows[:, lanes(up_idx[0, j])], w_up[0, j])
        zv, zt = z[0:8], z[8:16]
        hidden[j] = jnp.concatenate([zv * sigmoid(zv), keep[j] * zt], 0).astype(BF16)
    for i in range(blocks):
        at = lanes(i)
        pack[:, at] = (rows[:, at].astype(F32) + times(hidden[down_idx[0, i]], w_down[0, i])).astype(BF16)


def near_phase(count, per, up_idx, down_idx, w_up, w_down, near_in, keep, keep_tan, far, *refs):
    sends, (pulled, returned, hidden) = refs[:count], refs[count:]
    odd = odd_section()
    clear_pad(far, count * per)

    @pl.when(odd == 0)
    def _():
        back_second(count, per, up_idx, down_idx, w_up, w_down, near_in, keep, far, sends, pulled, returned)

    @pl.when(odd == 1)
    def _():
        forward_second(count * per, up_idx, down_idx, w_up, w_down, near_in, keep_tan, far, hidden)


def far_phase(count, per, up_idx, down_idx, w_up, w_down, far_in, keep, keep_tan, *refs):
    done, near, refs = refs[:count], refs[count], refs[count + 1:]
    sends, (pulled, returned, hidden) = refs[:count], refs[count:]
    odd = odd_section()

    @pl.when(odd == 0)
    def _():
        for source, target in zip(done, sends):
            target[...] = source[...]
        forward_second(count * per, up_idx, down_idx, w_up, w_down, far_in, keep_tan, near, hidden)

    @pl.when(odd == 1)
    def _():
        back_second(count, per, up_idx, down_idx, w_up, w_down, far_in, keep, near, sends, pulled, returned)


def early_grads(count, per, *refs):
    early, grads = refs[:count], refs[count]
    for place in range(per):
        at = lanes(place)
        for out, left, right in ((0, 0, 3), (1, 5, 8)):
            xs = [early[source][left + k, :, at] for source in range(count) for k in range(2)]
            es = [early[source][right + k, :, at] for source in range(count) for k in range(2)]
            grads[out, place] = outer(xs, es)


def finish(count, per, scale, far, near, grads, *rest):
    early, late = rest[:count], rest[count:2 * count]
    values, score, tangent, adjoint, grad_up, grad_down, came = rest[2 * count:]
    take_in(near, far, came)
    moved = came[0].astype(F32)
    values[0] = moved[0:8].astype(BF16)
    tangent[0] = moved[8:16].astype(BF16)
    moved = came[1].astype(F32)
    score[0] = moved[0:8].astype(BF16)
    adjoint[0] = moved[8:16].astype(BF16)
    for place in range(per):
        at = lanes(place)
        for k, (out, group) in enumerate(((grad_up, 2), (grad_down, 7))):
            xs = [early[source][group, :, at] for source in range(count)]
            es = [late[source][k, :, at] for source in range(count)]
            out[0, place] = ((grads[k, place] + outer(xs, es)) * scale).astype(BF16)


def call(body, operands, spaces, outs, scratch, after=(), cost=LIGHT):
    taken = len(operands)

    def kernel(*refs):
        body(*refs[:taken], *refs[taken + len(after):])

    return pl.pallas_call(
        kernel,
        out_shape=outs,
        in_specs=[pl.BlockSpec(memory_space=space) for space in spaces] + [pl.BlockSpec(memory_space=pl.ANY)] * len(after),
        out_specs=[pl.BlockSpec(memory_space=pltpu.VMEM)] * len(outs),
        scratch_shapes=scratch,
        compiler_params=pltpu.CompilerParams(vmem_limit_bytes=LIMIT),
        cost_estimate=pl.CostEstimate(flops=cost, bytes_accessed=cost // 100, transcendentals=0),
    )(*operands, *after)


def on_device(w_up, up_index, w_down, down_index, tick_order, values_in, score_grad_in, tangent_in, state_adjoint_in,
              saved_back, saved_tan, saved_second, saved_second_tan, saved_second_grad):
    count = lax.axis_size("dp")
    blocks = w_up.shape[1]
    per = blocks // count
    width = values_in.shape[2]
    part = per * BLOCK
    scale = 1.0 / (values_in.shape[1] * count)
    shape = jax.ShapeDtypeStruct
    pair = shape((16, width), BF16)
    vmem, smem = pltpu.VMEM, pltpu.SMEM

    def body(f, *args):
        def kernel(*refs):
            f(*args, *refs)
        return kernel

    def to_replicas(parts):
        steps = [count - 1] + list(range(1, count - 1))
        return [parts[0]] + [lax.ppermute(parts[step], "dp", swap_route(step, count)) for step in steps]

    rows = (score_grad_in, state_adjoint_in, saved_back, saved_second, saved_second_tan, saved_second_grad)
    ten = shape((10, 16, part), BF16)
    (token,) = call(open_launch, (), [], [shape((8, BLOCK), F32)], [], cost=WORK)
    tables = (up_index, down_index, tick_order, w_up, w_down)
    keep, pushes, *early = call(
        body(first_rows, count, per), tables + rows, [smem] * 3 + [vmem] * 8,
        [shape((blocks, 24, BLOCK), F32), pair] + [ten] * count,
        [vmem((blocks, 32, BLOCK), F32), vmem((blocks, 48, BLOCK), BF16)],
        after=(token,), cost=WORK)
    taken = tables + (score_grad_in, state_adjoint_in, pushes, values_in, tangent_in, saved_tan)
    long = shape((16, width + PAD), BF16)
    near, far, keep_tan = call(
        body(first_streams, blocks), taken, [smem] * 3 + [vmem] * 8, [pair, long, shape((blocks, 8, BLOCK), F32)],
        [vmem((2, 16, width), BF16), vmem((blocks, 16, BLOCK), F32), vmem((blocks, 16, BLOCK), BF16)], cost=C_STREAMS)
    near, far = swap_sections(near, far)
    early = to_replicas(early)
    tables = (up_index, down_index, w_up, w_down)
    two = [shape((2, 16, part), BF16)] * count
    scratch = [vmem((blocks, 16, BLOCK), F32), vmem((blocks, 16, BLOCK), F32), vmem((blocks, 16, BLOCK), BF16)]
    far_out, *late = call(
        body(near_phase, count, per), tables + (near, keep, keep_tan), [smem] * 2 + [vmem] * 5, [long] + two, scratch,
        cost=C_NEAR_PHASE)
    near_out, *late = call(
        body(far_phase, count, per), tables + (far, keep, keep_tan, *late), [smem] * 2 + [vmem] * (5 + count),
        [pair] + two, scratch, cost=C_FAR_PHASE)
    near, far = swap_sections(near_out, far_out)
    late = to_replicas(late)
    (grads,) = call(
        body(early_grads, count, per), tuple(early), [vmem] * count, [shape((2, per, BLOCK, BLOCK), F32)], [])
    stream = shape((1,) + values_in.shape[1:], BF16)
    grad = shape((1, per, BLOCK, BLOCK), BF16)
    return tuple(call(
        body(finish, count, per, scale), (far, near, grads, *early, *late), [vmem] * (3 + 2 * count),
        [stream, stream, stream, stream, grad, grad], [vmem((2, 16, width), BF16)]))


def solution(mesh):
    layer = P("section", None, None, None)
    table = P("section", None)
    stream = P("section", "dp", None)
    saved = P("section", None, "dp", None)
    return jax.shard_map(
        on_device,
        mesh=mesh,
        in_specs=(layer, table, layer, table, table) + (stream,) * 4 + (saved,) * 5,
        out_specs=(stream,) * 4 + (P("section", "dp", None, None),) * 2,
        check_vma=False,
    )
```

```python
import jax
import jax.numpy as jnp
from jax import lax
from jax.experimental import pallas as pl
from jax.experimental.pallas import tpu as pltpu
from jax.sharding import PartitionSpec as P

BLOCK = 128
F32 = jnp.float32
BF16 = jnp.bfloat16
LIMIT = 40 * 1024 * 1024
WORK = 10 ** 10
LIGHT = 10 ** 4
PAD = BLOCK
C_STREAMS = LIGHT
C_NEAR_PHASE = LIGHT
C_FAR_PHASE = LIGHT


def partner(me, step, count):
    if count & (count - 1) == 0:
        return me ^ step
    return lax.rem(me + step, count)


def swap_route(step, count):
    if count & (count - 1) == 0:
        return [(i, i ^ step) for i in range(count)]
    return [(i, (i + step) % count) for i in range(count)]


def swap_sections(near, far):
    count = lax.axis_size("section")
    far = lax.ppermute(far, "section", [(i, (i + 2 * (i % 2) - 1) % count) for i in range(count)])
    near = lax.ppermute(near, "section", [(i, i ^ 1) for i in range(count)])
    return near, far


def times(rows, weight):
    return lax.dot_general(rows, weight, (((1,), (0,)), ((), ())), preferred_element_type=F32)


def times_transposed(rows, weight):
    return lax.dot_general(rows, weight, (((1,), (1,)), ((), ())), preferred_element_type=F32)


def outer(xs, es):
    return lax.dot_general(jnp.concatenate(xs, 0), jnp.concatenate(es, 0), (((0,), (0,)), ((), ())),
                           preferred_element_type=F32)


def sigmoid(z):
    return 1.0 / (1.0 + jnp.exp(-z))


def slope_of(z, s):
    return s * (1.0 + z * (1.0 - s))


def lanes(block):
    if isinstance(block, int):
        return pl.ds(block * BLOCK, BLOCK)
    return pl.ds(pl.multiple_of(block * BLOCK, BLOCK), BLOCK)


def stack(parts):
    return jnp.concatenate([part.astype(F32) for part in parts], 0)


def send_order(me, count, per):
    for step in range(count):
        base = partner(me, step, count) * per
        for place in range(per):
            yield step, place, base + place


def odd_section():
    return lax.rem(lax.axis_index("section"), 2)


def take_in(near, far, packs):
    odd = odd_section()
    packs[1 - odd] = near[...]
    packs[odd] = far[:, :packs.shape[2]]


def open_launch(token):
    token[...] = jnp.zeros(token.shape, F32)


def first_rows(count, per, up_idx, down_idx, order, w_up, w_down, g_ref, a_ref, back, second, second_tan, second_grad,
               keep, pushes, *refs):
    sends, (pulled, hidden) = refs[:count], refs[count:]
    blocks = count * per
    me = lax.axis_index("dp")
    for b in range(blocks):
        pulled[b] = jnp.zeros(pulled.shape[1:], F32)
    m0 = order[0, 0]
    m1 = order[0, 1]
    for step, place, i in send_order(me, count, per):
        at = lanes(i)
        c = stack([g_ref[0, :, at], a_ref[0, :, at], second_grad[0, m0, :, at], second_grad[0, m1, :, at]]).astype(BF16)
        sends[step][8, :, lanes(place)] = c[0:16]
        sends[step][9, :, lanes(place)] = c[16:32]
        target = down_idx[0, i]
        pulled[target] = pulled[target] + times_transposed(c, w_down[0, i])
    for step, place, j in send_order(me, count, per):
        u = up_idx[0, j]
        at = lanes(u)
        x = stack([back[0, m0, :, at], second[0, m0, :, at], second_tan[0, m0, :, at],
                   second_tan[0, m1, :, at], back[0, m1, :, at], second[0, m1, :, at]]).astype(BF16)
        out = sends[step]
        here = lanes(place)
        for group in range(3):
            out[group, :, here] = x[16 * group:16 * group + 16]
        z = times(x, w_up[0, j])
        zb0, za0, ta0, ta1, zb1, za1 = (z[8 * k:8 * k + 8] for k in range(6))
        pg, pa, ga0, ga1 = (pulled[j, 8 * k:8 * k + 8] for k in range(4))
        sb0, sa0, sb1, sa1 = sigmoid(zb0), sigmoid(za0), sigmoid(zb1), sigmoid(za1)
        slope_a0 = slope_of(za0, sa0)
        slope_a1 = slope_of(za1, sa1)
        curve_a0 = sa0 * (1.0 - sa0) * (2.0 + za0 * (1.0 - 2.0 * sa0))
        curve_a1 = sa1 * (1.0 - sa1) * (2.0 + za1 * (1.0 - 2.0 * sa1))
        push = slope_a0 * pa + curve_a0 * ga0 * ta0
        e = jnp.concatenate([slope_of(zb0, sb0) * pg, push], 0).astype(BF16)
        out[3, :, here] = e
        out[4, :, here] = jnp.concatenate([slope_a0 * ga0, slope_a1 * ga1], 0).astype(BF16)
        hidden[j] = jnp.concatenate(
            [zb0 * sb0, za0 * sa0, slope_a0 * ta0, slope_a1 * ta1, zb1 * sb1, za1 * sa1], 0).astype(BF16)
        keep[j] = jnp.concatenate([slope_of(zb1, sb1), slope_a1, curve_a1 * ga1 * ta1], 0)
        pushes[:, lanes(j)] = e
    for step, place, i in send_order(me, count, per):
        y = hidden[down_idx[0, i]]
        for group in range(3):
            sends[step][5 + group, :, lanes(place)] = y[16 * group:16 * group + 16]


def forward_first(blocks, up_idx, down_idx, order, w_up, w_down, v_ref, t_ref, tan, pack, keep, hidden):
    m0 = order[0, 0]
    m1 = order[0, 1]
    for j in range(blocks):
        at = lanes(up_idx[0, j])
        x = stack([v_ref[0, :, at], t_ref[0, :, at], tan[0, m0, :, at], tan[0, m1, :, at]]).astype(BF16)
        z = times(x, w_up[0, j])
        zv, zt, z0, z1 = (z[8 * k:8 * k + 8] for k in range(4))
        hidden[j] = jnp.concatenate([zv * sigmoid(zv), slope_of(z0, sigmoid(z0)) * zt], 0).astype(BF16)
        keep[j] = slope_of(z1, sigmoid(z1))
    for i in range(blocks):
        at = lanes(i)
        moved = stack([v_ref[0, :, at], t_ref[0, :, at]]) + times(hidden[down_idx[0, i]], w_down[0, i])
        pack[:, at] = moved.astype(BF16)


def clear_pad(pack, blocks):
    if pack.shape[1] > blocks * BLOCK:
        pack[:, blocks * BLOCK:] = jnp.zeros((pack.shape[0], pack.shape[1] - blocks * BLOCK), BF16)


def back_streams(blocks, up_idx, w_up, g_ref, a_ref, pushes, pack, returned):
    for b in range(blocks):
        returned[b] = stack([g_ref[0, :, lanes(b)], a_ref[0, :, lanes(b)]])
    for j in range(blocks):
        u = up_idx[0, j]
        returned[u] = returned[u] + times_transposed(pushes[:, lanes(j)], w_up[0, j])
    for b in range(blocks):
        pack[:, lanes(b)] = returned[b].astype(BF16)


def first_streams(blocks, up_idx, down_idx, order, w_up, w_down, g_ref, a_ref, pushes, v_ref, t_ref, tan,
                  near, far, keep, packs, returned, hidden):
    odd = odd_section()
    clear_pad(far, blocks)
    back_streams(blocks, up_idx, w_up, g_ref, a_ref, pushes, packs.at[1], returned)
    forward_first(blocks, up_idx, down_idx, order, w_up, w_down, v_ref, t_ref, tan, packs.at[0], keep, hidden)
    near[...] = packs[odd]
    far[:, :packs.shape[2]] = packs[1 - odd]


def back_second(count, per, up_idx, down_idx, w_up, w_down, rows, keep, pack, sends, pulled, returned):
    blocks = count * per
    me = lax.axis_index("dp")
    for b in range(blocks):
        pulled[b] = jnp.zeros(pulled.shape[1:], F32)
        returned[b] = rows[:, lanes(b)].astype(F32)
    for step, place, i in send_order(me, count, per):
        c = rows[:, lanes(i)]
        sends[step][1, :, lanes(place)] = c
        target = down_idx[0, i]
        pulled[target] = pulled[target] + times_transposed(c, w_down[0, i])
    for step, place, j in send_order(me, count, per):
        u = up_idx[0, j]
        slope_b, slope_a, push = (keep[j, 8 * k:8 * k + 8] for k in range(3))
        e = jnp.concatenate([slope_b * pulled[j, 0:8], slope_a * pulled[j, 8:16] + push], 0).astype(BF16)
        sends[step][0, :, lanes(place)] = e
        returned[u] = returned[u] + times_transposed(e, w_up[0, j])
    for b in range(blocks):
        pack[:, lanes(b)] = returned[b].astype(BF16)


def forward_second(blocks, up_idx, down_idx, w_up, w_down, rows, keep, pack, hidden):
    for j in range(blocks):
        z = times(rows[:, lanes(up_idx[0, j])], w_up[0, j])
        zv, zt = z[0:8], z[8:16]
        hidden[j] = jnp.concatenate([zv * sigmoid(zv), keep[j] * zt], 0).astype(BF16)
    for i in range(blocks):
        at = lanes(i)
        pack[:, at] = (rows[:, at].astype(F32) + times(hidden[down_idx[0, i]], w_down[0, i])).astype(BF16)


def near_phase(count, per, up_idx, down_idx, w_up, w_down, near_in, keep, keep_tan, far, *refs):
    sends, (pulled, returned, hidden) = refs[:count], refs[count:]
    odd = odd_section()
    clear_pad(far, count * per)

    @pl.when(odd == 0)
    def _():
        back_second(count, per, up_idx, down_idx, w_up, w_down, near_in, keep, far, sends, pulled, returned)

    @pl.when(odd == 1)
    def _():
        forward_second(count * per, up_idx, down_idx, w_up, w_down, near_in, keep_tan, far, hidden)


def far_phase(count, per, up_idx, down_idx, w_up, w_down, far_in, keep, keep_tan, *refs):
    done, near, refs = refs[:count], refs[count], refs[count + 1:]
    sends, (pulled, returned, hidden) = refs[:count], refs[count:]
    odd = odd_section()

    @pl.when(odd == 0)
    def _():
        for source, target in zip(done, sends):
            target[...] = source[...]
        forward_second(count * per, up_idx, down_idx, w_up, w_down, far_in, keep_tan, near, hidden)

    @pl.when(odd == 1)
    def _():
        back_second(count, per, up_idx, down_idx, w_up, w_down, far_in, keep, near, sends, pulled, returned)


def early_grads(count, per, *refs):
    early, grads = refs[:count], refs[count]
    for place in range(per):
        at = lanes(place)
        for out, left, right in ((0, 0, 3), (1, 5, 8)):
            xs = [early[source][left + k, :, at] for source in range(count) for k in range(2)]
            es = [early[source][right + k, :, at] for source in range(count) for k in range(2)]
            grads[out, place] = outer(xs, es)


def finish(count, per, scale, far, near, grads, *rest):
    early, late = rest[:count], rest[count:2 * count]
    values, score, tangent, adjoint, grad_up, grad_down, came = rest[2 * count:]
    take_in(near, far, came)
    moved = came[0].astype(F32)
    values[0] = moved[0:8].astype(BF16)
    tangent[0] = moved[8:16].astype(BF16)
    moved = came[1].astype(F32)
    score[0] = moved[0:8].astype(BF16)
    adjoint[0] = moved[8:16].astype(BF16)
    for place in range(per):
        at = lanes(place)
        for k, (out, group) in enumerate(((grad_up, 2), (grad_down, 7))):
            xs = [early[source][group, :, at] for source in range(count)]
            es = [late[source][k, :, at] for source in range(count)]
            out[0, place] = ((grads[k, place] + outer(xs, es)) * scale).astype(BF16)


def call(body, operands, spaces, outs, scratch, after=(), cost=LIGHT):
    taken = len(operands)

    def kernel(*refs):
        body(*refs[:taken], *refs[taken + len(after):])

    return pl.pallas_call(
        kernel,
        out_shape=outs,
        in_specs=[pl.BlockSpec(memory_space=space) for space in spaces] + [pl.BlockSpec(memory_space=pl.ANY)] * len(after),
        out_specs=[pl.BlockSpec(memory_space=pltpu.VMEM)] * len(outs),
        scratch_shapes=scratch,
        compiler_params=pltpu.CompilerParams(vmem_limit_bytes=LIMIT),
        cost_estimate=pl.CostEstimate(flops=cost, bytes_accessed=cost // 100, transcendentals=0),
    )(*operands, *after)


def hand_on(*refs):
    half = len(refs) // 2
    for source, target in zip(refs[:half], refs[half:]):
        target[...] = source[...]


def held_until(there, arrays):
    shapes = [jax.ShapeDtypeStruct(x.shape, x.dtype) for x in arrays]
    return call(hand_on, tuple(arrays), [pltpu.VMEM] * len(arrays), shapes, [], after=(there,))


def on_device(w_up, up_index, w_down, down_index, tick_order, values_in, score_grad_in, tangent_in, state_adjoint_in,
              saved_back, saved_tan, saved_second, saved_second_tan, saved_second_grad):
    count = lax.axis_size("dp")
    blocks = w_up.shape[1]
    per = blocks // count
    width = values_in.shape[2]
    part = per * BLOCK
    scale = 1.0 / (values_in.shape[1] * count)
    shape = jax.ShapeDtypeStruct
    pair = shape((16, width), BF16)
    vmem, smem = pltpu.VMEM, pltpu.SMEM

    def body(f, *args):
        def kernel(*refs):
            f(*args, *refs)
        return kernel

    def to_replicas(parts):
        steps = [count - 1] + list(range(1, count - 1))
        return [parts[0]] + [lax.ppermute(parts[step], "dp", swap_route(step, count)) for step in steps]

    rows = (score_grad_in, state_adjoint_in, saved_back, saved_second, saved_second_tan, saved_second_grad)
    ten = shape((10, 16, part), BF16)
    (token,) = call(open_launch, (), [], [shape((8, BLOCK), F32)], [], cost=WORK)
    tables = (up_index, down_index, tick_order, w_up, w_down)
    keep, pushes, *early = call(
        body(first_rows, count, per), tables + rows, [smem] * 3 + [vmem] * 8,
        [shape((blocks, 24, BLOCK), F32), pair] + [ten] * count,
        [vmem((blocks, 32, BLOCK), F32), vmem((blocks, 48, BLOCK), BF16)],
        after=(token,), cost=WORK)
    taken = tables + (score_grad_in, state_adjoint_in, pushes, values_in, tangent_in, saved_tan)
    long = shape((16, width + PAD), BF16)
    near, far, keep_tan = call(
        body(first_streams, blocks), taken, [smem] * 3 + [vmem] * 8, [pair, long, shape((blocks, 8, BLOCK), F32)],
        [vmem((2, 16, width), BF16), vmem((blocks, 16, BLOCK), F32), vmem((blocks, 16, BLOCK), BF16)], cost=C_STREAMS)
    near, far = swap_sections(near, far)
    early = to_replicas(early)
    tables = (up_index, down_index, w_up, w_down)
    two = [shape((2, 16, part), BF16)] * count
    scratch = [vmem((blocks, 16, BLOCK), F32), vmem((blocks, 16, BLOCK), F32), vmem((blocks, 16, BLOCK), BF16)]
    far_out, *late = call(
        body(near_phase, count, per), tables + (near, keep, keep_tan), [smem] * 2 + [vmem] * 5, [long] + two, scratch,
        cost=C_NEAR_PHASE)
    near_out, *late = call(
        body(far_phase, count, per), tables + (far, keep, keep_tan, *late), [smem] * 2 + [vmem] * (5 + count),
        [pair] + two, scratch, cost=C_FAR_PHASE)
    near, far = swap_sections(near_out, far_out)
    late = to_replicas([late[0], *held_until(near, late[1:2]), *late[2:]])
    (grads,) = call(
        body(early_grads, count, per), tuple(early), [vmem] * count, [shape((2, per, BLOCK, BLOCK), F32)], [],
        after=(far,))
    stream = shape((1,) + values_in.shape[1:], BF16)
    grad = shape((1, per, BLOCK, BLOCK), BF16)
    return tuple(call(
        body(finish, count, per, scale), (far, near, grads, *early, *late), [vmem] * (3 + 2 * count),
        [stream, stream, stream, stream, grad, grad], [vmem((2, 16, width), BF16)]))


def solution(mesh):
    layer = P("section", None, None, None)
    table = P("section", None)
    stream = P("section", "dp", None)
    saved = P("section", None, "dp", None)
    return jax.shard_map(
        on_device,
        mesh=mesh,
        in_specs=(layer, table, layer, table, table) + (stream,) * 4 + (saved,) * 5,
        out_specs=(stream,) * 4 + (P("section", "dp", None, None),) * 2,
        check_vma=False,
    )
```

```python
import jax
import jax.numpy as jnp
from jax import lax
from jax.experimental import pallas as pl
from jax.experimental.pallas import tpu as pltpu
from jax.sharding import PartitionSpec as P

BLOCK = 128
F32 = jnp.float32
BF16 = jnp.bfloat16
LIMIT = 40 * 1024 * 1024
WORK = 10 ** 10
LIGHT = 10 ** 4
PAD = BLOCK
C_STREAMS = LIGHT
C_NEAR_PHASE = LIGHT
C_FAR_PHASE = LIGHT


def partner(me, step, count):
    if count & (count - 1) == 0:
        return me ^ step
    return lax.rem(me + step, count)


def swap_route(step, count):
    if count & (count - 1) == 0:
        return [(i, i ^ step) for i in range(count)]
    return [(i, (i + step) % count) for i in range(count)]


def swap_sections(near, far):
    count = lax.axis_size("section")
    far = lax.ppermute(far, "section", [(i, (i + 2 * (i % 2) - 1) % count) for i in range(count)])
    near = lax.ppermute(near, "section", [(i, i ^ 1) for i in range(count)])
    return near, far


def times(rows, weight):
    return lax.dot_general(rows, weight, (((1,), (0,)), ((), ())), preferred_element_type=F32)


def times_transposed(rows, weight):
    return lax.dot_general(rows, weight, (((1,), (1,)), ((), ())), preferred_element_type=F32)


def outer(xs, es):
    return lax.dot_general(jnp.concatenate(xs, 0), jnp.concatenate(es, 0), (((0,), (0,)), ((), ())),
                           preferred_element_type=F32)


def sigmoid(z):
    return 1.0 / (1.0 + jnp.exp(-z))


def slope_of(z, s):
    return s * (1.0 + z * (1.0 - s))


def lanes(block):
    if isinstance(block, int):
        return pl.ds(block * BLOCK, BLOCK)
    return pl.ds(pl.multiple_of(block * BLOCK, BLOCK), BLOCK)


def stack(parts):
    return jnp.concatenate([part.astype(F32) for part in parts], 0)


def send_order(me, count, per):
    for step in range(count):
        base = partner(me, step, count) * per
        for place in range(per):
            yield step, place, base + place


def odd_section():
    return lax.rem(lax.axis_index("section"), 2)


def take_in(near, far, packs):
    odd = odd_section()
    packs[1 - odd] = near[...]
    packs[odd] = far[:, :packs.shape[2]]


def open_launch(token):
    token[...] = jnp.zeros(token.shape, F32)


def first_rows(count, per, up_idx, down_idx, order, w_up, w_down, g_ref, a_ref, back, second, second_tan, second_grad,
               keep, pushes, *refs):
    sends, (pulled, hidden) = refs[:count], refs[count:]
    blocks = count * per
    me = lax.axis_index("dp")
    for b in range(blocks):
        pulled[b] = jnp.zeros(pulled.shape[1:], F32)
    m0 = order[0, 0]
    m1 = order[0, 1]
    for step, place, i in send_order(me, count, per):
        at = lanes(i)
        c = stack([g_ref[0, :, at], a_ref[0, :, at], second_grad[0, m0, :, at], second_grad[0, m1, :, at]]).astype(BF16)
        sends[step][8, :, lanes(place)] = c[0:16]
        sends[step][9, :, lanes(place)] = c[16:32]
        target = down_idx[0, i]
        pulled[target] = pulled[target] + times_transposed(c, w_down[0, i])
    for step, place, j in send_order(me, count, per):
        u = up_idx[0, j]
        at = lanes(u)
        x = stack([back[0, m0, :, at], second[0, m0, :, at], second_tan[0, m0, :, at],
                   second_tan[0, m1, :, at], back[0, m1, :, at], second[0, m1, :, at]]).astype(BF16)
        out = sends[step]
        here = lanes(place)
        for group in range(3):
            out[group, :, here] = x[16 * group:16 * group + 16]
        z = times(x, w_up[0, j])
        zb0, za0, ta0, ta1, zb1, za1 = (z[8 * k:8 * k + 8] for k in range(6))
        pg, pa, ga0, ga1 = (pulled[j, 8 * k:8 * k + 8] for k in range(4))
        sb0, sa0, sb1, sa1 = sigmoid(zb0), sigmoid(za0), sigmoid(zb1), sigmoid(za1)
        slope_a0 = slope_of(za0, sa0)
        slope_a1 = slope_of(za1, sa1)
        curve_a0 = sa0 * (1.0 - sa0) * (2.0 + za0 * (1.0 - 2.0 * sa0))
        curve_a1 = sa1 * (1.0 - sa1) * (2.0 + za1 * (1.0 - 2.0 * sa1))
        push = slope_a0 * pa + curve_a0 * ga0 * ta0
        e = jnp.concatenate([slope_of(zb0, sb0) * pg, push], 0).astype(BF16)
        out[3, :, here] = e
        out[4, :, here] = jnp.concatenate([slope_a0 * ga0, slope_a1 * ga1], 0).astype(BF16)
        hidden[j] = jnp.concatenate(
            [zb0 * sb0, za0 * sa0, slope_a0 * ta0, slope_a1 * ta1, zb1 * sb1, za1 * sa1], 0).astype(BF16)
        keep[j] = jnp.concatenate([slope_of(zb1, sb1), slope_a1, curve_a1 * ga1 * ta1], 0)
        pushes[:, lanes(j)] = e
    for step, place, i in send_order(me, count, per):
        y = hidden[down_idx[0, i]]
        for group in range(3):
            sends[step][5 + group, :, lanes(place)] = y[16 * group:16 * group + 16]


def forward_first(blocks, up_idx, down_idx, order, w_up, w_down, v_ref, t_ref, tan, pack, keep, hidden):
    m0 = order[0, 0]
    m1 = order[0, 1]
    for j in range(blocks):
        at = lanes(up_idx[0, j])
        x = stack([v_ref[0, :, at], t_ref[0, :, at], tan[0, m0, :, at], tan[0, m1, :, at]]).astype(BF16)
        z = times(x, w_up[0, j])
        zv, zt, z0, z1 = (z[8 * k:8 * k + 8] for k in range(4))
        hidden[j] = jnp.concatenate([zv * sigmoid(zv), slope_of(z0, sigmoid(z0)) * zt], 0).astype(BF16)
        keep[j] = slope_of(z1, sigmoid(z1))
    for i in range(blocks):
        at = lanes(i)
        moved = stack([v_ref[0, :, at], t_ref[0, :, at]]) + times(hidden[down_idx[0, i]], w_down[0, i])
        pack[:, at] = moved.astype(BF16)


def clear_pad(pack, blocks):
    if pack.shape[1] > blocks * BLOCK:
        pack[:, blocks * BLOCK:] = jnp.zeros((pack.shape[0], pack.shape[1] - blocks * BLOCK), BF16)


def back_streams(blocks, up_idx, w_up, g_ref, a_ref, pushes, pack, returned):
    for b in range(blocks):
        returned[b] = stack([g_ref[0, :, lanes(b)], a_ref[0, :, lanes(b)]])
    for j in range(blocks):
        u = up_idx[0, j]
        returned[u] = returned[u] + times_transposed(pushes[:, lanes(j)], w_up[0, j])
    for b in range(blocks):
        pack[:, lanes(b)] = returned[b].astype(BF16)


def first_streams(blocks, up_idx, down_idx, order, w_up, w_down, g_ref, a_ref, pushes, v_ref, t_ref, tan,
                  near, far, keep, packs, returned, hidden):
    odd = odd_section()
    clear_pad(far, blocks)
    back_streams(blocks, up_idx, w_up, g_ref, a_ref, pushes, packs.at[1], returned)
    forward_first(blocks, up_idx, down_idx, order, w_up, w_down, v_ref, t_ref, tan, packs.at[0], keep, hidden)
    near[...] = packs[odd]
    far[:, :packs.shape[2]] = packs[1 - odd]


def back_second(count, per, up_idx, down_idx, w_up, w_down, rows, keep, pack, sends, pulled, returned):
    blocks = count * per
    me = lax.axis_index("dp")
    for b in range(blocks):
        pulled[b] = jnp.zeros(pulled.shape[1:], F32)
        returned[b] = rows[:, lanes(b)].astype(F32)
    for step, place, i in send_order(me, count, per):
        c = rows[:, lanes(i)]
        sends[step][1, :, lanes(place)] = c
        target = down_idx[0, i]
        pulled[target] = pulled[target] + times_transposed(c, w_down[0, i])
    for step, place, j in send_order(me, count, per):
        u = up_idx[0, j]
        slope_b, slope_a, push = (keep[j, 8 * k:8 * k + 8] for k in range(3))
        e = jnp.concatenate([slope_b * pulled[j, 0:8], slope_a * pulled[j, 8:16] + push], 0).astype(BF16)
        sends[step][0, :, lanes(place)] = e
        returned[u] = returned[u] + times_transposed(e, w_up[0, j])
    for b in range(blocks):
        pack[:, lanes(b)] = returned[b].astype(BF16)


def forward_second(blocks, up_idx, down_idx, w_up, w_down, rows, keep, pack, hidden):
    for j in range(blocks):
        z = times(rows[:, lanes(up_idx[0, j])], w_up[0, j])
        zv, zt = z[0:8], z[8:16]
        hidden[j] = jnp.concatenate([zv * sigmoid(zv), keep[j] * zt], 0).astype(BF16)
    for i in range(blocks):
        at = lanes(i)
        pack[:, at] = (rows[:, at].astype(F32) + times(hidden[down_idx[0, i]], w_down[0, i])).astype(BF16)


def near_phase(count, per, up_idx, down_idx, w_up, w_down, near_in, keep, keep_tan, far, *refs):
    sends, (pulled, returned, hidden) = refs[:count], refs[count:]
    odd = odd_section()
    clear_pad(far, count * per)

    @pl.when(odd == 0)
    def _():
        back_second(count, per, up_idx, down_idx, w_up, w_down, near_in, keep, far, sends, pulled, returned)

    @pl.when(odd == 1)
    def _():
        forward_second(count * per, up_idx, down_idx, w_up, w_down, near_in, keep_tan, far, hidden)


def far_phase(count, per, up_idx, down_idx, w_up, w_down, far_in, keep, keep_tan, *refs):
    done, near, refs = refs[:count], refs[count], refs[count + 1:]
    sends, (pulled, returned, hidden) = refs[:count], refs[count:]
    odd = odd_section()

    @pl.when(odd == 0)
    def _():
        for source, target in zip(done, sends):
            target[...] = source[...]
        forward_second(count * per, up_idx, down_idx, w_up, w_down, far_in, keep_tan, near, hidden)

    @pl.when(odd == 1)
    def _():
        back_second(count, per, up_idx, down_idx, w_up, w_down, far_in, keep, near, sends, pulled, returned)


def early_grads(count, per, *refs):
    early, grads = refs[:count], refs[count]
    for place in range(per):
        at = lanes(place)
        for out, left, right in ((0, 0, 3), (1, 5, 8)):
            xs = [early[source][left + k, :, at] for source in range(count) for k in range(2)]
            es = [early[source][right + k, :, at] for source in range(count) for k in range(2)]
            grads[out, place] = outer(xs, es)


def finish(count, per, scale, far, near, grads, *rest):
    early, late = rest[:count], rest[count:2 * count]
    values, score, tangent, adjoint, grad_up, grad_down, came = rest[2 * count:]
    take_in(near, far, came)
    moved = came[0].astype(F32)
    values[0] = moved[0:8].astype(BF16)
    tangent[0] = moved[8:16].astype(BF16)
    moved = came[1].astype(F32)
    score[0] = moved[0:8].astype(BF16)
    adjoint[0] = moved[8:16].astype(BF16)
    for place in range(per):
        at = lanes(place)
        for k, (out, group) in enumerate(((grad_up, 2), (grad_down, 7))):
            xs = [early[source][group, :, at] for source in range(count)]
            es = [late[source][k, :, at] for source in range(count)]
            out[0, place] = ((grads[k, place] + outer(xs, es)) * scale).astype(BF16)


def call(body, operands, spaces, outs, scratch, after=(), cost=LIGHT):
    taken = len(operands)

    def kernel(*refs):
        body(*refs[:taken], *refs[taken + len(after):])

    return pl.pallas_call(
        kernel,
        out_shape=outs,
        in_specs=[pl.BlockSpec(memory_space=space) for space in spaces] + [pl.BlockSpec(memory_space=pl.ANY)] * len(after),
        out_specs=[pl.BlockSpec(memory_space=pltpu.VMEM)] * len(outs),
        scratch_shapes=scratch,
        compiler_params=pltpu.CompilerParams(vmem_limit_bytes=LIMIT),
        cost_estimate=pl.CostEstimate(flops=cost, bytes_accessed=cost // 100, transcendentals=0),
    )(*operands, *after)


def hand_on(*refs):
    half = len(refs) // 2
    for source, target in zip(refs[:half], refs[half:]):
        target[...] = source[...]


def held_until(there, arrays):
    shapes = [jax.ShapeDtypeStruct(x.shape, x.dtype) for x in arrays]
    return call(hand_on, tuple(arrays), [pltpu.VMEM] * len(arrays), shapes, [], after=(there,))


def on_device(w_up, up_index, w_down, down_index, tick_order, values_in, score_grad_in, tangent_in, state_adjoint_in,
              saved_back, saved_tan, saved_second, saved_second_tan, saved_second_grad):
    count = lax.axis_size("dp")
    blocks = w_up.shape[1]
    per = blocks // count
    width = values_in.shape[2]
    part = per * BLOCK
    scale = 1.0 / (values_in.shape[1] * count)
    shape = jax.ShapeDtypeStruct
    pair = shape((16, width), BF16)
    vmem, smem = pltpu.VMEM, pltpu.SMEM

    def body(f, *args):
        def kernel(*refs):
            f(*args, *refs)
        return kernel

    def to_replicas(parts):
        steps = [count - 1] + list(range(1, count - 1))
        return [parts[0]] + [lax.ppermute(parts[step], "dp", swap_route(step, count)) for step in steps]

    rows = (score_grad_in, state_adjoint_in, saved_back, saved_second, saved_second_tan, saved_second_grad)
    ten = shape((10, 16, part), BF16)
    (token,) = call(open_launch, (), [], [shape((8, BLOCK), F32)], [], cost=WORK)
    tables = (up_index, down_index, tick_order, w_up, w_down)
    keep, pushes, *early = call(
        body(first_rows, count, per), tables + rows, [smem] * 3 + [vmem] * 8,
        [shape((blocks, 24, BLOCK), F32), pair] + [ten] * count,
        [vmem((blocks, 32, BLOCK), F32), vmem((blocks, 48, BLOCK), BF16)],
        after=(token,), cost=WORK)
    taken = tables + (score_grad_in, state_adjoint_in, pushes, values_in, tangent_in, saved_tan)
    long = shape((16, width + PAD), BF16)
    near, far, keep_tan = call(
        body(first_streams, blocks), taken, [smem] * 3 + [vmem] * 8, [pair, long, shape((blocks, 8, BLOCK), F32)],
        [vmem((2, 16, width), BF16), vmem((blocks, 16, BLOCK), F32), vmem((blocks, 16, BLOCK), BF16)], cost=C_STREAMS)
    near, far = swap_sections(near, far)
    early = to_replicas(early)
    tables = (up_index, down_index, w_up, w_down)
    two = [shape((2, 16, part), BF16)] * count
    scratch = [vmem((blocks, 16, BLOCK), F32), vmem((blocks, 16, BLOCK), F32), vmem((blocks, 16, BLOCK), BF16)]
    far_out, *late = call(
        body(near_phase, count, per), tables + (near, keep, keep_tan), [smem] * 2 + [vmem] * 5, [long] + two, scratch,
        cost=C_NEAR_PHASE)
    near_out, *late = call(
        body(far_phase, count, per), tables + (far, keep, keep_tan, *late), [smem] * 2 + [vmem] * (5 + count),
        [pair] + two, scratch, cost=C_FAR_PHASE, after=(early[1],))
    near, far = swap_sections(near_out, far_out)
    late = to_replicas([late[0], *held_until(near, late[1:2]), *late[2:]])
    (grads,) = call(
        body(early_grads, count, per), tuple(early), [vmem] * count, [shape((2, per, BLOCK, BLOCK), F32)], [],
        after=(far,))
    stream = shape((1,) + values_in.shape[1:], BF16)
    grad = shape((1, per, BLOCK, BLOCK), BF16)
    return tuple(call(
        body(finish, count, per, scale), (far, near, grads, *early, *late), [vmem] * (3 + 2 * count),
        [stream, stream, stream, stream, grad, grad], [vmem((2, 16, width), BF16)]))


def solution(mesh):
    layer = P("section", None, None, None)
    table = P("section", None)
    stream = P("section", "dp", None)
    saved = P("section", None, "dp", None)
    return jax.shard_map(
        on_device,
        mesh=mesh,
        in_specs=(layer, table, layer, table, table) + (stream,) * 4 + (saved,) * 5,
        out_specs=(stream,) * 4 + (P("section", "dp", None, None),) * 2,
        check_vma=False,
    )
```

```python
import jax
import jax.numpy as jnp
from jax import lax
from jax.experimental import pallas as pl
from jax.experimental.pallas import tpu as pltpu
from jax.sharding import PartitionSpec as P

BLOCK = 128
F32 = jnp.float32
BF16 = jnp.bfloat16
LIMIT = 40 * 1024 * 1024
WORK = 10 ** 10
LIGHT = 10 ** 4
PAD = BLOCK
C_STREAMS = LIGHT
C_NEAR_PHASE = LIGHT
C_FAR_PHASE = LIGHT


def partner(me, step, count):
    if count & (count - 1) == 0:
        return me ^ step
    return lax.rem(me + step, count)


def swap_route(step, count):
    if count & (count - 1) == 0:
        return [(i, i ^ step) for i in range(count)]
    return [(i, (i + step) % count) for i in range(count)]


def swap_sections(near, far):
    count = lax.axis_size("section")
    far = lax.ppermute(far, "section", [(i, (i + 2 * (i % 2) - 1) % count) for i in range(count)])
    near = lax.ppermute(near, "section", [(i, i ^ 1) for i in range(count)])
    return near, far


def times(rows, weight):
    return lax.dot_general(rows, weight, (((1,), (0,)), ((), ())), preferred_element_type=F32)


def times_transposed(rows, weight):
    return lax.dot_general(rows, weight, (((1,), (1,)), ((), ())), preferred_element_type=F32)


def outer(xs, es):
    return lax.dot_general(jnp.concatenate(xs, 0), jnp.concatenate(es, 0), (((0,), (0,)), ((), ())),
                           preferred_element_type=F32)


def sigmoid(z):
    return 1.0 / (1.0 + jnp.exp(-z))


def slope_of(z, s):
    return s * (1.0 + z * (1.0 - s))


def lanes(block):
    if isinstance(block, int):
        return pl.ds(block * BLOCK, BLOCK)
    return pl.ds(pl.multiple_of(block * BLOCK, BLOCK), BLOCK)


def stack(parts):
    return jnp.concatenate([part.astype(F32) for part in parts], 0)


def send_order(me, count, per):
    for step in range(count):
        base = partner(me, step, count) * per
        for place in range(per):
            yield step, place, base + place


def odd_section():
    return lax.rem(lax.axis_index("section"), 2)


def take_in(near, far, packs):
    odd = odd_section()
    packs[1 - odd] = near[...]
    packs[odd] = far[:, :packs.shape[2]]


def open_launch(token):
    token[...] = jnp.zeros(token.shape, F32)


def first_rows(count, per, up_idx, down_idx, order, w_up, w_down, g_ref, a_ref, back, second, second_tan, second_grad,
               keep, pushes, *refs):
    sends, (pulled, hidden) = refs[:count], refs[count:]
    blocks = count * per
    me = lax.axis_index("dp")
    for b in range(blocks):
        pulled[b] = jnp.zeros(pulled.shape[1:], F32)
    m0 = order[0, 0]
    m1 = order[0, 1]
    for step, place, i in send_order(me, count, per):
        at = lanes(i)
        c = stack([g_ref[0, :, at], a_ref[0, :, at], second_grad[0, m0, :, at], second_grad[0, m1, :, at]]).astype(BF16)
        sends[step][8, :, lanes(place)] = c[0:16]
        sends[step][9, :, lanes(place)] = c[16:32]
        target = down_idx[0, i]
        pulled[target] = pulled[target] + times_transposed(c, w_down[0, i])
    for step, place, j in send_order(me, count, per):
        u = up_idx[0, j]
        at = lanes(u)
        x = stack([back[0, m0, :, at], second[0, m0, :, at], second_tan[0, m0, :, at],
                   second_tan[0, m1, :, at], back[0, m1, :, at], second[0, m1, :, at]]).astype(BF16)
        out = sends[step]
        here = lanes(place)
        for group in range(3):
            out[group, :, here] = x[16 * group:16 * group + 16]
        z = times(x, w_up[0, j])
        zb0, za0, ta0, ta1, zb1, za1 = (z[8 * k:8 * k + 8] for k in range(6))
        pg, pa, ga0, ga1 = (pulled[j, 8 * k:8 * k + 8] for k in range(4))
        sb0, sa0, sb1, sa1 = sigmoid(zb0), sigmoid(za0), sigmoid(zb1), sigmoid(za1)
        slope_a0 = slope_of(za0, sa0)
        slope_a1 = slope_of(za1, sa1)
        curve_a0 = sa0 * (1.0 - sa0) * (2.0 + za0 * (1.0 - 2.0 * sa0))
        curve_a1 = sa1 * (1.0 - sa1) * (2.0 + za1 * (1.0 - 2.0 * sa1))
        push = slope_a0 * pa + curve_a0 * ga0 * ta0
        e = jnp.concatenate([slope_of(zb0, sb0) * pg, push], 0).astype(BF16)
        out[3, :, here] = e
        out[4, :, here] = jnp.concatenate([slope_a0 * ga0, slope_a1 * ga1], 0).astype(BF16)
        hidden[j] = jnp.concatenate(
            [zb0 * sb0, za0 * sa0, slope_a0 * ta0, slope_a1 * ta1, zb1 * sb1, za1 * sa1], 0).astype(BF16)
        keep[j] = jnp.concatenate([slope_of(zb1, sb1), slope_a1, curve_a1 * ga1 * ta1], 0)
        pushes[:, lanes(j)] = e
    for step, place, i in send_order(me, count, per):
        y = hidden[down_idx[0, i]]
        for group in range(3):
            sends[step][5 + group, :, lanes(place)] = y[16 * group:16 * group + 16]


def forward_first(blocks, up_idx, down_idx, order, w_up, w_down, v_ref, t_ref, tan, pack, keep, hidden):
    m0 = order[0, 0]
    m1 = order[0, 1]
    for j in range(blocks):
        at = lanes(up_idx[0, j])
        x = stack([v_ref[0, :, at], t_ref[0, :, at], tan[0, m0, :, at], tan[0, m1, :, at]]).astype(BF16)
        z = times(x, w_up[0, j])
        zv, zt, z0, z1 = (z[8 * k:8 * k + 8] for k in range(4))
        hidden[j] = jnp.concatenate([zv * sigmoid(zv), slope_of(z0, sigmoid(z0)) * zt], 0).astype(BF16)
        keep[j] = slope_of(z1, sigmoid(z1))
    for i in range(blocks):
        at = lanes(i)
        moved = stack([v_ref[0, :, at], t_ref[0, :, at]]) + times(hidden[down_idx[0, i]], w_down[0, i])
        pack[:, at] = moved.astype(BF16)


def clear_pad(pack, blocks):
    if pack.shape[1] > blocks * BLOCK:
        pack[:, blocks * BLOCK:] = jnp.zeros((pack.shape[0], pack.shape[1] - blocks * BLOCK), BF16)


def back_streams(blocks, up_idx, w_up, g_ref, a_ref, pushes, pack, returned):
    for b in range(blocks):
        returned[b] = stack([g_ref[0, :, lanes(b)], a_ref[0, :, lanes(b)]])
    for j in range(blocks):
        u = up_idx[0, j]
        returned[u] = returned[u] + times_transposed(pushes[:, lanes(j)], w_up[0, j])
    for b in range(blocks):
        pack[:, lanes(b)] = returned[b].astype(BF16)


def first_streams(blocks, up_idx, down_idx, order, w_up, w_down, g_ref, a_ref, pushes, v_ref, t_ref, tan,
                  near, far, keep, packs, returned, hidden):
    odd = odd_section()
    clear_pad(far, blocks)
    back_streams(blocks, up_idx, w_up, g_ref, a_ref, pushes, packs.at[1], returned)
    forward_first(blocks, up_idx, down_idx, order, w_up, w_down, v_ref, t_ref, tan, packs.at[0], keep, hidden)
    near[...] = packs[odd]
    far[:, :packs.shape[2]] = packs[1 - odd]


def back_second(count, per, up_idx, down_idx, w_up, w_down, rows, keep, pack, sends, pulled, returned):
    blocks = count * per
    me = lax.axis_index("dp")
    for b in range(blocks):
        pulled[b] = jnp.zeros(pulled.shape[1:], F32)
        returned[b] = rows[:, lanes(b)].astype(F32)
    for step, place, i in send_order(me, count, per):
        c = rows[:, lanes(i)]
        sends[step][1, :, lanes(place)] = c
        target = down_idx[0, i]
        pulled[target] = pulled[target] + times_transposed(c, w_down[0, i])
    for step, place, j in send_order(me, count, per):
        u = up_idx[0, j]
        slope_b, slope_a, push = (keep[j, 8 * k:8 * k + 8] for k in range(3))
        e = jnp.concatenate([slope_b * pulled[j, 0:8], slope_a * pulled[j, 8:16] + push], 0).astype(BF16)
        sends[step][0, :, lanes(place)] = e
        returned[u] = returned[u] + times_transposed(e, w_up[0, j])
    for b in range(blocks):
        pack[:, lanes(b)] = returned[b].astype(BF16)


def forward_second(blocks, up_idx, down_idx, w_up, w_down, rows, keep, pack, hidden):
    for j in range(blocks):
        z = times(rows[:, lanes(up_idx[0, j])], w_up[0, j])
        zv, zt = z[0:8], z[8:16]
        hidden[j] = jnp.concatenate([zv * sigmoid(zv), keep[j] * zt], 0).astype(BF16)
    for i in range(blocks):
        at = lanes(i)
        pack[:, at] = (rows[:, at].astype(F32) + times(hidden[down_idx[0, i]], w_down[0, i])).astype(BF16)


def near_phase(count, per, up_idx, down_idx, w_up, w_down, near_in, keep, keep_tan, far, *refs):
    sends, (pulled, returned, hidden) = refs[:count], refs[count:]
    odd = odd_section()
    clear_pad(far, count * per)

    @pl.when(odd == 0)
    def _():
        back_second(count, per, up_idx, down_idx, w_up, w_down, near_in, keep, far, sends, pulled, returned)

    @pl.when(odd == 1)
    def _():
        forward_second(count * per, up_idx, down_idx, w_up, w_down, near_in, keep_tan, far, hidden)


def far_phase(count, per, up_idx, down_idx, w_up, w_down, far_in, keep, keep_tan, *refs):
    done, near, refs = refs[:count], refs[count], refs[count + 1:]
    sends, (pulled, returned, hidden) = refs[:count], refs[count:]
    odd = odd_section()

    @pl.when(odd == 0)
    def _():
        for source, target in zip(done, sends):
            target[...] = source[...]
        forward_second(count * per, up_idx, down_idx, w_up, w_down, far_in, keep_tan, near, hidden)

    @pl.when(odd == 1)
    def _():
        back_second(count, per, up_idx, down_idx, w_up, w_down, far_in, keep, near, sends, pulled, returned)


def early_grads(count, per, *refs):
    early, (far, near, grads, values, score, tangent, adjoint, came) = refs[:count], refs[count:]
    take_in(near, far, came)
    moved = came[0].astype(F32)
    values[0] = moved[0:8].astype(BF16)
    tangent[0] = moved[8:16].astype(BF16)
    moved = came[1].astype(F32)
    score[0] = moved[0:8].astype(BF16)
    adjoint[0] = moved[8:16].astype(BF16)
    for place in range(per):
        at = lanes(place)
        for out, left, right in ((0, 0, 3), (1, 5, 8)):
            xs = [early[source][left + k, :, at] for source in range(count) for k in range(2)]
            es = [early[source][right + k, :, at] for source in range(count) for k in range(2)]
            grads[out, place] = outer(xs, es)


def finish(count, per, scale, grads, *rest):
    early, late = rest[:count], rest[count:2 * count]
    grad_up, grad_down = rest[2 * count:]
    for place in range(per):
        at = lanes(place)
        for k, (out, group) in enumerate(((grad_up, 2), (grad_down, 7))):
            xs = [early[source][group, :, at] for source in range(count)]
            es = [late[source][k, :, at] for source in range(count)]
            out[0, place] = ((grads[k, place] + outer(xs, es)) * scale).astype(BF16)


def call(body, operands, spaces, outs, scratch, after=(), cost=LIGHT):
    taken = len(operands)

    def kernel(*refs):
        body(*refs[:taken], *refs[taken + len(after):])

    return pl.pallas_call(
        kernel,
        out_shape=outs,
        in_specs=[pl.BlockSpec(memory_space=space) for space in spaces] + [pl.BlockSpec(memory_space=pl.ANY)] * len(after),
        out_specs=[pl.BlockSpec(memory_space=pltpu.VMEM)] * len(outs),
        scratch_shapes=scratch,
        compiler_params=pltpu.CompilerParams(vmem_limit_bytes=LIMIT),
        cost_estimate=pl.CostEstimate(flops=cost, bytes_accessed=cost // 100, transcendentals=0),
    )(*operands, *after)


def hand_on(*refs):
    half = len(refs) // 2
    for source, target in zip(refs[:half], refs[half:]):
        target[...] = source[...]


def held_until(there, arrays):
    shapes = [jax.ShapeDtypeStruct(x.shape, x.dtype) for x in arrays]
    return call(hand_on, tuple(arrays), [pltpu.VMEM] * len(arrays), shapes, [], after=(there,))


def on_device(w_up, up_index, w_down, down_index, tick_order, values_in, score_grad_in, tangent_in, state_adjoint_in,
              saved_back, saved_tan, saved_second, saved_second_tan, saved_second_grad):
    count = lax.axis_size("dp")
    blocks = w_up.shape[1]
    per = blocks // count
    width = values_in.shape[2]
    part = per * BLOCK
    scale = 1.0 / (values_in.shape[1] * count)
    shape = jax.ShapeDtypeStruct
    pair = shape((16, width), BF16)
    vmem, smem = pltpu.VMEM, pltpu.SMEM

    def body(f, *args):
        def kernel(*refs):
            f(*args, *refs)
        return kernel

    def to_replicas(parts):
        steps = [count - 1] + list(range(1, count - 1))
        return [parts[0]] + [lax.ppermute(parts[step], "dp", swap_route(step, count)) for step in steps]

    rows = (score_grad_in, state_adjoint_in, saved_back, saved_second, saved_second_tan, saved_second_grad)
    ten = shape((10, 16, part), BF16)
    (token,) = call(open_launch, (), [], [shape((8, BLOCK), F32)], [], cost=WORK)
    tables = (up_index, down_index, tick_order, w_up, w_down)
    keep, pushes, *early = call(
        body(first_rows, count, per), tables + rows, [smem] * 3 + [vmem] * 8,
        [shape((blocks, 24, BLOCK), F32), pair] + [ten] * count,
        [vmem((blocks, 32, BLOCK), F32), vmem((blocks, 48, BLOCK), BF16)],
        after=(token,), cost=WORK)
    taken = tables + (score_grad_in, state_adjoint_in, pushes, values_in, tangent_in, saved_tan)
    long = shape((16, width + PAD), BF16)
    near, far, keep_tan = call(
        body(first_streams, blocks), taken, [smem] * 3 + [vmem] * 8, [pair, long, shape((blocks, 8, BLOCK), F32)],
        [vmem((2, 16, width), BF16), vmem((blocks, 16, BLOCK), F32), vmem((blocks, 16, BLOCK), BF16)], cost=C_STREAMS)
    near, far = swap_sections(near, far)
    early = to_replicas(early)
    tables = (up_index, down_index, w_up, w_down)
    two = [shape((2, 16, part), BF16)] * count
    scratch = [vmem((blocks, 16, BLOCK), F32), vmem((blocks, 16, BLOCK), F32), vmem((blocks, 16, BLOCK), BF16)]
    far_out, *late = call(
        body(near_phase, count, per), tables + (near, keep, keep_tan), [smem] * 2 + [vmem] * 5, [long] + two, scratch,
        cost=C_NEAR_PHASE)
    near_out, *late = call(
        body(far_phase, count, per), tables + (far, keep, keep_tan, *late), [smem] * 2 + [vmem] * (5 + count),
        [pair] + two, scratch, cost=C_FAR_PHASE, after=(early[1],))
    near, far = swap_sections(near_out, far_out)
    late = to_replicas([late[0], *held_until(near, late[1:2]), *late[2:]])
    stream = shape((1,) + values_in.shape[1:], BF16)
    grad = shape((1, per, BLOCK, BLOCK), BF16)
    grads, *streams = call(
        body(early_grads, count, per), (*early, far, near), [vmem] * (count + 2),
        [shape((2, per, BLOCK, BLOCK), F32)] + [stream] * 4, [vmem((2, 16, width), BF16)])
    grads = call(
        body(finish, count, per, scale), (grads, *early, *late), [vmem] * (1 + 2 * count), [grad] * 2, [])
    return (*streams, *grads)


def solution(mesh):
    layer = P("section", None, None, None)
    table = P("section", None)
    stream = P("section", "dp", None)
    saved = P("section", None, "dp", None)
    return jax.shard_map(
        on_device,
        mesh=mesh,
        in_specs=(layer, table, layer, table, table) + (stream,) * 4 + (saved,) * 5,
        out_specs=(stream,) * 4 + (P("section", "dp", None, None),) * 2,
        check_vma=False,
    )
```
